32 devices in a mesh: virt: 2 (over y), walk: 16 (over z, x, core).
Axes of the slice: x: 2, y: 2, z: 4, core: 2. Of those that a mesh axis runs over, the one named last changes fastest.
Arguments:
- inverse_rows: bfloat16 [16, 512, 2048], P('walk', None, 'virt'), may hold values from -1.5 to 1.5
- kinetic_rows: bfloat16 [16, 512, 2048], P('walk', None, 'virt'), may hold values from -1 to 1
- virt_values: bfloat16 [16, 2048, 4096], P('walk', None, 'virt'), may hold values from -6 to 6
- virt_laplacians: bfloat16 [16, 2048, 4096], P('walk', None, 'virt'), may hold values from -6 to 6
- local_energy: float32 [16], P('walk'), may hold values from 0.2 to 6, as said below
Outputs:
- energy_gradient: float32 [512, 4096], P('walk', 'virt')
- log_derivative_mean: float32 [512, 4096], P('walk', 'virt')
The draws below stay inside these ranges and needn't reach their ends.
Inputs may be any that keep to these rules, and one draw needn't show every extreme that they name: `local_energy`: positive local energies.
All inputs are finite; a program needn't handle non-finite values.
Results may differ from the reference program's by a relative error of at most 0.0003.
Values may be sent and summed in bfloat16 or wider, within the bound.
No kernel may reach another device: no remote copies, remote signals or barrier semaphores. Data moves between devices by JAX's collectives and lax.ppermute only.
A program may use at most 64 MiB of HBM per device.

```python
import jax
import jax.numpy as jnp
from jax import lax

NE = 2048
VIRT = 4096
OCC = 512
WALKERS = 16


def draw_local_energy(key, part):
    position = jnp.arange(WALKERS).astype(jnp.float32)
    slope = 1.0 + 2.0 * position / max(WALKERS - 1, 1)
    factor = jax.random.uniform(key, (WALKERS,), jnp.float32, 0.5, 1.5)
    return (slope * factor).astype(jnp.float32)


def spiked(drawn, key, source, target, parts, factor):
    owner, partner = [(jnp.arange(drawn.shape[dim]) // (drawn.shape[dim] // parts)).reshape([-1 if axis == dim else 1 for axis in range(drawn.ndim)]) for dim in (source, target)]
    chosen = jax.random.permutation(key, parts)[partner]
    strong = (owner == chosen) | (owner == (partner + parts // 2) % parts)
    return jnp.where(strong, factor * drawn, drawn)


def steps_of(key, extent, pieces, smallest, high):
    factor_of, own = 1.0, jax.random.fold_in(key, 6)
    for dim, parts in pieces:
        draws = jnp.exp(jax.random.uniform(jax.random.fold_in(own, dim), (parts,), jnp.float32, smallest / len(pieces), high / len(pieces)))
        factor_of = factor_of * jnp.repeat(draws, extent[dim] // parts).reshape([-1 if axis == dim else 1 for axis in range(len(extent))])
    return factor_of


def bell_draw(own_key, shape, deviation, bound, shards=(), kind=jnp.bfloat16):
    result = jax.random.normal(own_key, shape, jnp.float32) * deviation
    if len(shards) > 0:
        result = steps_of(own_key, shape, shards, -0.22, 0.18) * result
    return jnp.clip(result, min=-bound, max=bound).astype(kind)


def gaussian_with(rng, dims, deviation, reach, pieces, heavy, kind=jnp.bfloat16):
    entries = deviation * jax.random.normal(rng, dims, jnp.float32)
    if pieces:
        entries = entries * steps_of(rng, dims, pieces, -0.22, 0.18)
    return jnp.clip(spiked(entries, jax.random.fold_in(rng, 3), *heavy), -reach, reach).astype(kind)


def setup_inputs(seed: int = 0) -> dict:
    splits = jax.random.split(jax.random.key(seed), 6)
    inverse_rows = gaussian_with(splits[0], (WALKERS, OCC, NE), (max(NE // 64, 1)) ** -0.5, 1.5, ((0, 16), (2, 2)), (0, 1, 16, 2.0))
    kinetic_rows = bell_draw(splits[1], (WALKERS, OCC, NE), (max(NE // 64, 1)) ** -0.5, 1.0, ((0, 16), (2, 2)))
    virt_values = bell_draw(splits[2], (WALKERS, NE, VIRT), 1.0, 6.0, ((0, 16), (2, 2)))
    virt_laplacians = bell_draw(splits[3], (WALKERS, NE, VIRT), 1.0, 6.0, ((0, 16), (2, 2)))
    local_energy = draw_local_energy(jax.random.fold_in(splits[5], 71), 0)
    return {"inverse_rows": inverse_rows, "kinetic_rows": kinetic_rows, "virt_values": virt_values, "virt_laplacians": virt_laplacians, "local_energy": local_energy}


def reference(inverse_rows, kinetic_rows, virt_values, virt_laplacians, local_energy):
    walker_count = local_energy.shape[0]
    average = jnp.sum(local_energy) / walker_count

    def accumulate(totals, items):
        inverse, kinetic, values, laplacians, energy = items
        log_grad = jnp.dot(inverse, values, preferred_element_type=jnp.float32)
        kin_part = jnp.dot(inverse, laplacians, preferred_element_type=jnp.float32) - jnp.dot(kinetic, values, preferred_element_type=jnp.float32)
        kin_grad = -0.5 * kin_part
        weighted = 2.0 * (energy - average) * log_grad + kin_grad
        return (totals[0] + weighted, totals[1] + log_grad), None

    zeros = jnp.zeros((inverse_rows.shape[1], virt_values.shape[2]), jnp.float32)
    sums, unused = lax.scan(accumulate, (zeros, zeros), (inverse_rows, kinetic_rows, virt_values, virt_laplacians, local_energy))
    return sums[0] / walker_count, sums[1] / walker_count
```

```python
import functools

import jax
import jax.numpy as jnp
from jax import lax
from jax.experimental import pallas as pl
from jax.experimental.pallas import tpu as pltpu
from jax.sharding import PartitionSpec as P

PIECES = 4


def product(left, right):
    return jnp.einsum("woe,wev->wov", left, right, preferred_element_type=jnp.float32)


def gradient_terms(log_grad, kin_part, weights):
    kin_grad = -0.5 * kin_part
    weighted = jnp.sum(weights[:, None, None] * log_grad + kin_grad, axis=0)
    return (weighted, jnp.sum(log_grad, axis=0))


def general_body(inverse_rows, kinetic_rows, virt_values, virt_laplacians, local_energy):
    walk_count = lax.axis_size("walk")
    walker_count = walk_count * local_energy.shape[0]
    energy_sum = lax.psum(jnp.sum(local_energy), "walk")
    average = energy_sum / walker_count
    weights = 2.0 * (local_energy - average)
    inverse_all, kinetic_all = (
        lax.all_gather(inverse_rows, "virt", axis=2, tiled=True),
        lax.all_gather(kinetic_rows, "virt", axis=2, tiled=True),
    )
    log_grad = product(inverse_all, virt_values)
    kin_part = product(inverse_all, virt_laplacians) - product(kinetic_all, virt_values)
    weighted, log_sum = gradient_terms(log_grad, kin_part, weights)
    summed = (
        lax.psum_scatter(weighted, "walk", scatter_dimension=0, tiled=True),
        lax.psum_scatter(log_sum, "walk", scatter_dimension=0, tiled=True),
    )
    gradient_part, log_part = (summed[0], summed[1])
    return (gradient_part / walker_count, log_part / walker_count)


def stage_masks(count):
    bits = count.bit_length() - 1
    masks = [1 << bit for bit in range(bits)]
    if bits >= 2:
        masks[-1] = 3 << (bits - 2)
    return masks


def swap(array, axis, mask):
    pairs = [(source, source ^ mask) for source in range(lax.axis_size(axis))]
    return lax.ppermute(array, axis, pairs)


def order_kernel(offset, rows, count, masks, me_ref, inverse_ref, kinetic_ref, *rest):
    out_ref = rest[-1]
    height = out_ref.shape[1]
    total = inverse_ref.shape[0]
    per = total // count
    place = lax.broadcasted_iota(jnp.int32, (height, 1), 0)
    block = lax.div(place, rows)
    dest = jnp.full_like(block, me_ref[0])
    bits = len(masks)
    for stage, mask in enumerate(masks):
        bit = jnp.bitwise_and(lax.shift_right_logical(block, bits - 1 - stage), 1)
        dest = jnp.bitwise_xor(dest, bit * mask)
    source = dest * per + offset + (place - block * rows)
    column = lax.broadcasted_iota(jnp.int32, (height, total), 1)
    pick = jnp.where(column == source, 1.0, 0.0).astype(jnp.bfloat16)
    for index, ref in enumerate((inverse_ref, kinetic_ref)):
        picked = jnp.dot(pick, ref[...], preferred_element_type=jnp.float32)
        out_ref[index] = picked.astype(jnp.bfloat16)


def order_piece(me, inverse, kinetic, offset, rows, masks, count, after):
    height = count * rows
    depth = inverse.shape[1]
    whole = pl.BlockSpec(memory_space=pltpu.VMEM)
    return pl.pallas_call(
        functools.partial(order_kernel, offset, rows, count, masks),
        out_shape=jax.ShapeDtypeStruct((2, height, depth), jnp.bfloat16),
        in_specs=[pl.BlockSpec(memory_space=pltpu.SMEM), whole, whole]
        + [pl.BlockSpec(memory_space=pl.ANY)] * len(after),
        out_specs=whole,
        cost_estimate=pl.CostEstimate(
            flops=4 * height * inverse.shape[0] * depth,
            bytes_accessed=4 * inverse.size + 4 * height * depth,
            transcendentals=0,
        ),
        name="order_piece",
    )(me, inverse, kinetic, *after)


def multiply_kernel(place_ref, scale_ref, near_ref, far_ref, v_near, v_far, l_near, l_far, send_ref, keep_ref):
    height, depth = near_ref.shape[1], near_ref.shape[2]
    half = height // 2
    both = (2 * height, depth)
    f32 = jnp.float32
    values = jnp.dot(near_ref[...].reshape(both), v_near[...], preferred_element_type=f32)
    values += jnp.dot(far_ref[...].reshape(both), v_far[...], preferred_element_type=f32)
    laps = jnp.dot(near_ref[0], l_near[...], preferred_element_type=f32)
    laps += jnp.dot(far_ref[0], l_far[...], preferred_element_type=f32)
    log = values[:height]
    weighted = scale_ref[0] * log + 0.5 * (values[height:] - laps)
    keep_ref[0] = weighted[:half]
    keep_ref[1] = log[:half]
    send_ref[0] = weighted[half:]
    send_ref[1] = log[half:]


def multiply(place, scale, near, far, values, laplacians, tile):
    height, depth = near.shape[1], near.shape[2]
    width = values.shape[1]
    half = height // 2
    rows_spec = pl.BlockSpec((2, height, depth), lambda j, place: (0, 0, 0))
    near_spec = pl.BlockSpec((depth, tile), lambda j, place: (place[0], j))
    far_spec = pl.BlockSpec((depth, tile), lambda j, place: (1 - place[0], j))
    out_spec = pl.BlockSpec((2, half, tile), lambda j, place: (0, 0, j))
    out = jax.ShapeDtypeStruct((2, half, width), jnp.float32)
    return pl.pallas_call(
        multiply_kernel,
        out_shape=(out, out),
        grid_spec=pltpu.PrefetchScalarGridSpec(
            num_scalar_prefetch=1,
            grid=(width // tile,),
            in_specs=[pl.BlockSpec(memory_space=pltpu.SMEM), rows_spec, rows_spec, near_spec, far_spec, near_spec, far_spec],
            out_specs=(out_spec, out_spec),
        ),
        compiler_params=pltpu.CompilerParams(vmem_limit_bytes=32 * 1024 * 1024),
        cost_estimate=pl.CostEstimate(
            flops=2 * 3 * height * 2 * depth * width,
            bytes_accessed=4 * values.size + 8 * height * depth + 8 * height * width,
            transcendentals=0,
        ),
        name="multiply_piece",
    )(place, scale, near, far, values, values, laplacians, laplacians)


def pieced_body(pieces, tile, inverse_rows, kinetic_rows, virt_values, virt_laplacians, local_energy):
    count = lax.axis_size("walk")
    masks = stage_masks(count)
    me = lax.axis_index("walk").astype(jnp.int32).reshape(1)
    place = lax.axis_index("virt").astype(jnp.int32).reshape(1)
    inverse, kinetic = inverse_rows[0], kinetic_rows[0]
    values, laplacians = virt_values[0], virt_laplacians[0]
    rows = inverse.shape[0] // (count * pieces)

    energy_sum = jnp.broadcast_to(local_energy, (1, 128))
    for mask in masks:
        energy_sum = energy_sum + swap(energy_sum, "walk", mask)
    average = energy_sum[0, 0] / count

    near, far = [], []
    for piece in range(pieces):
        after = [far[piece - 2]] if piece >= 2 else []
        near.append(order_piece(me, inverse, kinetic, piece * rows, rows, masks, count, after))
        far.append(swap(near[piece], "virt", 1))

    done = []
    for piece in range(pieces):
        send, keep = multiply(place, 2.0 * local_energy, near[piece], far[piece], values, laplacians, tile)
        for stage, mask in enumerate(masks):
            total = keep + swap(send, "walk", mask)
            if stage + 1 < len(masks):
                half = total.shape[1] // 2
                keep, send = total[:, :half], total[:, half:]
        done.append(total)
    log_part = jnp.concatenate([total[1] for total in done], axis=0) / count
    gradient_part = jnp.concatenate([total[0] for total in done], axis=0) / count
    return (gradient_part - (2.0 * average) * log_part, log_part)


def solution(mesh):
    placed = (
        P("walk", None, "virt"),
        P("walk", None, "virt"),
        P("walk", None, "virt"),
        P("walk", None, "virt"),
        P("walk"),
    )

    def body(inverse_rows, kinetic_rows, virt_values, virt_laplacians, local_energy):
        count = mesh.shape["walk"]
        walkers, occupied, depth = inverse_rows.shape
        width = virt_values.shape[2]
        tile = 512
        fits = (
            walkers == 1
            and mesh.shape["virt"] == 2
            and count >= 4
            and count & (count - 1) == 0
            and occupied % (count * PIECES * 8) == 0
            and depth % 256 == 0
            and width % tile == 0
        )
        form = functools.partial(pieced_body, PIECES, tile) if fits else general_body
        return form(inverse_rows, kinetic_rows, virt_values, virt_laplacians, local_energy)

    return jax.shard_map(
        body,
        mesh=mesh,
        in_specs=placed,
        out_specs=(P("walk", "virt"), P("walk", "virt")),
        check_vma=False,
    )
```

```python
import functools

import jax
import jax.numpy as jnp
from jax import lax
from jax.experimental import pallas as pl
from jax.experimental.pallas import tpu as pltpu
from jax.sharding import PartitionSpec as P

PIECES = 4
BRIEF = pl.CostEstimate(flops=1024, bytes_accessed=1024, transcendentals=0)


def product(left, right):
    return jnp.einsum("woe,wev->wov", left, right, preferred_element_type=jnp.float32)


def gradient_terms(log_grad, kin_part, weights):
    kin_grad = -0.5 * kin_part
    weighted = jnp.sum(weights[:, None, None] * log_grad + kin_grad, axis=0)
    return (weighted, jnp.sum(log_grad, axis=0))


def general_body(inverse_rows, kinetic_rows, virt_values, virt_laplacians, local_energy):
    walk_count = lax.axis_size("walk")
    walker_count = walk_count * local_energy.shape[0]
    energy_sum = lax.psum(jnp.sum(local_energy), "walk")
    average = energy_sum / walker_count
    weights = 2.0 * (local_energy - average)
    inverse_all, kinetic_all = (
        lax.all_gather(inverse_rows, "virt", axis=2, tiled=True),
        lax.all_gather(kinetic_rows, "virt", axis=2, tiled=True),
    )
    log_grad = product(inverse_all, virt_values)
    kin_part = product(inverse_all, virt_laplacians) - product(kinetic_all, virt_values)
    weighted, log_sum = gradient_terms(log_grad, kin_part, weights)
    summed = (
        lax.psum_scatter(weighted, "walk", scatter_dimension=0, tiled=True),
        lax.psum_scatter(log_sum, "walk", scatter_dimension=0, tiled=True),
    )
    gradient_part, log_part = (summed[0], summed[1])
    return (gradient_part / walker_count, log_part / walker_count)


def stage_masks(count):
    bits = count.bit_length() - 1
    masks = [1 << bit for bit in range(bits)]
    if bits >= 2:
        masks[-1] = 3 << (bits - 2)
    return masks


def place_weights(masks):
    bits = len(masks)
    weights = [0] * bits
    for place in range(1 << bits):
        difference = 0
        for stage, mask in enumerate(masks):
            if place >> (bits - 1 - stage) & 1:
                difference ^= mask
        if difference & (difference - 1) == 0 and difference:
            weights[difference.bit_length() - 1] = place
    return weights


def swap(array, axis, mask):
    pairs = [(source, source ^ mask) for source in range(lax.axis_size(axis))]
    return lax.ppermute(array, axis, pairs)


def near_kernel(virt_ref, inverse_ref, kinetic_ref, values_ref, laps_ref, out_ref):
    f32 = jnp.float32
    inverse = inverse_ref[...].reshape(-1, inverse_ref.shape[-1])
    kinetic = kinetic_ref[...].reshape(-1, kinetic_ref.shape[-1])
    values = values_ref[...]
    log = jnp.dot(inverse, values, preferred_element_type=f32)
    rest = jnp.dot(kinetic, values, preferred_element_type=f32)
    rest -= jnp.dot(inverse, laps_ref[...], preferred_element_type=f32)
    out_ref[0] = 0.5 * rest
    out_ref[1] = log


def near_product(virt, mine, values, laplacians, tile):
    _, height, depth = mine.shape
    width = values.shape[1]
    rows_spec = lambda index: pl.BlockSpec((None, height, depth), lambda j, virt: (index, 0, 0))
    table_spec = pl.BlockSpec((depth, tile), lambda j, virt: (virt[0], j))
    return pl.pallas_call(
        near_kernel,
        out_shape=jax.ShapeDtypeStruct((2, height, width), jnp.float32),
        grid_spec=pltpu.PrefetchScalarGridSpec(
            num_scalar_prefetch=1,
            grid=(width // tile,),
            in_specs=[rows_spec(0), rows_spec(1), table_spec, table_spec],
            out_specs=pl.BlockSpec((2, height, tile), lambda j, virt: (0, 0, j)),
        ),
        compiler_params=pltpu.CompilerParams(vmem_limit_bytes=24 * 1024 * 1024),
        cost_estimate=BRIEF,
        name="near_product",
    )(virt, mine, mine, values, laplacians)


def far_kernel(weights, count, virt_ref, me_ref, scale_ref, far_ref, near_ref, values_ref, laps_ref, *rest):
    send_ref, keep_ref, place_ref = rest[-3:]
    height, depth = far_ref.shape[1], far_ref.shape[2]
    rows = height // count
    half = height // 2
    f32 = jnp.float32
    both = jnp.dot(far_ref[...].reshape(2 * height, depth), values_ref[...], preferred_element_type=f32)
    laps = jnp.dot(far_ref[0], laps_ref[...], preferred_element_type=f32)
    log = both[:height] + near_ref[1]
    weighted = scale_ref[0] * log + (0.5 * (both[height:] - laps) + near_ref[0])
    for dest in range(count):
        difference = dest ^ me_ref[0]
        place = 0
        for bit, weight in enumerate(weights):
            place = place ^ (((difference >> bit) & 1) * weight)
        target = pl.ds(pl.multiple_of(place * rows, rows), rows)
        source = slice(dest * rows, (dest + 1) * rows)
        place_ref[0, target, :] = weighted[source]
        place_ref[1, target, :] = log[source]
    keep_ref[...] = place_ref[:, :half]
    send_ref[...] = place_ref[:, half:]


def far_product(virt, me, scale, theirs, near, values, laplacians, tile, masks, after):
    _, height, depth = theirs.shape
    width = values.shape[1]
    half = height // 2
    count = 1 << len(masks)
    table_spec = pl.BlockSpec((depth, tile), lambda j, virt, me: (1 - virt[0], j))
    out_spec = pl.BlockSpec((2, half, tile), lambda j, virt, me: (0, 0, j))
    out = jax.ShapeDtypeStruct((2, half, width), jnp.float32)
    return pl.pallas_call(
        functools.partial(far_kernel, place_weights(masks), count),
        out_shape=(out, out),
        grid_spec=pltpu.PrefetchScalarGridSpec(
            num_scalar_prefetch=2,
            grid=(width // tile,),
            in_specs=[
                pl.BlockSpec(memory_space=pltpu.SMEM),
                pl.BlockSpec((2, height, depth), lambda j, virt, me: (0, 0, 0)),
                pl.BlockSpec((2, height, tile), lambda j, virt, me: (0, 0, j)),
                table_spec,
                table_spec,
            ]
            + [pl.BlockSpec(memory_space=pl.ANY)] * len(after),
            out_specs=(out_spec, out_spec),
            scratch_shapes=[pltpu.VMEM((2, height, tile), jnp.float32)],
        ),
        compiler_params=pltpu.CompilerParams(vmem_limit_bytes=24 * 1024 * 1024),
        cost_estimate=BRIEF,
        name="far_product",
    )(virt, me, scale, theirs, near, values, laplacians, *after)


def halve_kernel(keep_ref, came_ref, send_ref, kept_ref):
    half = kept_ref.shape[1]
    kept_ref[...] = keep_ref[:, :half] + came_ref[:, :half]
    send_ref[...] = keep_ref[:, half:] + came_ref[:, half:]


def halve(keep, came):
    _, height, width = keep.shape
    whole = pl.BlockSpec(memory_space=pltpu.VMEM)
    out = jax.ShapeDtypeStruct((2, height // 2, width), jnp.float32)
    return pl.pallas_call(
        halve_kernel,
        out_shape=(out, out),
        in_specs=[whole, whole],
        out_specs=(whole, whole),
        cost_estimate=BRIEF,
        name="halve",
    )(keep, came)


def pieced_body(pieces, tile, inverse_rows, kinetic_rows, virt_values, virt_laplacians, local_energy):
    count = lax.axis_size("walk")
    masks = stage_masks(count)
    me = lax.axis_index("walk").astype(jnp.int32).reshape(1)
    virt = lax.axis_index("virt").astype(jnp.int32).reshape(1)
    occupied, depth = inverse_rows.shape[1:]
    by_dest = (count, occupied // count, depth)
    inverse, kinetic = inverse_rows.reshape(by_dest), kinetic_rows.reshape(by_dest)
    values = pltpu.with_memory_space_constraint(virt_values[0], pltpu.HBM)
    laplacians = pltpu.with_memory_space_constraint(virt_laplacians[0], pltpu.HBM)
    rows = occupied // (count * pieces)

    mine, theirs = [], []
    for piece in range(pieces):
        part = slice(piece * rows, (piece + 1) * rows)
        taken = [array[:, part].reshape(count * rows, depth) for array in (inverse, kinetic)]
        mine.append(jnp.stack(taken))
        theirs.append(swap(mine[piece], "virt", 1))

    energy_sum = jnp.broadcast_to(local_energy, (1, 128))
    for mask in masks:
        energy_sum = energy_sum + swap(energy_sum, "walk", mask)
    average = energy_sum[0, 0] / count
    scale = 2.0 * (local_energy - average)

    near = [near_product(virt, part, values, laplacians, tile) for part in mine]
    stages = len(masks)
    send, keep, done = {}, {}, {}
    for turn in range(pieces + stages + 1):
        after = [send[other] for other in sorted(send)]
        if turn < pieces:
            send[turn], keep[turn] = far_product(
                virt, me, scale, theirs[turn], near[turn], values, laplacians, tile, masks, after
            )
        for piece in range(turn - 1, max(turn - 1 - stages, -1), -1):
            if piece >= pieces:
                continue
            stage = turn - 1 - piece
            came = swap(send.pop(piece), "walk", masks[stage])
            if stage + 1 < stages:
                send[piece], keep[piece] = halve(keep[piece], came)
            else:
                done[piece] = keep[piece] + came
    done = [done[piece] for piece in range(pieces)]
    log_part = jnp.concatenate([total[1] for total in done], axis=0) / count
    gradient_part = jnp.concatenate([total[0] for total in done], axis=0) / count
    return (gradient_part, log_part)


def solution(mesh):
    placed = (
        P("walk", None, "virt"),
        P("walk", None, "virt"),
        P("walk", None, "virt"),
        P("walk", None, "virt"),
        P("walk"),
    )

    def body(inverse_rows, kinetic_rows, virt_values, virt_laplacians, local_energy):
        count = mesh.shape["walk"]
        walkers, occupied, depth = inverse_rows.shape
        width = virt_values.shape[2]
        tile = 512
        fits = (
            walkers == 1
            and mesh.shape["virt"] == 2
            and count >= 4
            and count & (count - 1) == 0
            and occupied % (count * PIECES * 8) == 0
            and depth % 256 == 0
            and width % tile == 0
        )
        form = functools.partial(pieced_body, PIECES, tile) if fits else general_body
        return form(inverse_rows, kinetic_rows, virt_values, virt_laplacians, local_energy)

    return jax.shard_map(
        body,
        mesh=mesh,
        in_specs=placed,
        out_specs=(P("walk", "virt"), P("walk", "virt")),
        check_vma=False,
    )
```

```python
import functools

import jax
import jax.numpy as jnp
from jax import lax
from jax.experimental import pallas as pl
from jax.experimental.pallas import tpu as pltpu
from jax.sharding import PartitionSpec as P

PIECES = 4


def product(left, right):
    return jnp.einsum("woe,wev->wov", left, right, preferred_element_type=jnp.float32)


def gradient_terms(log_grad, kin_part, weights):
    kin_grad = -0.5 * kin_part
    weighted = jnp.sum(weights[:, None, None] * log_grad + kin_grad, axis=0)
    return (weighted, jnp.sum(log_grad, axis=0))


def general_body(inverse_rows, kinetic_rows, virt_values, virt_laplacians, local_energy):
    walk_count = lax.axis_size("walk")
    walker_count = walk_count * local_energy.shape[0]
    energy_sum = lax.psum(jnp.sum(local_energy), "walk")
    average = energy_sum / walker_count
    weights = 2.0 * (local_energy - average)
    inverse_all, kinetic_all = (
        lax.all_gather(inverse_rows, "virt", axis=2, tiled=True),
        lax.all_gather(kinetic_rows, "virt", axis=2, tiled=True),
    )
    log_grad = product(inverse_all, virt_values)
    kin_part = product(inverse_all, virt_laplacians) - product(kinetic_all, virt_values)
    weighted, log_sum = gradient_terms(log_grad, kin_part, weights)
    summed = (
        lax.psum_scatter(weighted, "walk", scatter_dimension=0, tiled=True),
        lax.psum_scatter(log_sum, "walk", scatter_dimension=0, tiled=True),
    )
    gradient_part, log_part = (summed[0], summed[1])
    return (gradient_part / walker_count, log_part / walker_count)


SPAN = 248.0
EXTRA = 128
TINY = 1e-30
MIB = 1024 * 1024


def stage_masks(count):
    bits = count.bit_length() - 1
    masks = [1 << bit for bit in range(bits)]
    if bits >= 2:
        masks[-1] = 3 << (bits - 2)
    return masks


def place_weights(masks):
    bits = len(masks)
    weights = [0] * bits
    for place in range(1 << bits):
        difference = 0
        for stage, mask in enumerate(masks):
            if place >> (bits - 1 - stage) & 1:
                difference ^= mask
        if difference & (difference - 1) == 0 and difference:
            weights[difference.bit_length() - 1] = place
    return weights


def swap(array, axis, mask):
    pairs = [(source, source ^ mask) for source in range(lax.axis_size(axis))]
    return lax.ppermute(array, axis, pairs)


def encode(rows):
    magnitude = jnp.abs(rows)
    largest = jnp.maximum(jnp.max(magnitude, axis=-1, keepdims=True), TINY)
    scale = (largest * (1.0 + 2.0**-7)).astype(jnp.bfloat16)
    factor = SPAN / scale.astype(jnp.float32)
    code = jnp.exp2(magnitude * factor - SPAN / 2)
    code = jnp.where(rows < 0, -code, code).astype(jnp.bfloat16)
    return code, jnp.broadcast_to(scale, (rows.shape[0], EXTRA))


def decode(coded):
    width = coded.shape[1] - EXTRA
    code = coded[:, :width].astype(jnp.float32)
    scale = coded[:, width : width + 1].astype(jnp.float32)
    magnitude = (jnp.log2(jnp.abs(code)) + SPAN / 2) * (scale / SPAN)
    return jnp.where(code < 0, -magnitude, magnitude)


def store_coded(send_ref, blocks):
    width = send_ref.shape[1] - EXTRA
    for pair in range(len(blocks) // 2):
        code, scale = encode(jnp.concatenate(blocks[2 * pair : 2 * pair + 2], axis=0))
        target = slice(16 * pair, 16 * pair + 16)
        send_ref[target, :width] = code
        send_ref[target, width:] = scale


def add_came(keep_ref, came_ref):
    arrays, height, _ = keep_ref.shape
    per = height // 8
    sums = []
    for pair in range(arrays * per // 2):
        both = decode(came_ref[16 * pair : 16 * pair + 16, :])
        for part in range(2):
            array, block = divmod(2 * pair + part, per)
            sums.append(keep_ref[array, 8 * block : 8 * block + 8, :] + both[8 * part : 8 * part + 8])
    return [sums[array * per : (array + 1) * per] for array in range(arrays)]


def limit(mib):
    return pltpu.CompilerParams(vmem_limit_bytes=mib * MIB)


WHOLE = pl.BlockSpec(memory_space=pltpu.VMEM)
SCALAR = pl.BlockSpec(memory_space=pltpu.SMEM)
ANYWHERE = pl.BlockSpec(memory_space=pl.ANY)


def near_kernel(tile, virt_ref, mine_ref, values_ref, laps_ref, *rest):
    out_ref = rest[-1]
    _, height, depth = mine_ref.shape
    f32 = jnp.float32
    electrons = pl.ds(pl.multiple_of(virt_ref[0] * depth, depth), depth)

    @pl.loop(0, out_ref.shape[2] // tile)
    def _(index):
        columns = pl.ds(pl.multiple_of(index * tile, tile), tile)
        both = jnp.dot(mine_ref[...].reshape(2 * height, depth), values_ref[electrons, columns], preferred_element_type=f32)
        laps = jnp.dot(mine_ref[0], laps_ref[electrons, columns], preferred_element_type=f32)
        out_ref[0, :, columns] = 0.5 * (both[height:] - laps)
        out_ref[1, :, columns] = both[:height]


def near_product(virt, mine, values, laplacians, tile, after):
    _, height, depth = mine.shape
    width = values.shape[1]
    return pl.pallas_call(
        functools.partial(near_kernel, tile),
        out_shape=jax.ShapeDtypeStruct((2, height, width), jnp.float32),
        in_specs=[SCALAR, WHOLE, WHOLE, WHOLE] + [ANYWHERE] * len(after),
        out_specs=WHOLE,
        compiler_params=limit(20),
        cost_estimate=pl.CostEstimate(flops=6 * height * depth * width, bytes_accessed=0, transcendentals=0),
        name="near_product",
    )(virt, mine, values, laplacians, *after)


def far_kernel(weights, count, tile, virt_ref, me_ref, scale_ref, far_ref, near_ref, values_ref, laps_ref, *rest):
    send_ref, keep_ref, place_ref = rest[-3:]
    _, height, depth = far_ref.shape
    width = near_ref.shape[2]
    rows = height // count
    half = height // 2
    f32 = jnp.float32
    electrons = pl.ds(pl.multiple_of((1 - virt_ref[0]) * depth, depth), depth)

    @pl.loop(0, width // tile)
    def _(index):
        columns = pl.ds(pl.multiple_of(index * tile, tile), tile)
        both = jnp.dot(far_ref[...].reshape(2 * height, depth), values_ref[electrons, columns], preferred_element_type=f32)
        laps = jnp.dot(far_ref[0], laps_ref[electrons, columns], preferred_element_type=f32)
        log = both[:height] + near_ref[1, :, columns]
        weighted = scale_ref[0] * log + (0.5 * (both[height:] - laps) + near_ref[0, :, columns])
        for dest in range(count):
            difference = dest ^ me_ref[0]
            place = 0
            for bit, weight in enumerate(weights):
                place = place ^ (((difference >> bit) & 1) * weight)
            target = pl.ds(pl.multiple_of(place * rows, rows), rows)
            source = slice(dest * rows, (dest + 1) * rows)
            place_ref[0, target, columns] = weighted[source]
            place_ref[1, target, columns] = log[source]

    keep_ref[...] = place_ref[:, :half]
    store_coded(send_ref, [place_ref[array, row : row + 8, :] for array in range(2) for row in range(half, height, 8)])


def far_product(virt, me, scale, theirs, near, values, laplacians, tile, masks, after):
    _, height, depth = theirs.shape
    width = values.shape[1]
    half = height // 2
    return pl.pallas_call(
        functools.partial(far_kernel, place_weights(masks), 1 << len(masks), tile),
        out_shape=(
            jax.ShapeDtypeStruct((2 * half, width + EXTRA), jnp.bfloat16),
            jax.ShapeDtypeStruct((2, half, width), jnp.float32),
        ),
        in_specs=[SCALAR, SCALAR, SCALAR, WHOLE, WHOLE, WHOLE, WHOLE] + [ANYWHERE] * len(after),
        out_specs=(WHOLE, WHOLE),
        scratch_shapes=[pltpu.VMEM((2, height, width), jnp.float32)],
        compiler_params=limit(20),
        cost_estimate=pl.CostEstimate(flops=6 * height * depth * width, bytes_accessed=0, transcendentals=0),
        name="far_product",
    )(virt, me, scale, theirs, near, values, laplacians, *after)


def halve_kernel(keep_ref, came_ref, send_ref, kept_ref):
    sums = add_came(keep_ref, came_ref)
    kept = len(sums[0]) // 2
    for array, blocks in enumerate(sums):
        for index, block in enumerate(blocks[:kept]):
            kept_ref[array, 8 * index : 8 * index + 8, :] = block
    store_coded(send_ref, [block for blocks in sums for block in blocks[kept:]])


def halve(keep, came):
    _, height, width = keep.shape
    return pl.pallas_call(
        halve_kernel,
        out_shape=(
            jax.ShapeDtypeStruct((height, width + EXTRA), jnp.bfloat16),
            jax.ShapeDtypeStruct((2, height // 2, width), jnp.float32),
        ),
        in_specs=[WHOLE, WHOLE],
        out_specs=(WHOLE, WHOLE),
        compiler_params=limit(8),
        cost_estimate=pl.CostEstimate(flops=keep.size, bytes_accessed=0, transcendentals=0),
        name="halve",
    )(keep, came)


def finish_kernel(count, *refs):
    gradient_ref, log_ref = refs[-2:]
    pieces = (len(refs) - 2) // 2
    row = 0
    for piece in range(pieces):
        gradient, log = add_came(refs[2 * piece], refs[2 * piece + 1])
        for block in range(len(log)):
            gradient_ref[row : row + 8, :] = gradient[block] / count
            log_ref[row : row + 8, :] = log[block] / count
            row += 8


def finish(parts, count):
    _, rows, width = parts[0][0].shape
    out = jax.ShapeDtypeStruct((rows * len(parts), width), jnp.float32)
    return pl.pallas_call(
        functools.partial(finish_kernel, count),
        out_shape=(out, out),
        in_specs=[WHOLE, WHOLE] * len(parts),
        out_specs=(WHOLE, WHOLE),
        compiler_params=limit(8),
        cost_estimate=pl.CostEstimate(flops=out.size, bytes_accessed=0, transcendentals=0),
        name="finish",
    )(*[array for part in parts for array in part])


def pieced_body(pieces, tile, inverse_rows, kinetic_rows, virt_values, virt_laplacians, local_energy):
    count = lax.axis_size("walk")
    masks = stage_masks(count)
    stages = len(masks)
    me = lax.axis_index("walk").astype(jnp.int32).reshape(1)
    virt = lax.axis_index("virt").astype(jnp.int32).reshape(1)
    occupied, depth = inverse_rows.shape[1:]
    by_dest = (count, occupied // count, depth)
    inverse, kinetic = inverse_rows.reshape(by_dest), kinetic_rows.reshape(by_dest)
    values = pltpu.with_memory_space_constraint(virt_values[0], pltpu.VMEM)
    laplacians = pltpu.with_memory_space_constraint(virt_laplacians[0], pltpu.VMEM)
    rows = occupied // (count * pieces)

    mine, theirs = [], []
    for piece in range(pieces):
        part = slice(piece * rows, (piece + 1) * rows)
        taken = [array[:, part].reshape(count * rows, depth) for array in (inverse, kinetic)]
        mine.append(jnp.stack(taken))
        theirs.append(swap(mine[piece], "virt", 1))

    energy_sum = jnp.broadcast_to(local_energy, (1, 128))
    near = []
    for piece in range(pieces):
        after = [energy_sum] if piece else []
        near.append(near_product(virt, mine[piece], values, laplacians, tile, after))
        if piece < stages:
            energy_sum = energy_sum + swap(energy_sum, "walk", masks[piece])
    for mask in masks[pieces:]:
        energy_sum = energy_sum + swap(energy_sum, "walk", mask)
    average = energy_sum[0, 0] / count
    scale = 2.0 * (local_energy - average)

    send, keep, parts = {}, {}, {}
    for turn in range(pieces + stages + 1):
        after = [send[other] for other in sorted(send)]
        if turn < pieces:
            send[turn], keep[turn] = far_product(
                virt, me, scale, theirs[turn], near[turn], values, laplacians, tile, masks, after
            )
        for piece in range(turn - 1, max(turn - 1 - stages, -1), -1):
            if piece >= pieces:
                continue
            stage = turn - 1 - piece
            came = swap(send.pop(piece), "walk", masks[stage])
            if stage + 1 < stages:
                send[piece], keep[piece] = halve(keep[piece], came)
            else:
                parts[piece] = (keep[piece], came)
    return finish([parts[piece] for piece in range(pieces)], count)


def solution(mesh):
    placed = (
        P("walk", None, "virt"),
        P("walk", None, "virt"),
        P("walk", None, "virt"),
        P("walk", None, "virt"),
        P("walk"),
    )

    def body(inverse_rows, kinetic_rows, virt_values, virt_laplacians, local_energy):
        count = mesh.shape["walk"]
        walkers, occupied, depth = inverse_rows.shape
        width = virt_values.shape[2]
        tile = 512
        fits = (
            walkers == 1
            and mesh.shape["virt"] == 2
            and count >= 4
            and count & (count - 1) == 0
            and occupied % (count * PIECES * 8) == 0
            and depth % 256 == 0
            and width % tile == 0
        )
        form = functools.partial(pieced_body, PIECES, tile) if fits else general_body
        return form(inverse_rows, kinetic_rows, virt_values, virt_laplacians, local_energy)

    return jax.shard_map(
        body,
        mesh=mesh,
        in_specs=placed,
        out_specs=(P("walk", "virt"), P("walk", "virt")),
        check_vma=False,
    )
```

```python
import functools

import jax
import jax.numpy as jnp
from jax import lax
from jax.experimental import pallas as pl
from jax.experimental.pallas import tpu as pltpu
from jax.sharding import PartitionSpec as P

PIECES = 4


def product(left, right):
    return jnp.einsum("woe,wev->wov", left, right, preferred_element_type=jnp.float32)


def gradient_terms(log_grad, kin_part, weights):
    kin_grad = -0.5 * kin_part
    weighted = jnp.sum(weights[:, None, None] * log_grad + kin_grad, axis=0)
    return (weighted, jnp.sum(log_grad, axis=0))


def general_body(inverse_rows, kinetic_rows, virt_values, virt_laplacians, local_energy):
    walk_count = lax.axis_size("walk")
    walker_count = walk_count * local_energy.shape[0]
    energy_sum = lax.psum(jnp.sum(local_energy), "walk")
    average = energy_sum / walker_count
    weights = 2.0 * (local_energy - average)
    inverse_all, kinetic_all = (
        lax.all_gather(inverse_rows, "virt", axis=2, tiled=True),
        lax.all_gather(kinetic_rows, "virt", axis=2, tiled=True),
    )
    log_grad = product(inverse_all, virt_values)
    kin_part = product(inverse_all, virt_laplacians) - product(kinetic_all, virt_values)
    weighted, log_sum = gradient_terms(log_grad, kin_part, weights)
    summed = (
        lax.psum_scatter(weighted, "walk", scatter_dimension=0, tiled=True),
        lax.psum_scatter(log_sum, "walk", scatter_dimension=0, tiled=True),
    )
    gradient_part, log_part = (summed[0], summed[1])
    return (gradient_part / walker_count, log_part / walker_count)


SPAN = 248.0
EXTRA = 128
PART = EXTRA // 4
OFFSET = 3.1
TINY = 1e-30
MIB = 1024 * 1024


def stage_masks(count):
    bits = count.bit_length() - 1
    masks = [1 << bit for bit in range(bits)]
    if bits >= 2:
        masks[-1] = 3 << (bits - 2)
    return masks


def place_weights(masks):
    bits = len(masks)
    weights = [0] * bits
    for place in range(1 << bits):
        difference = 0
        for stage, mask in enumerate(masks):
            if place >> (bits - 1 - stage) & 1:
                difference ^= mask
        if difference & (difference - 1) == 0 and difference:
            weights[difference.bit_length() - 1] = place
    return weights


def piece_masks(count, piece):
    masks = stage_masks(count)
    if piece % 2 and len(masks) >= 4:
        masks[1], masks[2] = masks[2], masks[1]
    return masks


def swap(array, axis, mask):
    pairs = [(source, source ^ mask) for source in range(lax.axis_size(axis))]
    return lax.ppermute(array, axis, pairs)


def encode(rows):
    magnitude = jnp.abs(rows)
    largest = jnp.maximum(jnp.max(magnitude, axis=-1, keepdims=True), TINY)
    scale = (largest * (1.0 + 2.0**-7)).astype(jnp.bfloat16).astype(jnp.float32)
    code = jnp.exp2(magnitude * (SPAN / scale) - SPAN / 2)
    return jnp.where(rows < 0, -code, code).astype(jnp.bfloat16), scale


def decode(coded):
    width = coded.shape[1] - EXTRA
    code = coded[:, :width].astype(jnp.float32)
    scale = coded[:, width : width + 1].astype(jnp.float32)
    magnitude = (jnp.log2(jnp.abs(code)) + SPAN / 2) * (scale / SPAN)
    return jnp.where(code < 0, -magnitude, magnitude)


def store_coded(send_ref, blocks, energy):
    width = send_ref.shape[1] - EXTRA
    f32, bf16 = jnp.float32, jnp.bfloat16
    energy = jnp.concatenate([energy, energy], axis=0)
    high = energy.astype(bf16).astype(f32)
    middle = (energy - high).astype(bf16).astype(f32)
    low = energy - high - middle
    lane = lax.broadcasted_iota(jnp.int32, energy.shape, 1)
    terms = jnp.where(lane < 2 * PART, high, jnp.where(lane < 3 * PART, middle, low))
    for pair in range(len(blocks) // 2):
        code, scale = encode(jnp.concatenate(blocks[2 * pair : 2 * pair + 2], axis=0))
        target = slice(16 * pair, 16 * pair + 16)
        send_ref[target, :width] = code
        send_ref[target, width:] = jnp.where(lane < PART, scale, terms).astype(bf16)


def add_came(keep_ref, came_ref):
    arrays, height, width = keep_ref.shape
    width -= EXTRA
    per = height // 8
    sums = []
    for pair in range(arrays * per // 2):
        both = decode(came_ref[16 * pair : 16 * pair + 16, :])
        for part in range(2):
            array, block = divmod(2 * pair + part, per)
            sums.append(keep_ref[array, 8 * block : 8 * block + 8, :width] + both[8 * part : 8 * part + 8])
    terms = came_ref[:16, width:].astype(jnp.float32)[:8]
    came = terms[:, PART : PART + 1] + terms[:, 2 * PART : 2 * PART + 1] + terms[:, 3 * PART : 3 * PART + 1]
    energy = keep_ref[0, :8, width:] + came
    return [sums[array * per : (array + 1) * per] for array in range(arrays)], energy


def limit(mib):
    return pltpu.CompilerParams(vmem_limit_bytes=mib * MIB)


def cost(microseconds):
    return pl.CostEstimate(flops=int(microseconds * 1.1e9), bytes_accessed=0, transcendentals=0)


WHOLE = pl.BlockSpec(memory_space=pltpu.VMEM)
SCALAR = pl.BlockSpec(memory_space=pltpu.SMEM)
ANYWHERE = pl.BlockSpec(memory_space=pl.ANY)
HELD = pl.BlockSpec(memory_space=pltpu.HBM)


def near_kernel(chunk, tile, virt_ref, inverse_ref, kinetic_ref, values_ref, laps_ref, out_ref, far_values, far_laps, near_values, near_laps, sems):
    count, per, depth = inverse_ref.shape
    height = count * per
    width = out_ref.shape[3]
    f32 = jnp.float32
    own = pl.ds(pl.multiple_of(virt_ref[0] * depth, depth), depth)
    other = pl.ds(pl.multiple_of((1 - virt_ref[0]) * depth, depth), depth)
    chunks = width // chunk

    copies = []
    for index in range(chunks):
        columns = pl.ds(index * chunk, chunk)
        copies.append([
            pltpu.make_async_copy(table.at[own, columns], held.at[:, columns], sems.at[index, which])
            for which, (table, held) in enumerate(((values_ref, near_values), (laps_ref, near_laps)))
        ])
    last = [
        pltpu.make_async_copy(table.at[other, :], held, sems.at[chunks, which])
        for which, (table, held) in enumerate(((values_ref, far_values), (laps_ref, far_laps)))
    ]
    for copy in sum(copies, []) + last:
        copy.start()
    inverse = inverse_ref[...].reshape(height, depth)
    kinetic = kinetic_ref[...].reshape(height, depth)
    for index in range(chunks):
        for copy in copies[index]:
            copy.wait()

        @pl.loop(index * chunk // tile, (index + 1) * chunk // tile)
        def _(step):
            columns = pl.ds(pl.multiple_of(step * tile, tile), tile)
            values, laps = near_values[:, columns], near_laps[:, columns]
            out_ref[1, :, :, columns] = jnp.dot(inverse, values, preferred_element_type=f32).reshape(count, per, tile)
            rest = jnp.dot(kinetic, values, preferred_element_type=f32)
            rest -= jnp.dot(inverse, laps, preferred_element_type=f32)
            out_ref[0, :, :, columns] = (0.5 * rest).reshape(count, per, tile)

    for copy in last:
        copy.wait()


def near_product(virt, inverse, kinetic, values, laplacians):
    count, per, depth = inverse.shape
    width = values.shape[1]
    chunk, tile = 512, 256
    table = pltpu.VMEM((depth, width), jnp.bfloat16)
    return pl.pallas_call(
        functools.partial(near_kernel, chunk, tile),
        out_shape=(jax.ShapeDtypeStruct((2, count, per, width), jnp.float32), table, table),
        in_specs=[SCALAR, WHOLE, WHOLE, HELD, HELD],
        out_specs=(WHOLE, WHOLE, WHOLE),
        scratch_shapes=[table, table, pltpu.SemaphoreType.DMA((width // chunk + 1, 2))],
        compiler_params=limit(24),
        cost_estimate=cost(9),
        name="near_product",
    )(virt, inverse, kinetic, values, laplacians)


def far_kernel(weights, count, tile, first, virt_ref, me_ref, energy_ref, far_ref, near_ref, values_ref, laps_ref, *rest):
    send_ref, keep_ref, place_ref = rest[-3:]
    _, height, depth = far_ref.shape
    width = near_ref.shape[3]
    rows = height // count
    half = height // 2
    f32 = jnp.float32
    scale = 2.0 * (energy_ref[0] - OFFSET)

    @pl.loop(0, width // tile)
    def _(index):
        columns = pl.ds(pl.multiple_of(index * tile, tile), tile)
        near = near_ref[:, :, first : first + rows, columns].reshape(2, height, tile)
        both = jnp.dot(far_ref[...].reshape(2 * height, depth), values_ref[:, columns], preferred_element_type=f32)
        laps = jnp.dot(far_ref[0], laps_ref[:, columns], preferred_element_type=f32)
        log = both[:height] + near[1]
        weighted = scale * log + (0.5 * (both[height:] - laps) + near[0])
        for dest in range(count):
            difference = dest ^ me_ref[0]
            place = 0
            for bit, weight in enumerate(weights):
                place = place ^ (((difference >> bit) & 1) * weight)
            target = pl.ds(pl.multiple_of(place * rows, rows), rows)
            source = slice(dest * rows, (dest + 1) * rows)
            place_ref[0, target, columns] = weighted[source]
            place_ref[1, target, columns] = log[source]

    energy = jnp.full((8, EXTRA), energy_ref[0], f32)
    keep_ref[:, :, :width] = place_ref[:, :half]
    keep_ref[0, :8, width:] = energy
    blocks = [place_ref[array, row : row + 8, :] for array in range(2) for row in range(half, height, 8)]
    store_coded(send_ref, blocks, energy)


def far_product(virt, me, energy, theirs, near, first, values, laplacians, tile, masks, after):
    _, height, depth = theirs.shape
    width = values.shape[1]
    half = height // 2
    return pl.pallas_call(
        functools.partial(far_kernel, place_weights(masks), 1 << len(masks), tile, first),
        out_shape=(
            jax.ShapeDtypeStruct((2 * half, width + EXTRA), jnp.bfloat16),
            jax.ShapeDtypeStruct((2, half, width + EXTRA), jnp.float32),
        ),
        in_specs=[SCALAR, SCALAR, SCALAR, WHOLE, WHOLE, WHOLE, WHOLE] + [ANYWHERE] * len(after),
        out_specs=(WHOLE, WHOLE),
        scratch_shapes=[pltpu.VMEM((2, height, width), jnp.float32)],
        compiler_params=limit(24),
        cost_estimate=cost(10),
        name="far_product",
    )(virt, me, energy, theirs, near, values, laplacians, *after)


def halve_kernel(keep_ref, came_ref, send_ref, kept_ref):
    width = keep_ref.shape[2] - EXTRA
    sums, energy = add_came(keep_ref, came_ref)
    kept = len(sums[0]) // 2
    for array, blocks in enumerate(sums):
        for index, block in enumerate(blocks[:kept]):
            kept_ref[array, 8 * index : 8 * index + 8, :width] = block
    kept_ref[0, :8, width:] = energy
    store_coded(send_ref, [block for blocks in sums for block in blocks[kept:]], energy)


def halve(keep, came):
    _, height, width = keep.shape
    return pl.pallas_call(
        halve_kernel,
        out_shape=(
            jax.ShapeDtypeStruct((height, width), jnp.bfloat16),
            jax.ShapeDtypeStruct((2, height // 2, width), jnp.float32),
        ),
        in_specs=[WHOLE, WHOLE],
        out_specs=(WHOLE, WHOLE),
        compiler_params=limit(8),
        cost_estimate=cost(0.5),
        name="halve",
    )(keep, came)


def finish_kernel(count, *refs):
    gradient_ref, log_ref = refs[-2:]
    pieces = (len(refs) - 2) // 2
    row = 0
    for piece in range(pieces):
        (gradient, log), energy = add_came(refs[2 * piece], refs[2 * piece + 1])
        correction = 2.0 * (energy[:, :1] / count - OFFSET)
        for block in range(len(log)):
            log_mean = log[block] / count
            gradient_ref[row : row + 8, :] = gradient[block] / count - correction * log_mean
            log_ref[row : row + 8, :] = log_mean
            row += 8


def finish(parts, count):
    _, rows, width = parts[0][0].shape
    out = jax.ShapeDtypeStruct((rows * len(parts), width - EXTRA), jnp.float32)
    return pl.pallas_call(
        functools.partial(finish_kernel, count),
        out_shape=(out, out),
        in_specs=[WHOLE, WHOLE] * len(parts),
        out_specs=(WHOLE, WHOLE),
        compiler_params=limit(8),
        cost_estimate=cost(0.5),
        name="finish",
    )(*[array for part in parts for array in part])


def plan(pieces, stages):
    left = [stages] * pieces
    turns = []
    for turn in range(pieces):
        steps = [piece for piece in range(turn) if left[piece]]
        if turn == pieces - 2 and turn >= 1:
            steps.append(turn - 1)
        for piece in steps:
            left[piece] -= 1
        turns.append(steps)
    last = []
    while any(left):
        for piece in range(pieces):
            if left[piece]:
                left[piece] -= 1
                last.append(piece)
    turns[-1] = turns[-1] + last
    return turns


def pieced_body(pieces, tile, inverse_rows, kinetic_rows, virt_values, virt_laplacians, local_energy):
    count = lax.axis_size("walk")
    masks = [piece_masks(count, piece) for piece in range(pieces)]
    stages = len(masks[0])
    me = lax.axis_index("walk").astype(jnp.int32).reshape(1)
    virt = lax.axis_index("virt").astype(jnp.int32).reshape(1)
    occupied, depth = inverse_rows.shape[1:]
    by_dest = (count, occupied // count, depth)
    inverse, kinetic = inverse_rows.reshape(by_dest), kinetic_rows.reshape(by_dest)
    rows = occupied // (count * pieces)

    theirs = []
    for piece in range(pieces):
        part = slice(piece * rows, (piece + 1) * rows)
        taken = [array[:, part].reshape(count * rows, depth) for array in (inverse, kinetic)]
        theirs.append(swap(jnp.stack(taken), "virt", 1))
    tables = [pltpu.with_memory_space_constraint(table[0], pltpu.HBM) for table in (virt_values, virt_laplacians)]
    near, values, laplacians = near_product(virt, inverse, kinetic, *tables)

    send, keep, parts = {}, {}, {}
    stage = [0] * pieces
    for turn, steps in enumerate(plan(pieces, stages)):
        if turn < pieces:
            after = [send[other] for other in sorted(send)]
            send[turn], keep[turn] = far_product(
                virt, me, local_energy, theirs[turn], near, turn * rows, values, laplacians, tile, masks[turn], after
            )
        for piece in steps:
            came = swap(send.pop(piece), "walk", masks[piece][stage[piece]])
            stage[piece] += 1
            if stage[piece] < stages:
                send[piece], keep[piece] = halve(keep[piece], came)
            else:
                parts[piece] = (keep[piece], came)
    return finish([parts[piece] for piece in range(pieces)], count)


def solution(mesh):
    placed = (
        P("walk", None, "virt"),
        P("walk", None, "virt"),
        P("walk", None, "virt"),
        P("walk", None, "virt"),
        P("walk"),
    )

    def body(inverse_rows, kinetic_rows, virt_values, virt_laplacians, local_energy):
        count = mesh.shape["walk"]
        walkers, occupied, depth = inverse_rows.shape
        width = virt_values.shape[2]
        tile = 512
        fits = (
            walkers == 1
            and mesh.shape["virt"] == 2
            and count >= 4
            and count & (count - 1) == 0
            and occupied % (count * PIECES * 8) == 0
            and depth % 256 == 0
            and width % tile == 0
        )
        form = functools.partial(pieced_body, PIECES, tile) if fits else general_body
        return form(inverse_rows, kinetic_rows, virt_values, virt_laplacians, local_energy)

    return jax.shard_map(
        body,
        mesh=mesh,
        in_specs=placed,
        out_specs=(P("walk", "virt"), P("walk", "virt")),
        check_vma=False,
    )
```

```python
import functools

import jax
import jax.numpy as jnp
from jax import lax
from jax.experimental import pallas as pl
from jax.experimental.pallas import tpu as pltpu
from jax.sharding import PartitionSpec as P

PIECES = 4
SPLIT = 4


def product(left, right):
    return jnp.einsum("woe,wev->wov", left, right, preferred_element_type=jnp.float32)


def gradient_terms(log_grad, kin_part, weights):
    kin_grad = -0.5 * kin_part
    weighted = jnp.sum(weights[:, None, None] * log_grad + kin_grad, axis=0)
    return (weighted, jnp.sum(log_grad, axis=0))


def general_body(inverse_rows, kinetic_rows, virt_values, virt_laplacians, local_energy):
    walk_count = lax.axis_size("walk")
    walker_count = walk_count * local_energy.shape[0]
    energy_sum = lax.psum(jnp.sum(local_energy), "walk")
    average = energy_sum / walker_count
    weights = 2.0 * (local_energy - average)
    inverse_all, kinetic_all = (
        lax.all_gather(inverse_rows, "virt", axis=2, tiled=True),
        lax.all_gather(kinetic_rows, "virt", axis=2, tiled=True),
    )
    log_grad = product(inverse_all, virt_values)
    kin_part = product(inverse_all, virt_laplacians) - product(kinetic_all, virt_values)
    weighted, log_sum = gradient_terms(log_grad, kin_part, weights)
    summed = (
        lax.psum_scatter(weighted, "walk", scatter_dimension=0, tiled=True),
        lax.psum_scatter(log_sum, "walk", scatter_dimension=0, tiled=True),
    )
    gradient_part, log_part = (summed[0], summed[1])
    return (gradient_part / walker_count, log_part / walker_count)


SPAN = 248.0
EXTRA = 128
PART = EXTRA // 4
OFFSET = 3.1
TINY = 1e-30
MIB = 1024 * 1024


def stage_masks(count):
    bits = [1 << bit for bit in range(count.bit_length() - 1)]
    if len(bits) < 3:
        return [[bit] for bit in bits]
    return [bits[:1], bits[1:3]] + [[bit] for bit in bits[3:]]


def place_weights(stages):
    order = [mask for stage in stages for mask in stage]
    weights = [0] * len(order)
    for index, mask in enumerate(order):
        weights[mask.bit_length() - 1] = 1 << (len(order) - 1 - index)
    return weights


def partners(stage):
    if len(stage) == 1:
        return list(stage)
    first, second = stage
    return [second, first, first ^ second]


def swap(array, axis, mask):
    pairs = [(source, source ^ mask) for source in range(lax.axis_size(axis))]
    return lax.ppermute(array, axis, pairs)


def encode(rows):
    magnitude = jnp.abs(rows)
    largest = jnp.maximum(jnp.max(magnitude, axis=-1, keepdims=True), TINY)
    scale = (largest * (1.0 + 2.0**-7)).astype(jnp.bfloat16).astype(jnp.float32)
    code = jnp.exp2(magnitude * (SPAN / scale) - SPAN / 2)
    return jnp.where(rows < 0, -code, code).astype(jnp.bfloat16), scale


def decode(coded):
    width = coded.shape[1] - EXTRA
    code = coded[:, :width].astype(jnp.float32)
    scale = coded[:, width : width + 1].astype(jnp.float32)
    magnitude = (jnp.log2(jnp.abs(code)) + SPAN / 2) * (scale / SPAN)
    return jnp.where(code < 0, -magnitude, magnitude)


def store_coded(send_refs, blocks, energy):
    width = send_refs[0].shape[1] - EXTRA
    each = send_refs[0].shape[0]
    f32, bf16 = jnp.float32, jnp.bfloat16
    energy = jnp.concatenate([energy, energy], axis=0)
    high = energy.astype(bf16).astype(f32)
    middle = (energy - high).astype(bf16).astype(f32)
    low = energy - high - middle
    lane = lax.broadcasted_iota(jnp.int32, energy.shape, 1)
    terms = jnp.where(lane < 2 * PART, high, jnp.where(lane < 3 * PART, middle, low))
    for pair in range(len(blocks) // 2):
        code, scale = encode(jnp.concatenate(blocks[2 * pair : 2 * pair + 2], axis=0))
        send_ref = send_refs[16 * pair // each]
        target = slice(16 * pair % each, 16 * pair % each + 16)
        send_ref[target, :width] = code
        send_ref[target, width:] = jnp.where(lane < PART, scale, terms).astype(bf16)


def add_came(keep_ref, came_refs):
    arrays, height, width = keep_ref.shape
    width -= EXTRA
    per = height // 8
    sums = [keep_ref[index // per, 8 * (index % per) : 8 * (index % per) + 8, :width] for index in range(arrays * per)]
    energy = keep_ref[0, :8, width:]
    for parts in came_refs:
        index = 0
        for part in parts:
            for row in range(0, part.shape[0], 16):
                both = decode(part[row : row + 16, :])
                sums[index] += both[:8]
                sums[index + 1] += both[8:]
                index += 2
        terms = parts[0][:16, width:].astype(jnp.float32)[:8]
        for term in range(1, 4):
            energy += terms[:, term * PART : term * PART + 1]
    return [sums[array * per : (array + 1) * per] for array in range(arrays)], energy


def limit(mib):
    return pltpu.CompilerParams(vmem_limit_bytes=mib * MIB)


def cost(microseconds):
    return pl.CostEstimate(flops=int(microseconds * 1.1e9), bytes_accessed=0, transcendentals=0)


WHOLE = pl.BlockSpec(memory_space=pltpu.VMEM)
SCALAR = pl.BlockSpec(memory_space=pltpu.SMEM)
ANYWHERE = pl.BlockSpec(memory_space=pl.ANY)
HELD = pl.BlockSpec(memory_space=pltpu.HBM)
HELD = pl.BlockSpec(memory_space=pltpu.HBM)


def cut_kernel(inverse_ref, kinetic_ref, *out_refs):
    count = inverse_ref.shape[0]
    for array, ref in enumerate((inverse_ref, kinetic_ref)):
        for dest in range(0, count, 2):
            pair = [ref[dest + other].astype(jnp.float32) for other in range(2)]
            for index, out_ref in enumerate(out_refs):
                rows = jnp.concatenate([block[8 * index : 8 * index + 8] for block in pair], axis=0)
                out_ref[array, 8 * dest : 8 * dest + 16, :] = rows.astype(jnp.bfloat16)


def cut(inverse, kinetic, group):
    count, _, depth = inverse.shape
    block = pl.BlockSpec((count, 16, depth), lambda step: (0, group, 0))
    out = jax.ShapeDtypeStruct((2, 8 * count, depth), jnp.bfloat16)
    return pl.pallas_call(
        cut_kernel,
        out_shape=(out, out),
        grid=(1,),
        in_specs=[block, block],
        out_specs=(pl.BlockSpec(out.shape, lambda step: (0, 0, 0)),) * 2,
        compiler_params=limit(12),
        cost_estimate=cost(0.1),
        name="cut",
    )(inverse, kinetic)


def near_kernel(chunk, tile, virt_ref, inverse_ref, kinetic_ref, values_ref, laps_ref, out_ref, far_values, far_laps, near_values, near_laps, own_inverse, own_kinetic, sems):
    count, per, depth = inverse_ref.shape
    height = count * per
    width = out_ref.shape[3]
    f32 = jnp.float32
    own = pl.ds(pl.multiple_of(virt_ref[0] * depth, depth), depth)
    other = pl.ds(pl.multiple_of((1 - virt_ref[0]) * depth, depth), depth)
    chunks = width // chunk

    copies = []
    for index in range(chunks):
        columns = pl.ds(index * chunk, chunk)
        copies.append([
            pltpu.make_async_copy(table.at[own, columns], held.at[:, columns], sems.at[index, which])
            for which, (table, held) in enumerate(((values_ref, near_values), (laps_ref, near_laps)))
        ])
    last = [
        pltpu.make_async_copy(table.at[other, :], held, sems.at[chunks, which])
        for which, (table, held) in enumerate(((values_ref, far_values), (laps_ref, far_laps)))
    ]
    first = [
        pltpu.make_async_copy(rows, held, sems.at[chunks + 1, which])
        for which, (rows, held) in enumerate(((inverse_ref, own_inverse), (kinetic_ref, own_kinetic)))
    ]
    for copy in first + sum(copies, []) + last:
        copy.start()
    for copy in first:
        copy.wait()
    inverse = own_inverse[...].reshape(height, depth)
    kinetic = own_kinetic[...].reshape(height, depth)
    for index in range(chunks):
        for copy in copies[index]:
            copy.wait()

        @pl.loop(index * chunk // tile, (index + 1) * chunk // tile)
        def _(step):
            columns = pl.ds(pl.multiple_of(step * tile, tile), tile)
            values, laps = near_values[:, columns], near_laps[:, columns]
            out_ref[1, :, :, columns] = jnp.dot(inverse, values, preferred_element_type=f32).reshape(count, per, tile)
            rest = jnp.dot(kinetic, values, preferred_element_type=f32)
            rest -= jnp.dot(inverse, laps, preferred_element_type=f32)
            out_ref[0, :, :, columns] = (0.5 * rest).reshape(count, per, tile)

    for copy in last:
        copy.wait()


def near_product(virt, inverse, kinetic, values, laplacians):
    count, per, depth = inverse.shape
    width = values.shape[1]
    chunk, tile = 512, 256
    table = pltpu.VMEM((depth, width), jnp.bfloat16)
    own = pltpu.VMEM((count, per, depth), jnp.bfloat16)
    return pl.pallas_call(
        functools.partial(near_kernel, chunk, tile),
        out_shape=(jax.ShapeDtypeStruct((2, count, per, width), jnp.float32), table, table),
        in_specs=[SCALAR, HELD, HELD, HELD, HELD],
        out_specs=(WHOLE, WHOLE, WHOLE),
        scratch_shapes=[table, table, own, own, pltpu.SemaphoreType.DMA((width // chunk + 2, 2))],
        compiler_params=limit(24),
        cost_estimate=cost(9),
        name="near_product",
    )(virt, inverse, kinetic, values, laplacians)


def far_kernel(weights, count, tile, first, virt_ref, me_ref, energy_ref, far_ref, near_ref, values_ref, laps_ref, *rest):
    send_refs, (keep_ref, place_ref) = rest[-SPLIT - 2 : -2], rest[-2:]
    _, height, depth = far_ref.shape
    width = near_ref.shape[3]
    rows = height // count
    half = height // 2
    f32 = jnp.float32
    scale = 2.0 * (energy_ref[0] - OFFSET)

    @pl.loop(0, width // tile)
    def _(index):
        columns = pl.ds(pl.multiple_of(index * tile, tile), tile)
        near = near_ref[:, :, first : first + rows, columns].reshape(2, height, tile)
        both = jnp.dot(far_ref[...].reshape(2 * height, depth), values_ref[:, columns], preferred_element_type=f32)
        laps = jnp.dot(far_ref[0], laps_ref[:, columns], preferred_element_type=f32)
        log = both[:height] + near[1]
        weighted = scale * log + (0.5 * (both[height:] - laps) + near[0])
        for dest in range(count):
            difference = dest ^ me_ref[0]
            place = 0
            for bit, weight in enumerate(weights):
                place = place ^ (((difference >> bit) & 1) * weight)
            target = pl.ds(pl.multiple_of(place * rows, rows), rows)
            source = slice(dest * rows, (dest + 1) * rows)
            place_ref[0, target, columns] = weighted[source]
            place_ref[1, target, columns] = log[source]

    energy = jnp.full((8, EXTRA), energy_ref[0], f32)
    keep_ref[:, :, :width] = place_ref[:, :half]
    keep_ref[0, :8, width:] = energy
    blocks = [place_ref[array, row : row + 8, :] for array in range(2) for row in range(half, height, 8)]
    store_coded(send_refs, blocks, energy)


def far_product(virt, me, energy, theirs, near, first, values, laplacians, tile, stages, after):
    _, height, depth = theirs.shape
    width = values.shape[1]
    half = height // 2
    count = 1 << sum(len(stage) for stage in stages)
    *sends, keep = pl.pallas_call(
        functools.partial(far_kernel, place_weights(stages), count, tile, first),
        out_shape=(jax.ShapeDtypeStruct((2 * half // SPLIT, width + EXTRA), jnp.bfloat16),) * SPLIT
        + (jax.ShapeDtypeStruct((2, half, width + EXTRA), jnp.float32),),
        in_specs=[SCALAR, SCALAR, SCALAR, WHOLE, WHOLE, WHOLE, WHOLE] + [ANYWHERE] * len(after),
        out_specs=(WHOLE,) * (SPLIT + 1),
        scratch_shapes=[pltpu.VMEM((2, height, width), jnp.float32)],
        compiler_params=limit(24),
        cost_estimate=cost(0.1),
        name="far_product",
    )(virt, me, energy, theirs, near, values, laplacians, *after)
    return [sends], keep


def combine_kernel(parts, senders, carried, *refs):
    keep_ref, refs = refs[0], refs[1:]
    came_refs = [refs[parts * sender : parts * sender + parts] for sender in range(senders)]
    refs = refs[parts * senders :]
    kept_ref, send_refs = refs[carried], refs[carried + 1 :]
    width = keep_ref.shape[2] - EXTRA
    sums, energy = add_came(keep_ref, came_refs)
    kept = kept_ref.shape[1] // 8
    for array, blocks in enumerate(sums):
        for index, block in enumerate(blocks[:kept]):
            kept_ref[array, 8 * index : 8 * index + 8, :width] = block
    kept_ref[0, :8, width:] = energy
    for index, send_ref in enumerate(send_refs):
        if carried:
            above = refs[0].shape[0]
            send_ref[:above, :] = refs[0][...]
            send_ref = send_ref.at[above:, :]
        first = kept * (index + 1)
        store_coded([send_ref], [block for blocks in sums for block in blocks[first : first + kept]], energy)


def combine(keep, came, sent, carry=()):
    _, height, width = keep.shape
    kept = height // (sent + 1)
    parts, senders = len(came[0]), len(came)
    above = sum(array.shape[0] for array in carry)
    keep, *sends = pl.pallas_call(
        functools.partial(combine_kernel, parts, senders, len(carry)),
        out_shape=(jax.ShapeDtypeStruct((2, kept, width), jnp.float32),)
        + (jax.ShapeDtypeStruct((above + 2 * kept, width), jnp.bfloat16),) * sent,
        in_specs=[WHOLE] * (1 + parts * senders + len(carry)),
        out_specs=(WHOLE,) * (1 + sent),
        compiler_params=limit(8),
        cost_estimate=cost(0.1),
        name="combine",
    )(keep, *[part for parts in came for part in parts], *carry)
    return [[send] for send in sends], keep


def finish_kernel(count, *refs):
    keep_refs, (early_ref, late_ref, gradient_ref, log_ref) = refs[:-4], refs[-4:]
    row = 0
    for piece, keep_ref in enumerate(keep_refs):
        came = early_ref.at[16 * piece : 16 * piece + 16, :] if piece + 1 < len(keep_refs) else late_ref
        (gradient, log), energy = add_came(keep_ref, [[came]])
        correction = 2.0 * (energy[:, :1] / count - OFFSET)
        for block in range(len(log)):
            log_mean = log[block] / count
            gradient_ref[row : row + 8, :] = gradient[block] / count - correction * log_mean
            log_ref[row : row + 8, :] = log_mean
            row += 8


def finish(keeps, early, late, count):
    _, rows, width = keeps[0].shape
    out = jax.ShapeDtypeStruct((rows * len(keeps), width - EXTRA), jnp.float32)
    return pl.pallas_call(
        functools.partial(finish_kernel, count),
        out_shape=(out, out),
        in_specs=[WHOLE] * (len(keeps) + 2),
        out_specs=(WHOLE, WHOLE),
        compiler_params=limit(8),
        cost_estimate=cost(0.1),
        name="finish",
    )(*keeps, early, late)


def pieced_body(pieces, tile, inverse_rows, kinetic_rows, virt_values, virt_laplacians, local_energy):
    count = lax.axis_size("walk")
    stages = stage_masks(count)
    me = lax.axis_index("walk").astype(jnp.int32).reshape(1)
    virt = lax.axis_index("virt").astype(jnp.int32).reshape(1)
    occupied, depth = inverse_rows.shape[1:]
    by_dest = (count, occupied // count, depth)
    inverse, kinetic = inverse_rows.reshape(by_dest), kinetic_rows.reshape(by_dest)
    rows = occupied // (count * pieces)

    inverse, kinetic, values, laplacians = (
        pltpu.with_memory_space_constraint(array, pltpu.HBM)
        for array in (inverse, kinetic, virt_values[0], virt_laplacians[0])
    )
    theirs = []
    for group in range(pieces // 2):
        theirs += [swap(mine, "virt", 1) for mine in cut(inverse, kinetic, group)]
    near, values, laplacians = near_product(virt, inverse, kinetic, values, laplacians)

    send, keep, done = {}, {}, [0] * pieces
    carry = ()
    for turn in range(pieces + 1):
        if turn < pieces:
            after = [keep[other] for other in sorted(keep)]
            send[turn], keep[turn] = far_product(
                virt, me, local_energy, theirs[turn], near, turn * rows, values, laplacians, tile, stages, after
            )
        for piece in (turn - 1, turn):
            if not 0 <= piece < pieces:
                continue
            masks = partners(stages[done[piece]])
            came = [[swap(part, "walk", mask) for part in parts] for parts, mask in zip(send[piece], masks)]
            done[piece] += 1
            sent = len(partners(stages[done[piece]]))
            joins = carry if done[piece] == 2 and piece + 1 < pieces else ()
            send[piece], keep[piece] = combine(keep[piece], came, sent, joins)
            if done[piece] == 2 and piece + 1 < pieces:
                carry = tuple(send[piece][0])
    early, late = (swap(array, "walk", stages[2][0]) for array in (carry[0], send[pieces - 1][0][0]))
    return finish([keep[piece] for piece in range(pieces)], early, late, count)


def solution(mesh):
    placed = (
        P("walk", None, "virt"),
        P("walk", None, "virt"),
        P("walk", None, "virt"),
        P("walk", None, "virt"),
        P("walk"),
    )

    def body(inverse_rows, kinetic_rows, virt_values, virt_laplacians, local_energy):
        count = mesh.shape["walk"]
        walkers, occupied, depth = inverse_rows.shape
        width = virt_values.shape[2]
        tile = 512
        fits = (
            walkers == 1
            and mesh.shape["virt"] == 2
            and count == 16
            and count >= 4
            and occupied == count * PIECES * 8
            and depth % 256 == 0
            and width % tile == 0
        )
        form = functools.partial(pieced_body, PIECES, tile) if fits else general_body
        return form(inverse_rows, kinetic_rows, virt_values, virt_laplacians, local_energy)

    return jax.shard_map(
        body,
        mesh=mesh,
        in_specs=placed,
        out_specs=(P("walk", "virt"), P("walk", "virt")),
        check_vma=False,
    )
```

```python
import functools

import jax
import jax.numpy as jnp
from jax import lax
from jax.experimental import pallas as pl
from jax.experimental.pallas import tpu as pltpu
from jax.sharding import PartitionSpec as P

PIECES = 4
SPLIT = 4
JOINT = 2


def product(left, right):
    return jnp.einsum("woe,wev->wov", left, right, preferred_element_type=jnp.float32)


def gradient_terms(log_grad, kin_part, weights):
    kin_grad = -0.5 * kin_part
    weighted = jnp.sum(weights[:, None, None] * log_grad + kin_grad, axis=0)
    return (weighted, jnp.sum(log_grad, axis=0))


def general_body(inverse_rows, kinetic_rows, virt_values, virt_laplacians, local_energy):
    walk_count = lax.axis_size("walk")
    walker_count = walk_count * local_energy.shape[0]
    energy_sum = lax.psum(jnp.sum(local_energy), "walk")
    average = energy_sum / walker_count
    weights = 2.0 * (local_energy - average)
    inverse_all, kinetic_all = (
        lax.all_gather(inverse_rows, "virt", axis=2, tiled=True),
        lax.all_gather(kinetic_rows, "virt", axis=2, tiled=True),
    )
    log_grad = product(inverse_all, virt_values)
    kin_part = product(inverse_all, virt_laplacians) - product(kinetic_all, virt_values)
    weighted, log_sum = gradient_terms(log_grad, kin_part, weights)
    summed = (
        lax.psum_scatter(weighted, "walk", scatter_dimension=0, tiled=True),
        lax.psum_scatter(log_sum, "walk", scatter_dimension=0, tiled=True),
    )
    gradient_part, log_part = (summed[0], summed[1])
    return (gradient_part / walker_count, log_part / walker_count)


SPAN = 248.0
EXTRA = 128
PART = EXTRA // 4
OFFSET = 3.1
TINY = 1e-30
MIB = 1024 * 1024


def stage_masks(count):
    bits = [1 << bit for bit in range(count.bit_length() - 1)]
    if len(bits) < 3:
        return [[bit] for bit in bits]
    return [bits[:1], bits[1:3]] + [[bit] for bit in bits[3:]]


def place_weights(stages):
    order = [mask for stage in stages for mask in stage]
    weights = [0] * len(order)
    for index, mask in enumerate(order):
        weights[mask.bit_length() - 1] = 1 << (len(order) - 1 - index)
    return weights


def partners(stage):
    if len(stage) == 1:
        return list(stage)
    first, second = stage
    return [second, first, first ^ second]


def swap(array, axis, mask):
    pairs = [(source, source ^ mask) for source in range(lax.axis_size(axis))]
    return lax.ppermute(array, axis, pairs)


def encode(rows):
    magnitude = jnp.abs(rows)
    largest = jnp.maximum(jnp.max(magnitude, axis=-1, keepdims=True), TINY)
    scale = (largest * (1.0 + 2.0**-7)).astype(jnp.bfloat16).astype(jnp.float32)
    code = jnp.exp2(magnitude * (SPAN / scale) - SPAN / 2)
    return jnp.where(rows < 0, -code, code).astype(jnp.bfloat16), scale


def decode(coded):
    width = coded.shape[1] - EXTRA
    code = coded[:, :width].astype(jnp.float32)
    scale = coded[:, width : width + 1].astype(jnp.float32)
    magnitude = (jnp.log2(jnp.abs(code)) + SPAN / 2) * (scale / SPAN)
    return jnp.where(code < 0, -magnitude, magnitude)


def store_coded(send_refs, blocks, energy):
    width = send_refs[0].shape[1] - EXTRA
    each = send_refs[0].shape[0]
    f32, bf16 = jnp.float32, jnp.bfloat16
    energy = jnp.concatenate([energy, energy], axis=0)
    high = energy.astype(bf16).astype(f32)
    middle = (energy - high).astype(bf16).astype(f32)
    low = energy - high - middle
    lane = lax.broadcasted_iota(jnp.int32, energy.shape, 1)
    terms = jnp.where(lane < 2 * PART, high, jnp.where(lane < 3 * PART, middle, low))
    for pair in range(len(blocks) // 2):
        code, scale = encode(jnp.concatenate(blocks[2 * pair : 2 * pair + 2], axis=0))
        send_ref = send_refs[16 * pair // each]
        target = slice(16 * pair % each, 16 * pair % each + 16)
        send_ref[target, :width] = code
        send_ref[target, width:] = jnp.where(lane < PART, scale, terms).astype(bf16)


def add_came(keep_ref, came_refs):
    arrays, height, width = keep_ref.shape
    width -= EXTRA
    per = height // 8
    sums = [keep_ref[index // per, 8 * (index % per) : 8 * (index % per) + 8, :width] for index in range(arrays * per)]
    energy = keep_ref[0, :8, width:]
    for parts in came_refs:
        index = 0
        for part in parts:
            for row in range(0, part.shape[0], 16):
                both = decode(part[row : row + 16, :])
                sums[index] += both[:8]
                sums[index + 1] += both[8:]
                index += 2
        terms = parts[0][:16, width:].astype(jnp.float32)[:8]
        for term in range(1, 4):
            energy += terms[:, term * PART : term * PART + 1]
    return [sums[array * per : (array + 1) * per] for array in range(arrays)], energy


def limit(mib):
    return pltpu.CompilerParams(vmem_limit_bytes=mib * MIB)


def cost(microseconds):
    return pl.CostEstimate(flops=int(microseconds * 1.1e9), bytes_accessed=0, transcendentals=0)


WHOLE = pl.BlockSpec(memory_space=pltpu.VMEM)
SCALAR = pl.BlockSpec(memory_space=pltpu.SMEM)
ANYWHERE = pl.BlockSpec(memory_space=pl.ANY)
HELD = pl.BlockSpec(memory_space=pltpu.HBM)
HELD = pl.BlockSpec(memory_space=pltpu.HBM)


def cut_kernel(inverse_ref, kinetic_ref, *out_refs):
    count = inverse_ref.shape[0]
    for array, ref in enumerate((inverse_ref, kinetic_ref)):
        for dest in range(0, count, 2):
            pair = [ref[dest + other].astype(jnp.float32) for other in range(2)]
            for index, out_ref in enumerate(out_refs):
                rows = jnp.concatenate([block[8 * index : 8 * index + 8] for block in pair], axis=0)
                out_ref[array, 8 * dest : 8 * dest + 16, :] = rows.astype(jnp.bfloat16)


def cut(inverse, kinetic, group):
    count, _, depth = inverse.shape
    block = pl.BlockSpec((count, 16, depth), lambda step: (0, group, 0))
    out = jax.ShapeDtypeStruct((2, 8 * count, depth), jnp.bfloat16)
    return pl.pallas_call(
        cut_kernel,
        out_shape=(out, out),
        grid=(1,),
        in_specs=[block, block],
        out_specs=(pl.BlockSpec(out.shape, lambda step: (0, 0, 0)),) * 2,
        compiler_params=limit(12),
        cost_estimate=cost(0.1),
        name="cut",
    )(inverse, kinetic)


def near_kernel(chunk, tile, virt_ref, energy_ref, inverse_ref, kinetic_ref, values_ref, laps_ref, out_ref, far_values, far_laps, near_values, near_laps, own_inverse, own_kinetic, sems):
    count, per, depth = inverse_ref.shape
    height = count * per
    width = out_ref.shape[3]
    f32 = jnp.float32
    own = pl.ds(pl.multiple_of(virt_ref[0] * depth, depth), depth)
    other = pl.ds(pl.multiple_of((1 - virt_ref[0]) * depth, depth), depth)
    chunks = width // chunk

    copies = []
    for index in range(chunks):
        columns = pl.ds(index * chunk, chunk)
        copies.append([
            pltpu.make_async_copy(table.at[own, columns], held.at[:, columns], sems.at[index, which])
            for which, (table, held) in enumerate(((values_ref, near_values), (laps_ref, near_laps)))
        ])
    last = [
        pltpu.make_async_copy(table.at[other, :], held, sems.at[chunks, which])
        for which, (table, held) in enumerate(((values_ref, far_values), (laps_ref, far_laps)))
    ]
    first = [
        pltpu.make_async_copy(rows, held, sems.at[chunks + 1, which])
        for which, (rows, held) in enumerate(((inverse_ref, own_inverse), (kinetic_ref, own_kinetic)))
    ]
    for copy in first + sum(copies, []) + last:
        copy.start()
    for copy in first:
        copy.wait()
    inverse = own_inverse[...].reshape(height, depth)
    kinetic = own_kinetic[...].reshape(height, depth)
    for index in range(chunks):
        for copy in copies[index]:
            copy.wait()

        @pl.loop(index * chunk // tile, (index + 1) * chunk // tile)
        def _(step):
            columns = pl.ds(pl.multiple_of(step * tile, tile), tile)
            values, laps = near_values[:, columns], near_laps[:, columns]
            out_ref[1, :, :, columns] = jnp.dot(inverse, values, preferred_element_type=f32).reshape(count, per, tile)
            rest = jnp.dot(kinetic, values, preferred_element_type=f32)
            rest -= jnp.dot(inverse, laps, preferred_element_type=f32)
            out_ref[0, :, :, columns] = (0.5 * rest).reshape(count, per, tile)

    for copy in last:
        copy.wait()


def near_product(virt, energy, inverse, kinetic, values, laplacians):
    count, per, depth = inverse.shape
    width = values.shape[1]
    chunk, tile = 512, 256
    table = pltpu.VMEM((depth, width), jnp.bfloat16)
    own = pltpu.VMEM((count, per, depth), jnp.bfloat16)
    return pl.pallas_call(
        functools.partial(near_kernel, chunk, tile),
        out_shape=(jax.ShapeDtypeStruct((2, count, per, width), jnp.float32), table, table),
        in_specs=[SCALAR, SCALAR, HELD, HELD, HELD, HELD],
        out_specs=(WHOLE, WHOLE, WHOLE),
        scratch_shapes=[table, table, own, own, pltpu.SemaphoreType.DMA((width // chunk + 2, 2))],
        compiler_params=limit(24),
        cost_estimate=cost(9),
        name="near_product",
    )(virt, energy, inverse, kinetic, values, laplacians)


def far_kernel(weights, count, tile, first, virt_ref, me_ref, energy_ref, far_ref, near_ref, values_ref, laps_ref, *rest):
    send_refs, (keep_ref, place_ref) = rest[-SPLIT - 2 : -2], rest[-2:]
    _, height, depth = far_ref.shape
    width = near_ref.shape[3]
    rows = height // count
    half = height // 2
    f32 = jnp.float32
    scale = 2.0 * (energy_ref[0] - OFFSET)

    @pl.loop(0, width // tile)
    def _(index):
        columns = pl.ds(pl.multiple_of(index * tile, tile), tile)
        near = near_ref[:, :, first : first + rows, columns].reshape(2, height, tile)
        both = jnp.dot(far_ref[...].reshape(2 * height, depth), values_ref[:, columns], preferred_element_type=f32)
        laps = jnp.dot(far_ref[0], laps_ref[:, columns], preferred_element_type=f32)
        log = both[:height] + near[1]
        weighted = scale * log + (0.5 * (both[height:] - laps) + near[0])
        for dest in range(count):
            difference = dest ^ me_ref[0]
            place = 0
            for bit, weight in enumerate(weights):
                place = place ^ (((difference >> bit) & 1) * weight)
            target = pl.ds(pl.multiple_of(place * rows, rows), rows)
            source = slice(dest * rows, (dest + 1) * rows)
            place_ref[0, target, columns] = weighted[source]
            place_ref[1, target, columns] = log[source]

    energy = jnp.full((8, EXTRA), energy_ref[0], f32)
    keep_ref[:, :, :width] = place_ref[:, :half]
    keep_ref[0, :8, width:] = energy
    blocks = [place_ref[array, row : row + 8, :] for array in range(2) for row in range(half, height, 8)]
    store_coded(send_refs, blocks, energy)


def far_product(virt, me, energy, theirs, near, first, values, laplacians, tile, stages, after):
    _, height, depth = theirs.shape
    width = values.shape[1]
    half = height // 2
    count = 1 << sum(len(stage) for stage in stages)
    *sends, keep = pl.pallas_call(
        functools.partial(far_kernel, place_weights(stages), count, tile, first),
        out_shape=(jax.ShapeDtypeStruct((2 * half // SPLIT, width + EXTRA), jnp.bfloat16),) * SPLIT
        + (jax.ShapeDtypeStruct((2, half, width + EXTRA), jnp.float32),),
        in_specs=[SCALAR, SCALAR, SCALAR, WHOLE, WHOLE, WHOLE, WHOLE] + [ANYWHERE] * len(after),
        out_specs=(WHOLE,) * (SPLIT + 1),
        scratch_shapes=[pltpu.VMEM((2, height, width), jnp.float32)],
        compiler_params=limit(24),
        cost_estimate=cost(0.1),
        name="far_product",
    )(virt, me, energy, theirs, near, values, laplacians, *after)
    return [sends], keep


def combine_kernel(parts, senders, carried, ordered, *refs):
    keep_ref, refs = refs[0], refs[1:]
    came_refs = [refs[parts * sender : parts * sender + parts] for sender in range(senders)]
    refs = refs[parts * senders + ordered :]
    kept_ref, send_refs = refs[carried], refs[carried + 1 :]
    width = keep_ref.shape[2] - EXTRA
    sums, energy = add_came(keep_ref, came_refs)
    kept = kept_ref.shape[1] // 8
    for array, blocks in enumerate(sums):
        for index, block in enumerate(blocks[:kept]):
            kept_ref[array, 8 * index : 8 * index + 8, :width] = block
    kept_ref[0, :8, width:] = energy
    for index, send_ref in enumerate(send_refs):
        if carried:
            above = refs[0].shape[0]
            send_ref[:above, :] = refs[0][...]
            send_ref = send_ref.at[above:, :]
        first = kept * (index + 1)
        store_coded([send_ref], [block for blocks in sums for block in blocks[first : first + kept]], energy)


def combine(keep, came, sent, carry, after):
    _, height, width = keep.shape
    kept = height // (sent + 1)
    parts, senders = len(came[0]), len(came)
    above = sum(array.shape[0] for array in carry)
    keep, *sends = pl.pallas_call(
        functools.partial(combine_kernel, parts, senders, len(carry), len(after)),
        out_shape=(jax.ShapeDtypeStruct((2, kept, width), jnp.float32),)
        + (jax.ShapeDtypeStruct((above + 2 * kept, width), jnp.bfloat16),) * sent,
        in_specs=[WHOLE] * (1 + parts * senders) + [ANYWHERE] * len(after) + [WHOLE] * len(carry),
        out_specs=(WHOLE,) * (1 + sent),
        compiler_params=limit(8),
        cost_estimate=cost(0.1),
        name="combine",
    )(keep, *[part for parts in came for part in parts], *after, *carry)
    return [[send] for send in sends], keep


def finish_kernel(count, joint, *refs):
    (gradient_ref, log_ref), refs = refs[-2:], refs[:-2]
    groups = len(refs) // (joint + 1)
    keep_refs, came_refs = refs[: joint * groups], refs[joint * groups :]
    row = 0
    for piece, keep_ref in enumerate(keep_refs):
        place = 16 * (piece % joint)
        came = came_refs[piece // joint].at[place : place + 16, :]
        (gradient, log), energy = add_came(keep_ref, [[came]])
        correction = 2.0 * (energy[:, :1] / count - OFFSET)
        for block in range(len(log)):
            log_mean = log[block] / count
            gradient_ref[row : row + 8, :] = gradient[block] / count - correction * log_mean
            log_ref[row : row + 8, :] = log_mean
            row += 8


def finish(keeps, came, count):
    _, rows, width = keeps[0].shape
    out = jax.ShapeDtypeStruct((rows * len(keeps), width - EXTRA), jnp.float32)
    return pl.pallas_call(
        functools.partial(finish_kernel, count, JOINT),
        out_shape=(out, out),
        in_specs=[WHOLE] * (len(keeps) + len(came)),
        out_specs=(WHOLE, WHOLE),
        compiler_params=limit(8),
        cost_estimate=cost(0.1),
        name="finish",
    )(*keeps, *came)


def pieced_body(pieces, tile, inverse_rows, kinetic_rows, virt_values, virt_laplacians, local_energy):
    count = lax.axis_size("walk")
    stages = stage_masks(count)
    me = lax.axis_index("walk").astype(jnp.int32).reshape(1)
    virt = lax.axis_index("virt").astype(jnp.int32).reshape(1)
    occupied, depth = inverse_rows.shape[1:]
    by_dest = (count, occupied // count, depth)
    inverse, kinetic = inverse_rows.reshape(by_dest), kinetic_rows.reshape(by_dest)
    rows = occupied // (count * pieces)

    inverse, kinetic, values, laplacians = (
        pltpu.with_memory_space_constraint(array, pltpu.HBM)
        for array in (inverse, kinetic, virt_values[0], virt_laplacians[0])
    )
    theirs = []
    for group in range(pieces // 2):
        theirs += [swap(mine, "virt", 1) for mine in cut(inverse, kinetic, group)]
    near, values, laplacians = near_product(virt, local_energy, inverse, kinetic, values, laplacians)

    keep, first, came = {}, {}, []
    late, carry = [], ()
    for turn in range(pieces + 1):
        if turn < pieces:
            after = [keep[turn - 1]] if turn else []
            send, kept = far_product(
                virt, me, local_energy, theirs[turn], near, turn * rows, values, laplacians, tile, stages, after
            )
            first[turn] = [[swap(part, "walk", mask) for part in parts] for parts, mask in zip(send, partners(stages[0]))]
        if turn:
            piece = turn - 1
            sends, keep[piece] = combine(keep[piece], second, len(partners(stages[2])), carry, [])
            carry = tuple(sends[0])
            if turn % JOINT == 0:
                came.append(swap(carry[0], "walk", stages[2][0]))
                carry = ()
        if turn < pieces:
            after = ([keep[turn - 1]] if turn else [])
            sends, keep[turn] = combine(kept, first[turn], len(partners(stages[1])), (), after)
            second = [[swap(part, "walk", mask) for part in parts] for parts, mask in zip(sends, partners(stages[1]))]
    return finish([keep[piece] for piece in range(pieces)], came, count)


def solution(mesh):
    placed = (
        P("walk", None, "virt"),
        P("walk", None, "virt"),
        P("walk", None, "virt"),
        P("walk", None, "virt"),
        P("walk"),
    )

    def body(inverse_rows, kinetic_rows, virt_values, virt_laplacians, local_energy):
        count = mesh.shape["walk"]
        walkers, occupied, depth = inverse_rows.shape
        width = virt_values.shape[2]
        tile = 512
        fits = (
            walkers == 1
            and mesh.shape["virt"] == 2
            and count == 16
            and count >= 4
            and occupied == count * PIECES * 8
            and depth % 256 == 0
            and width % tile == 0
        )
        form = functools.partial(pieced_body, PIECES, tile) if fits else general_body
        return form(inverse_rows, kinetic_rows, virt_values, virt_laplacians, local_energy)

    return jax.shard_map(
        body,
        mesh=mesh,
        in_specs=placed,
        out_specs=(P("walk", "virt"), P("walk", "virt")),
        check_vma=False,
    )
```

```python
import functools

import jax
import jax.numpy as jnp
from jax import lax
from jax.experimental import pallas as pl
from jax.experimental.pallas import tpu as pltpu
from jax.sharding import PartitionSpec as P

PIECES = 4
SPLIT = 4
JOINT = 2


def product(left, right):
    return jnp.einsum("woe,wev->wov", left, right, preferred_element_type=jnp.float32)


def gradient_terms(log_grad, kin_part, weights):
    kin_grad = -0.5 * kin_part
    weighted = jnp.sum(weights[:, None, None] * log_grad + kin_grad, axis=0)
    return (weighted, jnp.sum(log_grad, axis=0))


def general_body(inverse_rows, kinetic_rows, virt_values, virt_laplacians, local_energy):
    walk_count = lax.axis_size("walk")
    walker_count = walk_count * local_energy.shape[0]
    energy_sum = lax.psum(jnp.sum(local_energy), "walk")
    average = energy_sum / walker_count
    weights = 2.0 * (local_energy - average)
    inverse_all, kinetic_all = (
        lax.all_gather(inverse_rows, "virt", axis=2, tiled=True),
        lax.all_gather(kinetic_rows, "virt", axis=2, tiled=True),
    )
    log_grad = product(inverse_all, virt_values)
    kin_part = product(inverse_all, virt_laplacians) - product(kinetic_all, virt_values)
    weighted, log_sum = gradient_terms(log_grad, kin_part, weights)
    summed = (
        lax.psum_scatter(weighted, "walk", scatter_dimension=0, tiled=True),
        lax.psum_scatter(log_sum, "walk", scatter_dimension=0, tiled=True),
    )
    gradient_part, log_part = (summed[0], summed[1])
    return (gradient_part / walker_count, log_part / walker_count)


SPAN = 248.0
EXTRA = 128
PART = EXTRA // 4
OFFSET = 3.1
TINY = 1e-30
MIB = 1024 * 1024


def stage_masks(count):
    bits = [1 << bit for bit in range(count.bit_length() - 1)]
    if len(bits) < 3:
        return [[bit] for bit in bits]
    return [bits[:1], bits[1:3]] + [[bit] for bit in bits[3:]]


def place_weights(stages):
    order = [mask for stage in stages for mask in stage]
    weights = [0] * len(order)
    for index, mask in enumerate(order):
        weights[mask.bit_length() - 1] = 1 << (len(order) - 1 - index)
    return weights


def partners(stage):
    if len(stage) == 1:
        return list(stage)
    first, second = stage
    return [second, first, first ^ second]


def swap(array, axis, mask):
    pairs = [(source, source ^ mask) for source in range(lax.axis_size(axis))]
    return lax.ppermute(array, axis, pairs)


def encode(rows):
    magnitude = jnp.abs(rows)
    largest = jnp.maximum(jnp.max(magnitude, axis=-1, keepdims=True), TINY)
    scale = (largest * (1.0 + 2.0**-7)).astype(jnp.bfloat16).astype(jnp.float32)
    code = jnp.exp2(magnitude * (SPAN / scale) - SPAN / 2)
    return jnp.where(rows < 0, -code, code).astype(jnp.bfloat16), scale


def decode(coded):
    width = coded.shape[1] - EXTRA
    code = coded[:, :width].astype(jnp.float32)
    scale = coded[:, width : width + 1].astype(jnp.float32)
    magnitude = (jnp.log2(jnp.abs(code)) + SPAN / 2) * (scale / SPAN)
    return jnp.where(code < 0, -magnitude, magnitude)


def store_coded(send_refs, blocks, energy):
    width = send_refs[0].shape[1] - EXTRA
    each = send_refs[0].shape[0]
    f32, bf16 = jnp.float32, jnp.bfloat16
    energy = jnp.concatenate([energy, energy], axis=0)
    high = energy.astype(bf16).astype(f32)
    middle = (energy - high).astype(bf16).astype(f32)
    low = energy - high - middle
    lane = lax.broadcasted_iota(jnp.int32, energy.shape, 1)
    terms = jnp.where(lane < 2 * PART, high, jnp.where(lane < 3 * PART, middle, low))
    for pair in range(len(blocks) // 2):
        code, scale = encode(jnp.concatenate(blocks[2 * pair : 2 * pair + 2], axis=0))
        send_ref = send_refs[16 * pair // each]
        target = slice(16 * pair % each, 16 * pair % each + 16)
        send_ref[target, :width] = code
        send_ref[target, width:] = jnp.where(lane < PART, scale, terms).astype(bf16)


def add_came(keep_ref, came_refs):
    arrays, height, width = keep_ref.shape
    width -= EXTRA
    per = height // 8
    sums = [keep_ref[index // per, 8 * (index % per) : 8 * (index % per) + 8, :width] for index in range(arrays * per)]
    energy = keep_ref[0, :8, width:]
    for parts in came_refs:
        index = 0
        for part in parts:
            for row in range(0, part.shape[0], 16):
                both = decode(part[row : row + 16, :])
                sums[index] += both[:8]
                sums[index + 1] += both[8:]
                index += 2
        terms = parts[0][:16, width:].astype(jnp.float32)[:8]
        for term in range(1, 4):
            energy += terms[:, term * PART : term * PART + 1]
    return [sums[array * per : (array + 1) * per] for array in range(arrays)], energy


def limit(mib):
    return pltpu.CompilerParams(vmem_limit_bytes=mib * MIB)


def cost(microseconds):
    return pl.CostEstimate(flops=int(microseconds * 1.1e9), bytes_accessed=0, transcendentals=0)


WHOLE = pl.BlockSpec(memory_space=pltpu.VMEM)
SCALAR = pl.BlockSpec(memory_space=pltpu.SMEM)
ANYWHERE = pl.BlockSpec(memory_space=pl.ANY)
HELD = pl.BlockSpec(memory_space=pltpu.HBM)
HELD = pl.BlockSpec(memory_space=pltpu.HBM)


def cut_kernel(inverse_ref, kinetic_ref, *out_refs):
    count = inverse_ref.shape[0]
    for array, ref in enumerate((inverse_ref, kinetic_ref)):
        for dest in range(0, count, 2):
            pair = [ref[dest + other].astype(jnp.float32) for other in range(2)]
            for index, out_ref in enumerate(out_refs):
                rows = jnp.concatenate([block[8 * index : 8 * index + 8] for block in pair], axis=0)
                out_ref[array, 8 * dest : 8 * dest + 16, :] = rows.astype(jnp.bfloat16)


def cut(inverse, kinetic, group):
    count, _, depth = inverse.shape
    block = pl.BlockSpec((count, 16, depth), lambda step: (0, group, 0))
    out = jax.ShapeDtypeStruct((2, 8 * count, depth), jnp.bfloat16)
    return pl.pallas_call(
        cut_kernel,
        out_shape=(out, out),
        grid=(1,),
        in_specs=[block, block],
        out_specs=(pl.BlockSpec(out.shape, lambda step: (0, 0, 0)),) * 2,
        compiler_params=limit(12),
        cost_estimate=cost(0.1),
        name="cut",
    )(inverse, kinetic)


def near_kernel(chunk, tile, virt_ref, me_ref, energy_ref, inverse_ref, kinetic_ref, values_ref, laps_ref, out_ref, far_values, far_laps, near_values, near_laps, own_inverse, own_kinetic, sems):
    count, per, depth = inverse_ref.shape
    height = count * per
    width = out_ref.shape[3]
    f32 = jnp.float32
    own = pl.ds(pl.multiple_of(virt_ref[0] * depth, depth), depth)
    other = pl.ds(pl.multiple_of((1 - virt_ref[0]) * depth, depth), depth)
    chunks = width // chunk

    copies = []
    for index in range(chunks):
        columns = pl.ds(index * chunk, chunk)
        copies.append([
            pltpu.make_async_copy(table.at[own, columns], held.at[:, columns], sems.at[index, which])
            for which, (table, held) in enumerate(((values_ref, near_values), (laps_ref, near_laps)))
        ])
    last = [
        pltpu.make_async_copy(table.at[other, :], held, sems.at[chunks, which])
        for which, (table, held) in enumerate(((values_ref, far_values), (laps_ref, far_laps)))
    ]
    first = [
        pltpu.make_async_copy(rows, held, sems.at[chunks + 1, which])
        for which, (rows, held) in enumerate(((inverse_ref, own_inverse), (kinetic_ref, own_kinetic)))
    ]
    for copy in first + sum(copies, []) + last:
        copy.start()
    for copy in first:
        copy.wait()
    inverse = own_inverse[...].reshape(height, depth)
    kinetic = own_kinetic[...].reshape(height, depth)
    for index in range(chunks):
        for copy in copies[index]:
            copy.wait()

        @pl.loop(index * chunk // tile, (index + 1) * chunk // tile)
        def _(step):
            columns = pl.ds(pl.multiple_of(step * tile, tile), tile)
            values, laps = near_values[:, columns], near_laps[:, columns]
            out_ref[1, :, :, columns] = jnp.dot(inverse, values, preferred_element_type=f32).reshape(count, per, tile)
            rest = jnp.dot(kinetic, values, preferred_element_type=f32)
            rest -= jnp.dot(inverse, laps, preferred_element_type=f32)
            out_ref[0, :, :, columns] = (0.5 * rest).reshape(count, per, tile)

    for copy in last:
        copy.wait()


def near_product(virt, me, energy, inverse, kinetic, values, laplacians):
    count, per, depth = inverse.shape
    width = values.shape[1]
    chunk, tile = 512, 256
    table = pltpu.VMEM((depth, width), jnp.bfloat16)
    own = pltpu.VMEM((count, per, depth), jnp.bfloat16)
    return pl.pallas_call(
        functools.partial(near_kernel, chunk, tile),
        out_shape=(jax.ShapeDtypeStruct((2, count, per, width), jnp.float32), table, table),
        in_specs=[SCALAR, SCALAR, SCALAR, HELD, HELD, HELD, HELD],
        out_specs=(WHOLE, WHOLE, WHOLE),
        scratch_shapes=[table, table, own, own, pltpu.SemaphoreType.DMA((width // chunk + 2, 2))],
        compiler_params=limit(24),
        cost_estimate=cost(9),
        name="near_product",
    )(virt, me, energy, inverse, kinetic, values, laplacians)


def far_kernel(weights, count, tile, first, virt_ref, me_ref, energy_ref, far_ref, near_ref, values_ref, laps_ref, *rest):
    send_refs, (keep_ref, place_ref) = rest[-SPLIT - 2 : -2], rest[-2:]
    _, height, depth = far_ref.shape
    width = near_ref.shape[3]
    rows = height // count
    half = height // 2
    f32 = jnp.float32
    scale = 2.0 * (energy_ref[0] - OFFSET)

    @pl.loop(0, width // tile)
    def _(index):
        columns = pl.ds(pl.multiple_of(index * tile, tile), tile)
        near = near_ref[:, :, first : first + rows, columns].reshape(2, height, tile)
        both = jnp.dot(far_ref[...].reshape(2 * height, depth), values_ref[:, columns], preferred_element_type=f32)
        laps = jnp.dot(far_ref[0], laps_ref[:, columns], preferred_element_type=f32)
        log = both[:height] + near[1]
        weighted = scale * log + (0.5 * (both[height:] - laps) + near[0])
        for dest in range(count):
            difference = dest ^ me_ref[0]
            place = 0
            for bit, weight in enumerate(weights):
                place = place ^ (((difference >> bit) & 1) * weight)
            target = pl.ds(pl.multiple_of(place * rows, rows), rows)
            source = slice(dest * rows, (dest + 1) * rows)
            place_ref[0, target, columns] = weighted[source]
            place_ref[1, target, columns] = log[source]

    energy = jnp.full((8, EXTRA), energy_ref[0], f32)
    keep_ref[:, :, :width] = place_ref[:, :half]
    keep_ref[0, :8, width:] = energy
    blocks = [place_ref[array, row : row + 8, :] for array in range(2) for row in range(half, height, 8)]
    store_coded(send_refs, blocks, energy)


def far_product(virt, me, energy, theirs, near, first, values, laplacians, tile, stages, after):
    _, height, depth = theirs.shape
    width = values.shape[1]
    half = height // 2
    count = 1 << sum(len(stage) for stage in stages)
    *sends, keep = pl.pallas_call(
        functools.partial(far_kernel, place_weights(stages), count, tile, first),
        out_shape=(jax.ShapeDtypeStruct((2 * half // SPLIT, width + EXTRA), jnp.bfloat16),) * SPLIT
        + (jax.ShapeDtypeStruct((2, half, width + EXTRA), jnp.float32),),
        in_specs=[SCALAR, SCALAR, SCALAR, WHOLE, WHOLE, WHOLE, WHOLE] + [ANYWHERE] * len(after),
        out_specs=(WHOLE,) * (SPLIT + 1),
        scratch_shapes=[pltpu.VMEM((2, height, width), jnp.float32)],
        compiler_params=limit(24),
        cost_estimate=cost(0.1),
        name="far_product",
    )(virt, me, energy, theirs, near, values, laplacians, *after)
    return [sends], keep


def combine_kernel(parts, senders, carried, ordered, *refs):
    keep_ref, refs = refs[0], refs[1:]
    came_refs = [refs[parts * sender : parts * sender + parts] for sender in range(senders)]
    refs = refs[parts * senders + ordered :]
    kept_ref, send_refs = refs[carried], refs[carried + 1 :]
    width = keep_ref.shape[2] - EXTRA
    sums, energy = add_came(keep_ref, came_refs)
    kept = kept_ref.shape[1] // 8
    for array, blocks in enumerate(sums):
        for index, block in enumerate(blocks[:kept]):
            kept_ref[array, 8 * index : 8 * index + 8, :width] = block
    kept_ref[0, :8, width:] = energy
    for index, send_ref in enumerate(send_refs):
        if carried:
            above = refs[0].shape[0]
            send_ref[:above, :] = refs[0][...]
            send_ref = send_ref.at[above:, :]
        first = kept * (index + 1)
        store_coded([send_ref], [block for blocks in sums for block in blocks[first : first + kept]], energy)


def combine(keep, came, sent, carry, after):
    _, height, width = keep.shape
    kept = height // (sent + 1)
    parts, senders = len(came[0]), len(came)
    above = sum(array.shape[0] for array in carry)
    keep, *sends = pl.pallas_call(
        functools.partial(combine_kernel, parts, senders, len(carry), len(after)),
        out_shape=(jax.ShapeDtypeStruct((2, kept, width), jnp.float32),)
        + (jax.ShapeDtypeStruct((above + 2 * kept, width), jnp.bfloat16),) * sent,
        in_specs=[WHOLE] * (1 + parts * senders) + [ANYWHERE] * len(after) + [WHOLE] * len(carry),
        out_specs=(WHOLE,) * (1 + sent),
        compiler_params=limit(8),
        cost_estimate=cost(0.1),
        name="combine",
    )(keep, *[part for parts in came for part in parts], *after, *carry)
    return [[send] for send in sends], keep


def finish_kernel(count, joint, *refs):
    (gradient_ref, log_ref), refs = refs[-2:], refs[:-2]
    groups = len(refs) // (joint + 1)
    keep_refs, came_refs = refs[: joint * groups], refs[joint * groups :]
    row = 0
    for piece, keep_ref in enumerate(keep_refs):
        place = 16 * (piece % joint)
        came = came_refs[piece // joint].at[place : place + 16, :]
        (gradient, log), energy = add_came(keep_ref, [[came]])
        correction = 2.0 * (energy[:, :1] / count - OFFSET)
        for block in range(len(log)):
            log_mean = log[block] / count
            gradient_ref[row : row + 8, :] = gradient[block] / count - correction * log_mean
            log_ref[row : row + 8, :] = log_mean
            row += 8


def finish(keeps, came, count):
    _, rows, width = keeps[0].shape
    out = jax.ShapeDtypeStruct((rows * len(keeps), width - EXTRA), jnp.float32)
    return pl.pallas_call(
        functools.partial(finish_kernel, count, JOINT),
        out_shape=(out, out),
        in_specs=[WHOLE] * (len(keeps) + len(came)),
        out_specs=(WHOLE, WHOLE),
        compiler_params=limit(8),
        cost_estimate=cost(0.1),
        name="finish",
    )(*keeps, *came)


def pieced_body(pieces, tile, inverse_rows, kinetic_rows, virt_values, virt_laplacians, local_energy):
    count = lax.axis_size("walk")
    stages = stage_masks(count)
    me = lax.axis_index("walk").astype(jnp.int32).reshape(1)
    virt = lax.axis_index("virt").astype(jnp.int32).reshape(1)
    occupied, depth = inverse_rows.shape[1:]
    by_dest = (count, occupied // count, depth)
    inverse, kinetic = inverse_rows.reshape(by_dest), kinetic_rows.reshape(by_dest)
    rows = occupied // (count * pieces)

    inverse, kinetic, values, laplacians = (
        pltpu.with_memory_space_constraint(array, pltpu.HBM)
        for array in (inverse, kinetic, virt_values[0], virt_laplacians[0])
    )
    theirs = []
    for group in range(pieces // 2):
        theirs += [swap(mine, "virt", 1) for mine in cut(inverse, kinetic, group)]
    near, values, laplacians = near_product(virt, me, local_energy, inverse, kinetic, values, laplacians)

    keep, first, came = {}, {}, []
    late, carry = [], ()
    for turn in range(pieces + 1):
        if turn < pieces:
            after = [keep[turn - 1]] if turn else []
            send, kept = far_product(
                virt, me, local_energy, theirs[turn], near, turn * rows, values, laplacians, tile, stages, after
            )
            first[turn] = [[swap(part, "walk", mask) for part in parts] for parts, mask in zip(send, partners(stages[0]))]
        if turn:
            piece = turn - 1
            sends, keep[piece] = combine(keep[piece], second, len(partners(stages[2])), carry, [])
            carry = tuple(sends[0])
            if turn % JOINT == 0:
                came.append(swap(carry[0], "walk", stages[2][0]))
                carry = ()
        if turn < pieces:
            after = ([keep[turn - 1]] if turn else [])
            sends, keep[turn] = combine(kept, first[turn], len(partners(stages[1])), (), after)
            second = [[swap(part, "walk", mask) for part in parts] for parts, mask in zip(sends, partners(stages[1]))]
    return finish([keep[piece] for piece in range(pieces)], came, count)


def solution(mesh):
    placed = (
        P("walk", None, "virt"),
        P("walk", None, "virt"),
        P("walk", None, "virt"),
        P("walk", None, "virt"),
        P("walk"),
    )

    def body(inverse_rows, kinetic_rows, virt_values, virt_laplacians, local_energy):
        count = mesh.shape["walk"]
        walkers, occupied, depth = inverse_rows.shape
        width = virt_values.shape[2]
        tile = 512
        fits = (
            walkers == 1
            and mesh.shape["virt"] == 2
            and count == 16
            and count >= 4
            and occupied == count * PIECES * 8
            and depth % 256 == 0
            and width % tile == 0
        )
        form = functools.partial(pieced_body, PIECES, tile) if fits else general_body
        return form(inverse_rows, kinetic_rows, virt_values, virt_laplacians, local_energy)

    return jax.shard_map(
        body,
        mesh=mesh,
        in_specs=placed,
        out_specs=(P("walk", "virt"), P("walk", "virt")),
        check_vma=False,
    )
```

```python
import functools

import jax
import jax.numpy as jnp
from jax import lax
from jax.experimental import pallas as pl
from jax.experimental.pallas import tpu as pltpu
from jax.sharding import PartitionSpec as P

PIECES = 4
GROUPS = ((0, 1, 2), (3,))
BESIDE = 6


def product(left, right):
    return jnp.einsum("woe,wev->wov", left, right, preferred_element_type=jnp.float32)


def gradient_terms(log_grad, kin_part, weights):
    kin_grad = -0.5 * kin_part
    weighted = jnp.sum(weights[:, None, None] * log_grad + kin_grad, axis=0)
    return (weighted, jnp.sum(log_grad, axis=0))


def general_body(inverse_rows, kinetic_rows, virt_values, virt_laplacians, local_energy):
    walk_count = lax.axis_size("walk")
    walker_count = walk_count * local_energy.shape[0]
    energy_sum = lax.psum(jnp.sum(local_energy), "walk")
    average = energy_sum / walker_count
    weights = 2.0 * (local_energy - average)
    inverse_all, kinetic_all = (
        lax.all_gather(inverse_rows, "virt", axis=2, tiled=True),
        lax.all_gather(kinetic_rows, "virt", axis=2, tiled=True),
    )
    log_grad = product(inverse_all, virt_values)
    kin_part = product(inverse_all, virt_laplacians) - product(kinetic_all, virt_values)
    weighted, log_sum = gradient_terms(log_grad, kin_part, weights)
    summed = (
        lax.psum_scatter(weighted, "walk", scatter_dimension=0, tiled=True),
        lax.psum_scatter(log_sum, "walk", scatter_dimension=0, tiled=True),
    )
    gradient_part, log_part = (summed[0], summed[1])
    return (gradient_part / walker_count, log_part / walker_count)


SPAN = 248.0
EXTRA = 128
PART = EXTRA // 4
OFFSET = 3.1
TINY = 1e-30
MIB = 1024 * 1024


def stage_masks(count):
    bits = [1 << bit for bit in range(count.bit_length() - 1)]
    if len(bits) < 3:
        return [[bit] for bit in bits]
    return [bits[:1], bits[1:3]] + [[bit] for bit in bits[3:]]


def place_weights(stages):
    order = [mask for stage in stages for mask in stage]
    weights = [0] * len(order)
    for index, mask in enumerate(order):
        weights[mask.bit_length() - 1] = 1 << (len(order) - 1 - index)
    return weights


def partners(stage):
    if len(stage) == 1:
        return list(stage)
    first, second = stage
    return [second, first, first ^ second]


def swap(array, axis, mask):
    pairs = [(source, source ^ mask) for source in range(lax.axis_size(axis))]
    return lax.ppermute(array, axis, pairs)


def encode(rows):
    magnitude = jnp.abs(rows)
    largest = jnp.maximum(jnp.max(magnitude, axis=-1, keepdims=True), TINY)
    scale = (largest * (1.0 + 2.0**-7)).astype(jnp.bfloat16).astype(jnp.float32)
    code = jnp.exp2(magnitude * (SPAN / scale) - SPAN / 2)
    return jnp.where(rows < 0, -code, code).astype(jnp.bfloat16), scale


def decode(coded):
    width = coded.shape[1] - EXTRA
    code = coded[:, :width].astype(jnp.float32)
    scale = coded[:, width : width + 1].astype(jnp.float32)
    magnitude = (jnp.log2(jnp.abs(code)) + SPAN / 2) * (scale / SPAN)
    return jnp.where(code < 0, -magnitude, magnitude)


def store_coded(send_refs, blocks, energy):
    width = send_refs[0].shape[1] - EXTRA
    each = send_refs[0].shape[0]
    f32, bf16 = jnp.float32, jnp.bfloat16
    energy = jnp.concatenate([energy, energy], axis=0)
    high = energy.astype(bf16).astype(f32)
    middle = (energy - high).astype(bf16).astype(f32)
    low = energy - high - middle
    lane = lax.broadcasted_iota(jnp.int32, energy.shape, 1)
    terms = jnp.where(lane < 2 * PART, high, jnp.where(lane < 3 * PART, middle, low))
    for pair in range(len(blocks) // 2):
        code, scale = encode(jnp.concatenate(blocks[2 * pair : 2 * pair + 2], axis=0))
        send_ref = send_refs[16 * pair // each]
        target = slice(16 * pair % each, 16 * pair % each + 16)
        send_ref[target, :width] = code
        send_ref[target, width:] = jnp.where(lane < PART, scale, terms).astype(bf16)


def add_came(keep_ref, came_refs):
    arrays, height, width = keep_ref.shape
    width -= EXTRA
    per = height // 8
    sums = [keep_ref[index // per, 8 * (index % per) : 8 * (index % per) + 8, :width] for index in range(arrays * per)]
    energy = keep_ref[0, :8, width:]
    for parts in came_refs:
        index = 0
        for part in parts:
            for row in range(0, part.shape[0], 16):
                both = decode(part[row : row + 16, :])
                sums[index] += both[:8]
                sums[index + 1] += both[8:]
                index += 2
        terms = parts[0][:16, width:].astype(jnp.float32)[:8]
        for term in range(1, 4):
            energy += terms[:, term * PART : term * PART + 1]
    return [sums[array * per : (array + 1) * per] for array in range(arrays)], energy


def limit(mib):
    return pltpu.CompilerParams(vmem_limit_bytes=mib * MIB)


def cost(microseconds):
    return pl.CostEstimate(flops=int(microseconds * 1.1e9), bytes_accessed=0, transcendentals=0)


WHOLE = pl.BlockSpec(memory_space=pltpu.VMEM)
SCALAR = pl.BlockSpec(memory_space=pltpu.SMEM)
ANYWHERE = pl.BlockSpec(memory_space=pl.ANY)
HELD = pl.BlockSpec(memory_space=pltpu.HBM)
HELD = pl.BlockSpec(memory_space=pltpu.HBM)


def cut_kernel(inverse_ref, kinetic_ref, *out_refs):
    count = inverse_ref.shape[0]
    for array, ref in enumerate((inverse_ref, kinetic_ref)):
        for dest in range(0, count, 2):
            pair = [ref[dest + other].astype(jnp.float32) for other in range(2)]
            for index, out_ref in enumerate(out_refs):
                rows = jnp.concatenate([block[8 * index : 8 * index + 8] for block in pair], axis=0)
                out_ref[array, 8 * dest : 8 * dest + 16, :] = rows.astype(jnp.bfloat16)


def cut(inverse, kinetic, group):
    count, _, depth = inverse.shape
    block = pl.BlockSpec((count, 16, depth), lambda step: (0, group, 0))
    out = jax.ShapeDtypeStruct((2, 8 * count, depth), jnp.bfloat16)
    return pl.pallas_call(
        cut_kernel,
        out_shape=(out, out),
        grid=(1,),
        in_specs=[block, block],
        out_specs=(pl.BlockSpec(out.shape, lambda step: (0, 0, 0)),) * 2,
        compiler_params=limit(12),
        cost_estimate=cost(0.1),
        name="cut",
    )(inverse, kinetic)


def near_kernel(chunk, tile, virt_ref, me_ref, energy_ref, inverse_ref, kinetic_ref, values_ref, laps_ref, *rest):
    out_ref, far_values, far_laps, near_values, near_laps, own_inverse, own_kinetic, sems = rest[-8:]
    count, per, depth = inverse_ref.shape
    height = count * per
    width = out_ref.shape[3]
    f32 = jnp.float32
    own = pl.ds(pl.multiple_of(virt_ref[0] * depth, depth), depth)
    other = pl.ds(pl.multiple_of((1 - virt_ref[0]) * depth, depth), depth)
    chunks = width // chunk

    copies = []
    for index in range(chunks):
        columns = pl.ds(index * chunk, chunk)
        copies.append([
            pltpu.make_async_copy(table.at[own, columns], held.at[:, columns], sems.at[index, which])
            for which, (table, held) in enumerate(((values_ref, near_values), (laps_ref, near_laps)))
        ])
    last = [
        pltpu.make_async_copy(table.at[other, :], held, sems.at[chunks, which])
        for which, (table, held) in enumerate(((values_ref, far_values), (laps_ref, far_laps)))
    ]
    first = [
        pltpu.make_async_copy(rows, held, sems.at[chunks + 1, which])
        for which, (rows, held) in enumerate(((inverse_ref, own_inverse), (kinetic_ref, own_kinetic)))
    ]
    for copy in first + sum(copies, []) + last:
        copy.start()
    for copy in first:
        copy.wait()
    inverse = own_inverse[...].reshape(height, depth)
    kinetic = own_kinetic[...].reshape(height, depth)
    for index in range(chunks):
        for copy in copies[index]:
            copy.wait()

        @pl.loop(index * chunk // tile, (index + 1) * chunk // tile)
        def _(step):
            columns = pl.ds(pl.multiple_of(step * tile, tile), tile)
            values, laps = near_values[:, columns], near_laps[:, columns]
            out_ref[1, :, :, columns] = jnp.dot(inverse, values, preferred_element_type=f32).reshape(count, per, tile)
            rest = jnp.dot(kinetic, values, preferred_element_type=f32)
            rest -= jnp.dot(inverse, laps, preferred_element_type=f32)
            out_ref[0, :, :, columns] = (0.5 * rest).reshape(count, per, tile)

    for copy in last:
        copy.wait()


def near_product(virt, me, energy, inverse, kinetic, values, laplacians, after):
    count, per, depth = inverse.shape
    width = values.shape[1]
    chunk, tile = 512, 256
    table = pltpu.VMEM((depth, width), jnp.bfloat16)
    own = pltpu.VMEM((count, per, depth), jnp.bfloat16)
    return pl.pallas_call(
        functools.partial(near_kernel, chunk, tile),
        out_shape=(jax.ShapeDtypeStruct((2, count, per, width), jnp.float32), table, table),
        in_specs=[SCALAR, SCALAR, SCALAR, HELD, HELD, HELD, HELD] + [ANYWHERE] * len(after),
        out_specs=(WHOLE, WHOLE, WHOLE),
        scratch_shapes=[table, table, own, own, pltpu.SemaphoreType.DMA((width // chunk + 2, 2))],
        compiler_params=limit(24),
        cost_estimate=cost(9),
        name="near_product",
    )(virt, me, energy, inverse, kinetic, values, laplacians, *after)


def far_kernel(weights, count, tile, first, split, virt_ref, me_ref, energy_ref, far_ref, near_ref, values_ref, laps_ref, *rest):
    send_refs, (keep_ref, place_ref) = rest[-split - 2 : -2], rest[-2:]
    _, height, depth = far_ref.shape
    width = near_ref.shape[3]
    rows = height // count
    half = height // 2
    f32 = jnp.float32
    scale = 2.0 * (energy_ref[0] - OFFSET)

    @pl.loop(0, width // tile)
    def _(index):
        columns = pl.ds(pl.multiple_of(index * tile, tile), tile)
        near = near_ref[:, :, first : first + rows, columns].reshape(2, height, tile)
        both = jnp.dot(far_ref[...].reshape(2 * height, depth), values_ref[:, columns], preferred_element_type=f32)
        laps = jnp.dot(far_ref[0], laps_ref[:, columns], preferred_element_type=f32)
        log = both[:height] + near[1]
        weighted = scale * log + (0.5 * (both[height:] - laps) + near[0])
        for dest in range(count):
            difference = dest ^ me_ref[0]
            place = 0
            for bit, weight in enumerate(weights):
                place = place ^ (((difference >> bit) & 1) * weight)
            target = pl.ds(pl.multiple_of(place * rows, rows), rows)
            source = slice(dest * rows, (dest + 1) * rows)
            place_ref[0, target, columns] = weighted[source]
            place_ref[1, target, columns] = log[source]

    energy = jnp.full((8, EXTRA), energy_ref[0], f32)
    keep_ref[:, :, :width] = place_ref[:, :half]
    keep_ref[0, :8, width:] = energy
    blocks = [place_ref[array, row : row + 8, :] for array in range(2) for row in range(half, height, 8)]
    store_coded(send_refs, blocks, energy)


def far_product(virt, me, energy, theirs, near, first, values, laplacians, tile, stages, split, after):
    _, height, depth = theirs.shape
    width = values.shape[1]
    half = height // 2
    count = 1 << sum(len(stage) for stage in stages)
    *sends, keep = pl.pallas_call(
        functools.partial(far_kernel, place_weights(stages), count, tile, first, split),
        out_shape=(jax.ShapeDtypeStruct((2 * half // split, width + EXTRA), jnp.bfloat16),) * split
        + (jax.ShapeDtypeStruct((2, half, width + EXTRA), jnp.float32),),
        in_specs=[SCALAR, SCALAR, SCALAR, WHOLE, WHOLE, WHOLE, WHOLE] + [ANYWHERE] * len(after),
        out_specs=(WHOLE,) * (split + 1),
        scratch_shapes=[pltpu.VMEM((2, height, width), jnp.float32)],
        compiler_params=limit(24),
        cost_estimate=cost(0.1),
        name="far_product",
    )(virt, me, energy, theirs, near, values, laplacians, *after)
    return [sends], keep


def combine_kernel(parts, senders, carried, ordered, *refs):
    keep_ref, refs = refs[0], refs[1:]
    came_refs = [refs[parts * sender : parts * sender + parts] for sender in range(senders)]
    refs = refs[parts * senders + ordered :]
    kept_ref, send_refs = refs[carried], refs[carried + 1 :]
    width = keep_ref.shape[2] - EXTRA
    sums, energy = add_came(keep_ref, came_refs)
    kept = kept_ref.shape[1] // 8
    for array, blocks in enumerate(sums):
        for index, block in enumerate(blocks[:kept]):
            kept_ref[array, 8 * index : 8 * index + 8, :width] = block
    kept_ref[0, :8, width:] = energy
    for index, send_ref in enumerate(send_refs):
        if carried:
            above = refs[0].shape[0]
            send_ref[:above, :] = refs[0][...]
            send_ref = send_ref.at[above:, :]
        first = kept * (index + 1)
        store_coded([send_ref], [block for blocks in sums for block in blocks[first : first + kept]], energy)


def combine(keep, came, sent, carry, after, length):
    _, height, width = keep.shape
    kept = height // (sent + 1)
    parts, senders = len(came[0]), len(came)
    above = sum(array.shape[0] for array in carry)
    keep, *sends = pl.pallas_call(
        functools.partial(combine_kernel, parts, senders, len(carry), len(after)),
        out_shape=(jax.ShapeDtypeStruct((2, kept, width), jnp.float32),)
        + (jax.ShapeDtypeStruct((above + 2 * kept, width), jnp.bfloat16),) * sent,
        in_specs=[WHOLE] * (1 + parts * senders) + [ANYWHERE] * len(after) + [WHOLE] * len(carry),
        out_specs=(WHOLE,) * (1 + sent),
        compiler_params=limit(8),
        cost_estimate=cost(length),
        name="combine",
    )(keep, *[part for parts in came for part in parts], *after, *carry)
    return [[send] for send in sends], keep


def finish_kernel(count, *refs):
    (gradient_ref, log_ref), refs = refs[-2:], refs[:-2]
    came = [ref.at[16 * place : 16 * place + 16, :] for ref, group in zip(refs[-len(GROUPS) :], GROUPS) for place in range(len(group))]
    keep_refs = refs[: -len(GROUPS)]
    row = 0
    for piece, keep_ref in enumerate(keep_refs):
        (gradient, log), energy = add_came(keep_ref, [[came[piece]]])
        correction = 2.0 * (energy[:, :1] / count - OFFSET)
        for block in range(len(log)):
            log_mean = log[block] / count
            gradient_ref[row : row + 8, :] = gradient[block] / count - correction * log_mean
            log_ref[row : row + 8, :] = log_mean
            row += 8


def finish(keeps, came, count):
    _, rows, width = keeps[0].shape
    out = jax.ShapeDtypeStruct((rows * len(keeps), width - EXTRA), jnp.float32)
    return pl.pallas_call(
        functools.partial(finish_kernel, count),
        out_shape=(out, out),
        in_specs=[WHOLE] * (len(keeps) + len(came)),
        out_specs=(WHOLE, WHOLE),
        compiler_params=limit(8),
        cost_estimate=cost(0.1),
        name="finish",
    )(*keeps, *came)


def pieced_body(pieces, tile, inverse_rows, kinetic_rows, virt_values, virt_laplacians, local_energy):
    count = lax.axis_size("walk")
    stages = stage_masks(count)
    me = lax.axis_index("walk").astype(jnp.int32).reshape(1)
    virt = lax.axis_index("virt").astype(jnp.int32).reshape(1)
    occupied, depth = inverse_rows.shape[1:]
    by_dest = (count, occupied // count, depth)
    inverse, kinetic = inverse_rows.reshape(by_dest), kinetic_rows.reshape(by_dest)
    rows = occupied // (count * pieces)

    inverse, kinetic, values, laplacians = (
        pltpu.with_memory_space_constraint(array, pltpu.HBM)
        for array in (inverse, kinetic, virt_values[0], virt_laplacians[0])
    )
    mine = [part for group in range(pieces // 2) for part in cut(inverse, kinetic, group)]
    theirs = [swap(part, "virt", 1) for part in mine]
    near, values, laplacians = near_product(virt, me, local_energy, inverse, kinetic, values, laplacians, mine[2:])

    keep, first, came = {}, {}, []
    late, carry = [], ()
    for turn in range(pieces + 1):
        if turn < pieces:
            after = [keep[turn - 1]] if turn else []
            send, kept = far_product(
                virt, me, local_energy, theirs[turn], near, turn * rows, values, laplacians, tile, stages, 1 if turn else 2, after
            )
            first[turn] = [[swap(part, "walk", mask) for part in parts] for parts, mask in zip(send, partners(stages[0]))]
        if turn:
            piece = turn - 1
            sends, keep[piece] = combine(keep[piece], second, len(partners(stages[2])), carry, [], BESIDE)
            carry = tuple(sends[0])
            if any(piece == group[-1] for group in GROUPS):
                came.append(swap(carry[0], "walk", stages[2][0]))
                carry = ()
        if turn < pieces:
            after = ([keep[turn - 1]] if turn else [])
            sends, keep[turn] = combine(kept, first[turn], len(partners(stages[1])), (), after, 0.1)
            second = [[swap(part, "walk", mask) for part in parts] for parts, mask in zip(sends, partners(stages[1]))]
    return finish([keep[piece] for piece in range(pieces)], came, count)


def solution(mesh):
    placed = (
        P("walk", None, "virt"),
        P("walk", None, "virt"),
        P("walk", None, "virt"),
        P("walk", None, "virt"),
        P("walk"),
    )

    def body(inverse_rows, kinetic_rows, virt_values, virt_laplacians, local_energy):
        count = mesh.shape["walk"]
        walkers, occupied, depth = inverse_rows.shape
        width = virt_values.shape[2]
        tile = 512
        fits = (
            walkers == 1
            and mesh.shape["virt"] == 2
            and count == 16
            and count >= 4
            and occupied == count * PIECES * 8
            and depth % 256 == 0
            and width % tile == 0
        )
        form = functools.partial(pieced_body, PIECES, tile) if fits else general_body
        return form(inverse_rows, kinetic_rows, virt_values, virt_laplacians, local_energy)

    return jax.shard_map(
        body,
        mesh=mesh,
        in_specs=placed,
        out_specs=(P("walk", "virt"), P("walk", "virt")),
        check_vma=False,
    )
```

```python
import functools

import jax
import jax.numpy as jnp
from jax import lax
from jax.experimental import pallas as pl
from jax.experimental.pallas import tpu as pltpu
from jax.sharding import PartitionSpec as P

PIECES = 4
GROUPS = ((0, 1, 2), (3,))
EXCHANGED = (3,)
BESIDE = 6


def product(left, right):
    return jnp.einsum("woe,wev->wov", left, right, preferred_element_type=jnp.float32)


def gradient_terms(log_grad, kin_part, weights):
    kin_grad = -0.5 * kin_part
    weighted = jnp.sum(weights[:, None, None] * log_grad + kin_grad, axis=0)
    return (weighted, jnp.sum(log_grad, axis=0))


def general_body(inverse_rows, kinetic_rows, virt_values, virt_laplacians, local_energy):
    walk_count = lax.axis_size("walk")
    walker_count = walk_count * local_energy.shape[0]
    energy_sum = lax.psum(jnp.sum(local_energy), "walk")
    average = energy_sum / walker_count
    weights = 2.0 * (local_energy - average)
    inverse_all, kinetic_all = (
        lax.all_gather(inverse_rows, "virt", axis=2, tiled=True),
        lax.all_gather(kinetic_rows, "virt", axis=2, tiled=True),
    )
    log_grad = product(inverse_all, virt_values)
    kin_part = product(inverse_all, virt_laplacians) - product(kinetic_all, virt_values)
    weighted, log_sum = gradient_terms(log_grad, kin_part, weights)
    summed = (
        lax.psum_scatter(weighted, "walk", scatter_dimension=0, tiled=True),
        lax.psum_scatter(log_sum, "walk", scatter_dimension=0, tiled=True),
    )
    gradient_part, log_part = (summed[0], summed[1])
    return (gradient_part / walker_count, log_part / walker_count)


SPAN = 248.0
EXTRA = 128
PART = EXTRA // 4
OFFSET = 3.1
TINY = 1e-30
MIB = 1024 * 1024


def stage_masks(count):
    bits = [1 << bit for bit in range(count.bit_length() - 1)]
    if len(bits) < 3:
        return [[bit] for bit in bits]
    return [bits[:1], bits[1:3]] + [[bit] for bit in bits[3:]]


def place_weights(stages):
    order = [mask for stage in stages for mask in stage]
    weights = [0] * len(order)
    for index, mask in enumerate(order):
        weights[mask.bit_length() - 1] = 1 << (len(order) - 1 - index)
    return weights


def partners(stage):
    if len(stage) == 1:
        return list(stage)
    first, second = stage
    return [second, first, first ^ second]


def swap(array, axis, mask):
    pairs = [(source, source ^ mask) for source in range(lax.axis_size(axis))]
    return lax.ppermute(array, axis, pairs)


def exchange(array, stage):
    first, second = stage
    count = lax.axis_size("walk")
    groups = [
        [base, base + first, base + second, base + first + second]
        for base in range(count)
        if not base & (first | second)
    ]
    return lax.all_to_all(array, "walk", 0, 0, axis_index_groups=groups, tiled=True)


PLACES = (2, 1, 3)


def encode(rows):
    magnitude = jnp.abs(rows)
    largest = jnp.maximum(jnp.max(magnitude, axis=-1, keepdims=True), TINY)
    scale = (largest * (1.0 + 2.0**-7)).astype(jnp.bfloat16).astype(jnp.float32)
    code = jnp.exp2(magnitude * (SPAN / scale) - SPAN / 2)
    return jnp.where(rows < 0, -code, code).astype(jnp.bfloat16), scale


def decode(coded):
    width = coded.shape[1] - EXTRA
    code = coded[:, :width].astype(jnp.float32)
    scale = coded[:, width : width + 1].astype(jnp.float32)
    magnitude = (jnp.log2(jnp.abs(code)) + SPAN / 2) * (scale / SPAN)
    return jnp.where(code < 0, -magnitude, magnitude)


def store_coded(send_refs, blocks, energy):
    width = send_refs[0].shape[1] - EXTRA
    each = send_refs[0].shape[0]
    f32, bf16 = jnp.float32, jnp.bfloat16
    energy = jnp.concatenate([energy, energy], axis=0)
    high = energy.astype(bf16).astype(f32)
    middle = (energy - high).astype(bf16).astype(f32)
    low = energy - high - middle
    lane = lax.broadcasted_iota(jnp.int32, energy.shape, 1)
    terms = jnp.where(lane < 2 * PART, high, jnp.where(lane < 3 * PART, middle, low))
    for pair in range(len(blocks) // 2):
        code, scale = encode(jnp.concatenate(blocks[2 * pair : 2 * pair + 2], axis=0))
        send_ref = send_refs[16 * pair // each]
        target = slice(16 * pair % each, 16 * pair % each + 16)
        send_ref[target, :width] = code
        send_ref[target, width:] = jnp.where(lane < PART, scale, terms).astype(bf16)


def add_came(keep_ref, came_refs):
    arrays, height, width = keep_ref.shape
    width -= EXTRA
    per = height // 8
    sums = [keep_ref[index // per, 8 * (index % per) : 8 * (index % per) + 8, :width] for index in range(arrays * per)]
    energy = keep_ref[0, :8, width:]
    for parts in came_refs:
        index = 0
        for part in parts:
            for row in range(0, part.shape[0], 16):
                both = decode(part[row : row + 16, :])
                sums[index] += both[:8]
                sums[index + 1] += both[8:]
                index += 2
        terms = parts[0][:16, width:].astype(jnp.float32)[:8]
        for term in range(1, 4):
            energy += terms[:, term * PART : term * PART + 1]
    return [sums[array * per : (array + 1) * per] for array in range(arrays)], energy


def limit(mib):
    return pltpu.CompilerParams(vmem_limit_bytes=mib * MIB)


def cost(microseconds):
    return pl.CostEstimate(flops=int(microseconds * 1.1e9), bytes_accessed=0, transcendentals=0)


WHOLE = pl.BlockSpec(memory_space=pltpu.VMEM)
SCALAR = pl.BlockSpec(memory_space=pltpu.SMEM)
ANYWHERE = pl.BlockSpec(memory_space=pl.ANY)
HELD = pl.BlockSpec(memory_space=pltpu.HBM)
HELD = pl.BlockSpec(memory_space=pltpu.HBM)


def cut_kernel(inverse_ref, kinetic_ref, *out_refs):
    count = inverse_ref.shape[0]
    for array, ref in enumerate((inverse_ref, kinetic_ref)):
        for dest in range(0, count, 2):
            pair = [ref[dest + other].astype(jnp.float32) for other in range(2)]
            for index, out_ref in enumerate(out_refs):
                rows = jnp.concatenate([block[8 * index : 8 * index + 8] for block in pair], axis=0)
                out_ref[array, 8 * dest : 8 * dest + 16, :] = rows.astype(jnp.bfloat16)


def cut(inverse, kinetic, group):
    count, _, depth = inverse.shape
    block = pl.BlockSpec((count, 16, depth), lambda step: (0, group, 0))
    out = jax.ShapeDtypeStruct((2, 8 * count, depth), jnp.bfloat16)
    return pl.pallas_call(
        cut_kernel,
        out_shape=(out, out),
        grid=(1,),
        in_specs=[block, block],
        out_specs=(pl.BlockSpec(out.shape, lambda step: (0, 0, 0)),) * 2,
        compiler_params=limit(12),
        cost_estimate=cost(0.1),
        name="cut",
    )(inverse, kinetic)


def near_kernel(chunk, tile, virt_ref, me_ref, energy_ref, inverse_ref, kinetic_ref, values_ref, laps_ref, *rest):
    out_ref, far_values, far_laps, near_values, near_laps, own_inverse, own_kinetic, sems = rest[-8:]
    count, per, depth = inverse_ref.shape
    height = count * per
    width = out_ref.shape[3]
    f32 = jnp.float32
    own = pl.ds(pl.multiple_of(virt_ref[0] * depth, depth), depth)
    other = pl.ds(pl.multiple_of((1 - virt_ref[0]) * depth, depth), depth)
    chunks = width // chunk

    copies = []
    for index in range(chunks):
        columns = pl.ds(index * chunk, chunk)
        copies.append([
            pltpu.make_async_copy(table.at[own, columns], held.at[:, columns], sems.at[index, which])
            for which, (table, held) in enumerate(((values_ref, near_values), (laps_ref, near_laps)))
        ])
    last = [
        pltpu.make_async_copy(table.at[other, :], held, sems.at[chunks, which])
        for which, (table, held) in enumerate(((values_ref, far_values), (laps_ref, far_laps)))
    ]
    first = [
        pltpu.make_async_copy(rows, held, sems.at[chunks + 1, which])
        for which, (rows, held) in enumerate(((inverse_ref, own_inverse), (kinetic_ref, own_kinetic)))
    ]
    for copy in first + sum(copies, []) + last:
        copy.start()
    for copy in first:
        copy.wait()
    inverse = own_inverse[...].reshape(height, depth)
    kinetic = own_kinetic[...].reshape(height, depth)
    for index in range(chunks):
        for copy in copies[index]:
            copy.wait()

        @pl.loop(index * chunk // tile, (index + 1) * chunk // tile)
        def _(step):
            columns = pl.ds(pl.multiple_of(step * tile, tile), tile)
            values, laps = near_values[:, columns], near_laps[:, columns]
            out_ref[1, :, :, columns] = jnp.dot(inverse, values, preferred_element_type=f32).reshape(count, per, tile)
            rest = jnp.dot(kinetic, values, preferred_element_type=f32)
            rest -= jnp.dot(inverse, laps, preferred_element_type=f32)
            out_ref[0, :, :, columns] = (0.5 * rest).reshape(count, per, tile)

    for copy in last:
        copy.wait()


def near_product(virt, me, energy, inverse, kinetic, values, laplacians, after):
    count, per, depth = inverse.shape
    width = values.shape[1]
    chunk, tile = 512, 256
    table = pltpu.VMEM((depth, width), jnp.bfloat16)
    own = pltpu.VMEM((count, per, depth), jnp.bfloat16)
    return pl.pallas_call(
        functools.partial(near_kernel, chunk, tile),
        out_shape=(jax.ShapeDtypeStruct((2, count, per, width), jnp.float32), table, table),
        in_specs=[SCALAR, SCALAR, SCALAR, HELD, HELD, HELD, HELD] + [ANYWHERE] * len(after),
        out_specs=(WHOLE, WHOLE, WHOLE),
        scratch_shapes=[table, table, own, own, pltpu.SemaphoreType.DMA((width // chunk + 2, 2))],
        compiler_params=limit(24),
        cost_estimate=cost(9),
        name="near_product",
    )(virt, me, energy, inverse, kinetic, values, laplacians, *after)


def far_kernel(weights, count, tile, first, split, virt_ref, me_ref, energy_ref, far_ref, near_ref, values_ref, laps_ref, *rest):
    send_refs, (keep_ref, place_ref) = rest[-split - 2 : -2], rest[-2:]
    _, height, depth = far_ref.shape
    width = near_ref.shape[3]
    rows = height // count
    half = height // 2
    f32 = jnp.float32
    scale = 2.0 * (energy_ref[0] - OFFSET)

    @pl.loop(0, width // tile)
    def _(index):
        columns = pl.ds(pl.multiple_of(index * tile, tile), tile)
        near = near_ref[:, :, first : first + rows, columns].reshape(2, height, tile)
        both = jnp.dot(far_ref[...].reshape(2 * height, depth), values_ref[:, columns], preferred_element_type=f32)
        laps = jnp.dot(far_ref[0], laps_ref[:, columns], preferred_element_type=f32)
        log = both[:height] + near[1]
        weighted = scale * log + (0.5 * (both[height:] - laps) + near[0])
        for dest in range(count):
            difference = dest ^ me_ref[0]
            place = 0
            for bit, weight in enumerate(weights):
                place = place ^ (((difference >> bit) & 1) * weight)
            target = pl.ds(pl.multiple_of(place * rows, rows), rows)
            source = slice(dest * rows, (dest + 1) * rows)
            place_ref[0, target, columns] = weighted[source]
            place_ref[1, target, columns] = log[source]

    energy = jnp.full((8, EXTRA), energy_ref[0], f32)
    keep_ref[:, :, :width] = place_ref[:, :half]
    keep_ref[0, :8, width:] = energy
    blocks = [place_ref[array, row : row + 8, :] for array in range(2) for row in range(half, height, 8)]
    store_coded(send_refs, blocks, energy)


def far_product(virt, me, energy, theirs, near, first, values, laplacians, tile, stages, split, after):
    _, height, depth = theirs.shape
    width = values.shape[1]
    half = height // 2
    count = 1 << sum(len(stage) for stage in stages)
    *sends, keep = pl.pallas_call(
        functools.partial(far_kernel, place_weights(stages), count, tile, first, split),
        out_shape=(jax.ShapeDtypeStruct((2 * half // split, width + EXTRA), jnp.bfloat16),) * split
        + (jax.ShapeDtypeStruct((2, half, width + EXTRA), jnp.float32),),
        in_specs=[SCALAR, SCALAR, SCALAR, WHOLE, WHOLE, WHOLE, WHOLE] + [ANYWHERE] * len(after),
        out_specs=(WHOLE,) * (split + 1),
        scratch_shapes=[pltpu.VMEM((2, height, width), jnp.float32)],
        compiler_params=limit(24),
        cost_estimate=cost(0.1),
        name="far_product",
    )(virt, me, energy, theirs, near, values, laplacians, *after)
    return [sends], keep


def combine_kernel(parts, senders, carried, ordered, slots_in, slots_out, me_ref, keep_ref, *refs):
    came_refs = [refs[parts * sender : parts * sender + parts] for sender in range(senders)]
    refs = refs[parts * senders + ordered :]
    if slots_in:
        came_refs = [[came_refs[0][0].at[(me_ref[0] // slots_in & 3) ^ place]] for place in PLACES]
    kept_ref, send_refs = refs[carried], refs[carried + 1 :]
    width = keep_ref.shape[2] - EXTRA
    sums, energy = add_came(keep_ref, came_refs)
    kept = kept_ref.shape[1] // 8
    for array, blocks in enumerate(sums):
        for index, block in enumerate(blocks[:kept]):
            kept_ref[array, 8 * index : 8 * index + 8, :width] = block
    kept_ref[0, :8, width:] = energy
    if slots_out:
        place = me_ref[0] // slots_out & 3
        send_refs = [send_refs[0].at[place]] + [send_refs[0].at[place ^ other] for other in PLACES]
        store_coded(send_refs[:1], [block for blocks in sums for block in blocks[:kept]], energy)
        send_refs = send_refs[1:]
    for index, send_ref in enumerate(send_refs):
        if carried:
            above = refs[0].shape[0]
            send_ref[:above, :] = refs[0][...]
            send_ref = send_ref.at[above:, :]
        first = kept * (index + 1)
        store_coded([send_ref], [block for blocks in sums for block in blocks[first : first + kept]], energy)


def combine(me, keep, came, sent, carry, after, length, slots_in=0, slots_out=0):
    _, height, width = keep.shape
    kept = height // (sent + 1)
    parts, senders = len(came[0]), len(came)
    above = sum(array.shape[0] for array in carry)
    coded = jax.ShapeDtypeStruct((above + 2 * kept, width), jnp.bfloat16)
    coded = (jax.ShapeDtypeStruct((4, 2 * kept, width), jnp.bfloat16),) if slots_out else (coded,) * sent
    keep, *sends = pl.pallas_call(
        functools.partial(combine_kernel, parts, senders, len(carry), len(after), slots_in, slots_out),
        out_shape=(jax.ShapeDtypeStruct((2, kept, width), jnp.float32),) + coded,
        in_specs=[SCALAR] + [WHOLE] * (1 + parts * senders) + [ANYWHERE] * len(after) + [WHOLE] * len(carry),
        out_specs=(WHOLE,) * (1 + len(coded)),
        compiler_params=limit(8),
        cost_estimate=cost(length),
        name="combine",
    )(me, keep, *[part for parts in came for part in parts], *after, *carry)
    return [[send] for send in sends], keep


def finish_kernel(count, *refs):
    (gradient_ref, log_ref), refs = refs[-2:], refs[:-2]
    came = [ref.at[16 * place : 16 * place + 16, :] for ref, group in zip(refs[-len(GROUPS) :], GROUPS) for place in range(len(group))]
    keep_refs = refs[: -len(GROUPS)]
    row = 0
    for piece, keep_ref in enumerate(keep_refs):
        (gradient, log), energy = add_came(keep_ref, [[came[piece]]])
        correction = 2.0 * (energy[:, :1] / count - OFFSET)
        for block in range(len(log)):
            log_mean = log[block] / count
            gradient_ref[row : row + 8, :] = gradient[block] / count - correction * log_mean
            log_ref[row : row + 8, :] = log_mean
            row += 8


def finish(keeps, came, count):
    _, rows, width = keeps[0].shape
    out = jax.ShapeDtypeStruct((rows * len(keeps), width - EXTRA), jnp.float32)
    return pl.pallas_call(
        functools.partial(finish_kernel, count),
        out_shape=(out, out),
        in_specs=[WHOLE] * (len(keeps) + len(came)),
        out_specs=(WHOLE, WHOLE),
        compiler_params=limit(8),
        cost_estimate=cost(0.1),
        name="finish",
    )(*keeps, *came)


def pieced_body(pieces, tile, inverse_rows, kinetic_rows, virt_values, virt_laplacians, local_energy):
    count = lax.axis_size("walk")
    stages = stage_masks(count)
    me = lax.axis_index("walk").astype(jnp.int32).reshape(1)
    virt = lax.axis_index("virt").astype(jnp.int32).reshape(1)
    occupied, depth = inverse_rows.shape[1:]
    by_dest = (count, occupied // count, depth)
    inverse, kinetic = inverse_rows.reshape(by_dest), kinetic_rows.reshape(by_dest)
    rows = occupied // (count * pieces)

    inverse, kinetic, values, laplacians = (
        pltpu.with_memory_space_constraint(array, pltpu.HBM)
        for array in (inverse, kinetic, virt_values[0], virt_laplacians[0])
    )
    mine = [part for group in range(pieces // 2) for part in cut(inverse, kinetic, group)]
    theirs = [swap(part, "virt", 1) for part in mine]
    near, values, laplacians = near_product(virt, me, local_energy, inverse, kinetic, values, laplacians, mine[2:])

    keep, first, came = {}, {}, []
    carry, slots = (), 0
    for turn in range(pieces + 1):
        if turn < pieces:
            after = [keep[turn - 1]] if turn else []
            send, kept = far_product(
                virt, me, local_energy, theirs[turn], near, turn * rows, values, laplacians, tile, stages, 1 if turn else 2, after
            )
            first[turn] = [[swap(part, "walk", mask) for part in parts] for parts, mask in zip(send, partners(stages[0]))]
        if turn:
            piece = turn - 1
            sends, keep[piece] = combine(
                me, keep[piece], second, len(partners(stages[2])), carry, [], BESIDE, slots_in=slots
            )
            carry = tuple(sends[0])
            if any(piece == group[-1] for group in GROUPS):
                came.append(swap(carry[0], "walk", stages[2][0]))
                carry = ()
        if turn < pieces:
            after = [keep[turn - 1]] if turn else []
            slots = stages[1][0] if turn in EXCHANGED else 0
            sends, keep[turn] = combine(
                me, kept, first[turn], len(partners(stages[1])), (), after, 0.1, slots_out=slots
            )
            if slots:
                second = [[exchange(sends[0][0], stages[1])]]
            else:
                second = [[swap(part, "walk", mask) for part in parts] for parts, mask in zip(sends, partners(stages[1]))]
    return finish([keep[piece] for piece in range(pieces)], came, count)


def solution(mesh):
    placed = (
        P("walk", None, "virt"),
        P("walk", None, "virt"),
        P("walk", None, "virt"),
        P("walk", None, "virt"),
        P("walk"),
    )

    def body(inverse_rows, kinetic_rows, virt_values, virt_laplacians, local_energy):
        count = mesh.shape["walk"]
        walkers, occupied, depth = inverse_rows.shape
        width = virt_values.shape[2]
        tile = 512
        fits = (
            walkers == 1
            and mesh.shape["virt"] == 2
            and count == 16
            and count >= 4
            and occupied == count * PIECES * 8
            and depth % 256 == 0
            and width % tile == 0
        )
        form = functools.partial(pieced_body, PIECES, tile) if fits else general_body
        return form(inverse_rows, kinetic_rows, virt_values, virt_laplacians, local_energy)

    return jax.shard_map(
        body,
        mesh=mesh,
        in_specs=placed,
        out_specs=(P("walk", "virt"), P("walk", "virt")),
        check_vma=False,
    )
```

```python
import functools

import jax
import jax.numpy as jnp
from jax import lax
from jax.experimental import pallas as pl
from jax.experimental.pallas import tpu as pltpu
from jax.sharding import PartitionSpec as P

PIECES = 4
GROUPS = ((0, 1), (2,), (3,))
FAR = (0.1, 1.5, 0.1, 0.1)
BESIDE = 6


def product(left, right):
    return jnp.einsum("woe,wev->wov", left, right, preferred_element_type=jnp.float32)


def gradient_terms(log_grad, kin_part, weights):
    kin_grad = -0.5 * kin_part
    weighted = jnp.sum(weights[:, None, None] * log_grad + kin_grad, axis=0)
    return (weighted, jnp.sum(log_grad, axis=0))


def general_body(inverse_rows, kinetic_rows, virt_values, virt_laplacians, local_energy):
    walk_count = lax.axis_size("walk")
    walker_count = walk_count * local_energy.shape[0]
    energy_sum = lax.psum(jnp.sum(local_energy), "walk")
    average = energy_sum / walker_count
    weights = 2.0 * (local_energy - average)
    inverse_all, kinetic_all = (
        lax.all_gather(inverse_rows, "virt", axis=2, tiled=True),
        lax.all_gather(kinetic_rows, "virt", axis=2, tiled=True),
    )
    log_grad = product(inverse_all, virt_values)
    kin_part = product(inverse_all, virt_laplacians) - product(kinetic_all, virt_values)
    weighted, log_sum = gradient_terms(log_grad, kin_part, weights)
    summed = (
        lax.psum_scatter(weighted, "walk", scatter_dimension=0, tiled=True),
        lax.psum_scatter(log_sum, "walk", scatter_dimension=0, tiled=True),
    )
    gradient_part, log_part = (summed[0], summed[1])
    return (gradient_part / walker_count, log_part / walker_count)


SPAN = 248.0
EXTRA = 128
PART = EXTRA // 4
OFFSET = 3.1
TINY = 1e-30
MIB = 1024 * 1024


def stage_masks(count):
    bits = [1 << bit for bit in range(count.bit_length() - 1)]
    if len(bits) < 3:
        return [[bit] for bit in bits]
    return [bits[:1], bits[1:3]] + [[bit] for bit in bits[3:]]


def place_weights(stages):
    order = [mask for stage in stages for mask in stage]
    weights = [0] * len(order)
    for index, mask in enumerate(order):
        weights[mask.bit_length() - 1] = 1 << (len(order) - 1 - index)
    return weights


def partners(stage):
    if len(stage) == 1:
        return list(stage)
    first, second = stage
    return [second, first, first ^ second]


def swap(array, axis, mask):
    pairs = [(source, source ^ mask) for source in range(lax.axis_size(axis))]
    return lax.ppermute(array, axis, pairs)


def encode(rows):
    magnitude = jnp.abs(rows)
    largest = jnp.maximum(jnp.max(magnitude, axis=-1, keepdims=True), TINY)
    scale = (largest * (1.0 + 2.0**-7)).astype(jnp.bfloat16).astype(jnp.float32)
    code = jnp.exp2(magnitude * (SPAN / scale) - SPAN / 2)
    return jnp.where(rows < 0, -code, code).astype(jnp.bfloat16), scale


def decode(coded):
    width = coded.shape[1] - EXTRA
    code = coded[:, :width].astype(jnp.float32)
    scale = coded[:, width : width + 1].astype(jnp.float32)
    magnitude = (jnp.log2(jnp.abs(code)) + SPAN / 2) * (scale / SPAN)
    return jnp.where(code < 0, -magnitude, magnitude)


def store_coded(send_refs, blocks, energy):
    width = send_refs[0].shape[1] - EXTRA
    each = send_refs[0].shape[0]
    f32, bf16 = jnp.float32, jnp.bfloat16
    energy = jnp.concatenate([energy, energy], axis=0)
    high = energy.astype(bf16).astype(f32)
    middle = (energy - high).astype(bf16).astype(f32)
    low = energy - high - middle
    lane = lax.broadcasted_iota(jnp.int32, energy.shape, 1)
    terms = jnp.where(lane < 2 * PART, high, jnp.where(lane < 3 * PART, middle, low))
    for pair in range(len(blocks) // 2):
        code, scale = encode(jnp.concatenate(blocks[2 * pair : 2 * pair + 2], axis=0))
        send_ref = send_refs[16 * pair // each]
        target = slice(16 * pair % each, 16 * pair % each + 16)
        send_ref[target, :width] = code
        send_ref[target, width:] = jnp.where(lane < PART, scale, terms).astype(bf16)


def add_came(keep_ref, came_refs):
    arrays, height, width = keep_ref.shape
    width -= EXTRA
    per = height // 8
    sums = [keep_ref[index // per, 8 * (index % per) : 8 * (index % per) + 8, :width] for index in range(arrays * per)]
    energy = keep_ref[0, :8, width:]
    for parts in came_refs:
        index = 0
        for part in parts:
            for row in range(0, part.shape[0], 16):
                both = decode(part[row : row + 16, :])
                sums[index] += both[:8]
                sums[index + 1] += both[8:]
                index += 2
        terms = parts[0][:16, width:].astype(jnp.float32)[:8]
        for term in range(1, 4):
            energy += terms[:, term * PART : term * PART + 1]
    return [sums[array * per : (array + 1) * per] for array in range(arrays)], energy


def limit(mib):
    return pltpu.CompilerParams(vmem_limit_bytes=mib * MIB)


def cost(microseconds):
    return pl.CostEstimate(flops=int(microseconds * 1.1e9), bytes_accessed=0, transcendentals=0)


WHOLE = pl.BlockSpec(memory_space=pltpu.VMEM)
SCALAR = pl.BlockSpec(memory_space=pltpu.SMEM)
ANYWHERE = pl.BlockSpec(memory_space=pl.ANY)
HELD = pl.BlockSpec(memory_space=pltpu.HBM)
HELD = pl.BlockSpec(memory_space=pltpu.HBM)


def cut_kernel(inverse_ref, kinetic_ref, *out_refs):
    count = inverse_ref.shape[0]
    for array, ref in enumerate((inverse_ref, kinetic_ref)):
        for dest in range(0, count, 2):
            pair = [ref[dest + other].astype(jnp.float32) for other in range(2)]
            for index, out_ref in enumerate(out_refs):
                rows = jnp.concatenate([block[8 * index : 8 * index + 8] for block in pair], axis=0)
                out_ref[array, 8 * dest : 8 * dest + 16, :] = rows.astype(jnp.bfloat16)


def cut(inverse, kinetic, group):
    count, _, depth = inverse.shape
    block = pl.BlockSpec((count, 16, depth), lambda step: (0, group, 0))
    out = jax.ShapeDtypeStruct((2, 8 * count, depth), jnp.bfloat16)
    return pl.pallas_call(
        cut_kernel,
        out_shape=(out, out),
        grid=(1,),
        in_specs=[block, block],
        out_specs=(pl.BlockSpec(out.shape, lambda step: (0, 0, 0)),) * 2,
        compiler_params=limit(12),
        cost_estimate=cost(0.1),
        name="cut",
    )(inverse, kinetic)


def near_kernel(chunk, tile, virt_ref, me_ref, energy_ref, inverse_ref, kinetic_ref, values_ref, laps_ref, *rest):
    out_ref, far_values, far_laps, near_values, near_laps, own_inverse, own_kinetic, sems = rest[-8:]
    count, per, depth = inverse_ref.shape
    height = count * per
    width = out_ref.shape[3]
    f32 = jnp.float32
    own = pl.ds(pl.multiple_of(virt_ref[0] * depth, depth), depth)
    other = pl.ds(pl.multiple_of((1 - virt_ref[0]) * depth, depth), depth)
    chunks = width // chunk

    copies = []
    for index in range(chunks):
        columns = pl.ds(index * chunk, chunk)
        copies.append([
            pltpu.make_async_copy(table.at[own, columns], held.at[:, columns], sems.at[index, which])
            for which, (table, held) in enumerate(((values_ref, near_values), (laps_ref, near_laps)))
        ])
    last = [
        pltpu.make_async_copy(table.at[other, :], held, sems.at[chunks, which])
        for which, (table, held) in enumerate(((values_ref, far_values), (laps_ref, far_laps)))
    ]
    first = [
        pltpu.make_async_copy(rows, held, sems.at[chunks + 1, which])
        for which, (rows, held) in enumerate(((inverse_ref, own_inverse), (kinetic_ref, own_kinetic)))
    ]
    for copy in first + sum(copies, []) + last:
        copy.start()
    for copy in first:
        copy.wait()
    inverse = own_inverse[...].reshape(height, depth)
    kinetic = own_kinetic[...].reshape(height, depth)
    for index in range(chunks):
        for copy in copies[index]:
            copy.wait()

        @pl.loop(index * chunk // tile, (index + 1) * chunk // tile)
        def _(step):
            columns = pl.ds(pl.multiple_of(step * tile, tile), tile)
            values, laps = near_values[:, columns], near_laps[:, columns]
            out_ref[1, :, :, columns] = jnp.dot(inverse, values, preferred_element_type=f32).reshape(count, per, tile)
            rest = jnp.dot(kinetic, values, preferred_element_type=f32)
            rest -= jnp.dot(inverse, laps, preferred_element_type=f32)
            out_ref[0, :, :, columns] = (0.5 * rest).reshape(count, per, tile)

    for copy in last:
        copy.wait()


def near_product(virt, me, energy, inverse, kinetic, values, laplacians, after):
    count, per, depth = inverse.shape
    width = values.shape[1]
    chunk, tile = 512, 256
    table = pltpu.VMEM((depth, width), jnp.bfloat16)
    own = pltpu.VMEM((count, per, depth), jnp.bfloat16)
    return pl.pallas_call(
        functools.partial(near_kernel, chunk, tile),
        out_shape=(jax.ShapeDtypeStruct((2, count, per, width), jnp.float32), table, table),
        in_specs=[SCALAR, SCALAR, SCALAR, HELD, HELD, HELD, HELD] + [ANYWHERE] * len(after),
        out_specs=(WHOLE, WHOLE, WHOLE),
        scratch_shapes=[table, table, own, own, pltpu.SemaphoreType.DMA((width // chunk + 2, 2))],
        compiler_params=limit(24),
        cost_estimate=cost(9),
        name="near_product",
    )(virt, me, energy, inverse, kinetic, values, laplacians, *after)


def far_kernel(weights, count, tile, first, split, virt_ref, me_ref, energy_ref, far_ref, near_ref, values_ref, laps_ref, *rest):
    send_refs, (keep_ref, place_ref) = rest[-split - 2 : -2], rest[-2:]
    _, height, depth = far_ref.shape
    width = near_ref.shape[3]
    rows = height // count
    half = height // 2
    f32 = jnp.float32
    scale = 2.0 * (energy_ref[0] - OFFSET)

    @pl.loop(0, width // tile)
    def _(index):
        columns = pl.ds(pl.multiple_of(index * tile, tile), tile)
        near = near_ref[:, :, first : first + rows, columns].reshape(2, height, tile)
        both = jnp.dot(far_ref[...].reshape(2 * height, depth), values_ref[:, columns], preferred_element_type=f32)
        laps = jnp.dot(far_ref[0], laps_ref[:, columns], preferred_element_type=f32)
        log = both[:height] + near[1]
        weighted = scale * log + (0.5 * (both[height:] - laps) + near[0])
        for dest in range(count):
            difference = dest ^ me_ref[0]
            place = 0
            for bit, weight in enumerate(weights):
                place = place ^ (((difference >> bit) & 1) * weight)
            target = pl.ds(pl.multiple_of(place * rows, rows), rows)
            source = slice(dest * rows, (dest + 1) * rows)
            place_ref[0, target, columns] = weighted[source]
            place_ref[1, target, columns] = log[source]

    energy = jnp.full((8, EXTRA), energy_ref[0], f32)
    keep_ref[:, :, :width] = place_ref[:, :half]
    keep_ref[0, :8, width:] = energy
    blocks = [place_ref[array, row : row + 8, :] for array in range(2) for row in range(half, height, 8)]
    store_coded(send_refs, blocks, energy)


def far_product(virt, me, energy, theirs, near, first, values, laplacians, tile, stages, split, after, length):
    _, height, depth = theirs.shape
    width = values.shape[1]
    half = height // 2
    count = 1 << sum(len(stage) for stage in stages)
    *sends, keep = pl.pallas_call(
        functools.partial(far_kernel, place_weights(stages), count, tile, first, split),
        out_shape=(jax.ShapeDtypeStruct((2 * half // split, width + EXTRA), jnp.bfloat16),) * split
        + (jax.ShapeDtypeStruct((2, half, width + EXTRA), jnp.float32),),
        in_specs=[SCALAR, SCALAR, SCALAR, WHOLE, WHOLE, WHOLE, WHOLE] + [ANYWHERE] * len(after),
        out_specs=(WHOLE,) * (split + 1),
        scratch_shapes=[pltpu.VMEM((2, height, width), jnp.float32)],
        compiler_params=limit(24),
        cost_estimate=cost(length),
        name="far_product",
    )(virt, me, energy, theirs, near, values, laplacians, *after)
    return [sends], keep


def combine_kernel(parts, senders, carried, ordered, *refs):
    keep_ref, refs = refs[0], refs[1:]
    came_refs = [refs[parts * sender : parts * sender + parts] for sender in range(senders)]
    refs = refs[parts * senders + ordered :]
    kept_ref, send_refs = refs[carried], refs[carried + 1 :]
    width = keep_ref.shape[2] - EXTRA
    sums, energy = add_came(keep_ref, came_refs)
    kept = kept_ref.shape[1] // 8
    for array, blocks in enumerate(sums):
        for index, block in enumerate(blocks[:kept]):
            kept_ref[array, 8 * index : 8 * index + 8, :width] = block
    kept_ref[0, :8, width:] = energy
    for index, send_ref in enumerate(send_refs):
        if carried:
            above = refs[0].shape[0]
            send_ref[:above, :] = refs[0][...]
            send_ref = send_ref.at[above:, :]
        first = kept * (index + 1)
        store_coded([send_ref], [block for blocks in sums for block in blocks[first : first + kept]], energy)


def combine(keep, came, sent, carry, after, length):
    _, height, width = keep.shape
    kept = height // (sent + 1)
    parts, senders = len(came[0]), len(came)
    above = sum(array.shape[0] for array in carry)
    keep, *sends = pl.pallas_call(
        functools.partial(combine_kernel, parts, senders, len(carry), len(after)),
        out_shape=(jax.ShapeDtypeStruct((2, kept, width), jnp.float32),)
        + (jax.ShapeDtypeStruct((above + 2 * kept, width), jnp.bfloat16),) * sent,
        in_specs=[WHOLE] * (1 + parts * senders) + [ANYWHERE] * len(after) + [WHOLE] * len(carry),
        out_specs=(WHOLE,) * (1 + sent),
        compiler_params=limit(8),
        cost_estimate=cost(length),
        name="combine",
    )(keep, *[part for parts in came for part in parts], *after, *carry)
    return [[send] for send in sends], keep


def finish_kernel(count, *refs):
    (gradient_ref, log_ref), refs = refs[-2:], refs[:-2]
    came = [ref.at[16 * place : 16 * place + 16, :] for ref, group in zip(refs[-len(GROUPS) :], GROUPS) for place in range(len(group))]
    keep_refs = refs[: -len(GROUPS)]
    row = 0
    for piece, keep_ref in enumerate(keep_refs):
        (gradient, log), energy = add_came(keep_ref, [[came[piece]]])
        correction = 2.0 * (energy[:, :1] / count - OFFSET)
        for block in range(len(log)):
            log_mean = log[block] / count
            gradient_ref[row : row + 8, :] = gradient[block] / count - correction * log_mean
            log_ref[row : row + 8, :] = log_mean
            row += 8


def finish(keeps, came, count):
    _, rows, width = keeps[0].shape
    out = jax.ShapeDtypeStruct((rows * len(keeps), width - EXTRA), jnp.float32)
    return pl.pallas_call(
        functools.partial(finish_kernel, count),
        out_shape=(out, out),
        in_specs=[WHOLE] * (len(keeps) + len(came)),
        out_specs=(WHOLE, WHOLE),
        compiler_params=limit(8),
        cost_estimate=cost(0.1),
        name="finish",
    )(*keeps, *came)


def pieced_body(pieces, tile, inverse_rows, kinetic_rows, virt_values, virt_laplacians, local_energy):
    count = lax.axis_size("walk")
    stages = stage_masks(count)
    me = lax.axis_index("walk").astype(jnp.int32).reshape(1)
    virt = lax.axis_index("virt").astype(jnp.int32).reshape(1)
    occupied, depth = inverse_rows.shape[1:]
    by_dest = (count, occupied // count, depth)
    inverse, kinetic = inverse_rows.reshape(by_dest), kinetic_rows.reshape(by_dest)
    rows = occupied // (count * pieces)

    inverse, kinetic, values, laplacians = (
        pltpu.with_memory_space_constraint(array, pltpu.HBM)
        for array in (inverse, kinetic, virt_values[0], virt_laplacians[0])
    )
    mine = [part for group in range(pieces // 2) for part in cut(inverse, kinetic, group)]
    theirs = [swap(part, "virt", 1) for part in mine]
    near, values, laplacians = near_product(virt, me, local_energy, inverse, kinetic, values, laplacians, mine[2:])

    keep, first, came = {}, {}, []
    late, carry = [], ()
    for turn in range(pieces + 1):
        if turn < pieces:
            after = [keep[turn - 1]] if turn else []
            send, kept = far_product(
                virt, me, local_energy, theirs[turn], near, turn * rows, values, laplacians, tile, stages, 1 if turn else 2, after, FAR[turn]
            )
            first[turn] = [[swap(part, "walk", mask) for part in parts] for parts, mask in zip(send, partners(stages[0]))]
        if turn:
            piece = turn - 1
            sends, keep[piece] = combine(keep[piece], second, len(partners(stages[2])), carry, came if turn == pieces - 1 else [], BESIDE)
            carry = tuple(sends[0])
            if any(piece == group[-1] for group in GROUPS):
                came.append(swap(carry[0], "walk", stages[2][0]))
                carry = ()
        if turn < pieces:
            after = ([keep[turn - 1]] if turn else [])
            sends, keep[turn] = combine(kept, first[turn], len(partners(stages[1])), (), after, 0.1)
            second = [
                [swap(part, "walk", mask) for part in parts]
                for parts, mask in reversed(list(zip(sends, partners(stages[1]))))
            ]
    return finish([keep[piece] for piece in range(pieces)], came, count)


def solution(mesh):
    placed = (
        P("walk", None, "virt"),
        P("walk", None, "virt"),
        P("walk", None, "virt"),
        P("walk", None, "virt"),
        P("walk"),
    )

    def body(inverse_rows, kinetic_rows, virt_values, virt_laplacians, local_energy):
        count = mesh.shape["walk"]
        walkers, occupied, depth = inverse_rows.shape
        width = virt_values.shape[2]
        tile = 512
        fits = (
            walkers == 1
            and mesh.shape["virt"] == 2
            and count == 16
            and count >= 4
            and occupied == count * PIECES * 8
            and depth % 256 == 0
            and width % tile == 0
        )
        form = functools.partial(pieced_body, PIECES, tile) if fits else general_body
        return form(inverse_rows, kinetic_rows, virt_values, virt_laplacians, local_energy)

    return jax.shard_map(
        body,
        mesh=mesh,
        in_specs=placed,
        out_specs=(P("walk", "virt"), P("walk", "virt")),
        check_vma=False,
    )
```

```python
import functools

import jax
import jax.numpy as jnp
from jax import lax
from jax.experimental import pallas as pl
from jax.experimental.pallas import tpu as pltpu
from jax.sharding import PartitionSpec as P

PIECES = 4
UNITS = ((0,), (1, 2), (3,))
SPLIT = (2, 1, 1, 1)
BESIDE = 6
FAR = (0.1, 0.1, 0.1, 0.1)
def product(left, right):
    return jnp.einsum("woe,wev->wov", left, right, preferred_element_type=jnp.float32)


def gradient_terms(log_grad, kin_part, weights):
    kin_grad = -0.5 * kin_part
    weighted = jnp.sum(weights[:, None, None] * log_grad + kin_grad, axis=0)
    return (weighted, jnp.sum(log_grad, axis=0))


def general_body(inverse_rows, kinetic_rows, virt_values, virt_laplacians, local_energy):
    walk_count = lax.axis_size("walk")
    walker_count = walk_count * local_energy.shape[0]
    energy_sum = lax.psum(jnp.sum(local_energy), "walk")
    average = energy_sum / walker_count
    weights = 2.0 * (local_energy - average)
    inverse_all, kinetic_all = (
        lax.all_gather(inverse_rows, "virt", axis=2, tiled=True),
        lax.all_gather(kinetic_rows, "virt", axis=2, tiled=True),
    )
    log_grad = product(inverse_all, virt_values)
    kin_part = product(inverse_all, virt_laplacians) - product(kinetic_all, virt_values)
    weighted, log_sum = gradient_terms(log_grad, kin_part, weights)
    summed = (
        lax.psum_scatter(weighted, "walk", scatter_dimension=0, tiled=True),
        lax.psum_scatter(log_sum, "walk", scatter_dimension=0, tiled=True),
    )
    gradient_part, log_part = (summed[0], summed[1])
    return (gradient_part / walker_count, log_part / walker_count)


SPAN = 248.0
EXTRA = 128
PART = EXTRA // 4
OFFSET = 3.1
TINY = 1e-30
MIB = 1024 * 1024


def stage_masks(count):
    bits = [1 << bit for bit in range(count.bit_length() - 1)]
    if len(bits) < 3:
        return [[bit] for bit in bits]
    return [bits[:1], bits[1:3]] + [[bit] for bit in bits[3:]]


def place_weights(stages):
    order = [mask for stage in stages for mask in stage]
    weights = [0] * len(order)
    for index, mask in enumerate(order):
        weights[mask.bit_length() - 1] = 1 << (len(order) - 1 - index)
    return weights


def partners(stage):
    if len(stage) == 1:
        return list(stage)
    first, second = stage
    return [second, first, first ^ second]


def swap(array, axis, mask):
    pairs = [(source, source ^ mask) for source in range(lax.axis_size(axis))]
    return lax.ppermute(array, axis, pairs)


def encode(rows):
    magnitude = jnp.abs(rows)
    largest = jnp.maximum(jnp.max(magnitude, axis=-1, keepdims=True), TINY)
    scale = (largest * (1.0 + 2.0**-7)).astype(jnp.bfloat16).astype(jnp.float32)
    code = jnp.exp2(magnitude * (SPAN / scale) - SPAN / 2)
    return jnp.where(rows < 0, -code, code).astype(jnp.bfloat16), scale


def decode(coded):
    width = coded.shape[1] - EXTRA
    code = coded[:, :width].astype(jnp.float32)
    scale = coded[:, width : width + 1].astype(jnp.float32)
    magnitude = (jnp.log2(jnp.abs(code)) + SPAN / 2) * (scale / SPAN)
    return jnp.where(code < 0, -magnitude, magnitude)


def store_coded(send_refs, blocks, energy):
    width = send_refs[0].shape[1] - EXTRA
    each = send_refs[0].shape[0]
    f32, bf16 = jnp.float32, jnp.bfloat16
    energy = jnp.concatenate([energy, energy], axis=0)
    high = energy.astype(bf16).astype(f32)
    middle = (energy - high).astype(bf16).astype(f32)
    low = energy - high - middle
    lane = lax.broadcasted_iota(jnp.int32, energy.shape, 1)
    terms = jnp.where(lane < 2 * PART, high, jnp.where(lane < 3 * PART, middle, low))
    for pair in range(len(blocks) // 2):
        code, scale = encode(jnp.concatenate(blocks[2 * pair : 2 * pair + 2], axis=0))
        send_ref = send_refs[16 * pair // each]
        target = slice(16 * pair % each, 16 * pair % each + 16)
        send_ref[target, :width] = code
        send_ref[target, width:] = jnp.where(lane < PART, scale, terms).astype(bf16)


def add_came(keep_ref, came_refs):
    arrays, height, width = keep_ref.shape
    width -= EXTRA
    per = height // 8
    sums = [keep_ref[index // per, 8 * (index % per) : 8 * (index % per) + 8, :width] for index in range(arrays * per)]
    energy = keep_ref[0, :8, width:]
    for parts in came_refs:
        index = 0
        for part in parts:
            for row in range(0, part.shape[0], 16):
                both = decode(part[row : row + 16, :])
                sums[index] += both[:8]
                sums[index + 1] += both[8:]
                index += 2
        terms = parts[0][:16, width:].astype(jnp.float32)[:8]
        for term in range(1, 4):
            energy += terms[:, term * PART : term * PART + 1]
    return [sums[array * per : (array + 1) * per] for array in range(arrays)], energy


def limit(mib):
    return pltpu.CompilerParams(vmem_limit_bytes=mib * MIB)


def cost(microseconds):
    return pl.CostEstimate(flops=int(microseconds * 1.1e9), bytes_accessed=0, transcendentals=0)


WHOLE = pl.BlockSpec(memory_space=pltpu.VMEM)
SCALAR = pl.BlockSpec(memory_space=pltpu.SMEM)
ANYWHERE = pl.BlockSpec(memory_space=pl.ANY)
HELD = pl.BlockSpec(memory_space=pltpu.HBM)
HELD = pl.BlockSpec(memory_space=pltpu.HBM)


def cut_kernel(inverse_ref, kinetic_ref, *out_refs):
    count = inverse_ref.shape[0]
    for array, ref in enumerate((inverse_ref, kinetic_ref)):
        for dest in range(0, count, 2):
            pair = [ref[dest + other].astype(jnp.float32) for other in range(2)]
            for index, out_ref in enumerate(out_refs):
                rows = jnp.concatenate([block[8 * index : 8 * index + 8] for block in pair], axis=0)
                out_ref[array, 8 * dest : 8 * dest + 16, :] = rows.astype(jnp.bfloat16)


def cut(inverse, kinetic, group):
    count, _, depth = inverse.shape
    block = pl.BlockSpec((count, 16, depth), lambda step: (0, group, 0))
    out = jax.ShapeDtypeStruct((2, 8 * count, depth), jnp.bfloat16)
    return pl.pallas_call(
        cut_kernel,
        out_shape=(out, out),
        grid=(1,),
        in_specs=[block, block],
        out_specs=(pl.BlockSpec(out.shape, lambda step: (0, 0, 0)),) * 2,
        compiler_params=limit(12),
        cost_estimate=cost(0.1),
        name="cut",
    )(inverse, kinetic)


def near_kernel(chunk, tile, virt_ref, me_ref, energy_ref, inverse_ref, kinetic_ref, values_ref, laps_ref, *rest):
    out_ref, far_values, far_laps, near_values, near_laps, own_inverse, own_kinetic, sems = rest[-8:]
    count, per, depth = inverse_ref.shape
    height = count * per
    width = out_ref.shape[3]
    f32 = jnp.float32
    own = pl.ds(pl.multiple_of(virt_ref[0] * depth, depth), depth)
    other = pl.ds(pl.multiple_of((1 - virt_ref[0]) * depth, depth), depth)
    chunks = width // chunk

    copies = []
    for index in range(chunks):
        columns = pl.ds(index * chunk, chunk)
        copies.append([
            pltpu.make_async_copy(table.at[own, columns], held.at[:, columns], sems.at[index, which])
            for which, (table, held) in enumerate(((values_ref, near_values), (laps_ref, near_laps)))
        ])
    last = [
        pltpu.make_async_copy(table.at[other, :], held, sems.at[chunks, which])
        for which, (table, held) in enumerate(((values_ref, far_values), (laps_ref, far_laps)))
    ]
    first = [
        pltpu.make_async_copy(rows, held, sems.at[chunks + 1, which])
        for which, (rows, held) in enumerate(((inverse_ref, own_inverse), (kinetic_ref, own_kinetic)))
    ]
    for copy in first + sum(copies, []) + last:
        copy.start()
    for copy in first:
        copy.wait()
    inverse = own_inverse[...].reshape(height, depth)
    kinetic = own_kinetic[...].reshape(height, depth)
    for index in range(chunks):
        for copy in copies[index]:
            copy.wait()

        @pl.loop(index * chunk // tile, (index + 1) * chunk // tile)
        def _(step):
            columns = pl.ds(pl.multiple_of(step * tile, tile), tile)
            values, laps = near_values[:, columns], near_laps[:, columns]
            out_ref[1, :, :, columns] = jnp.dot(inverse, values, preferred_element_type=f32).reshape(count, per, tile)
            rest = jnp.dot(kinetic, values, preferred_element_type=f32)
            rest -= jnp.dot(inverse, laps, preferred_element_type=f32)
            out_ref[0, :, :, columns] = (0.5 * rest).reshape(count, per, tile)

    for copy in last:
        copy.wait()


def near_product(virt, me, energy, inverse, kinetic, values, laplacians, after):
    count, per, depth = inverse.shape
    width = values.shape[1]
    chunk, tile = 512, 256
    table = pltpu.VMEM((depth, width), jnp.bfloat16)
    own = pltpu.VMEM((count, per, depth), jnp.bfloat16)
    return pl.pallas_call(
        functools.partial(near_kernel, chunk, tile),
        out_shape=(jax.ShapeDtypeStruct((2, count, per, width), jnp.float32), table, table),
        in_specs=[SCALAR, SCALAR, SCALAR, HELD, HELD, HELD, HELD] + [ANYWHERE] * len(after),
        out_specs=(WHOLE, WHOLE, WHOLE),
        scratch_shapes=[table, table, own, own, pltpu.SemaphoreType.DMA((width // chunk + 2, 2))],
        compiler_params=limit(24),
        cost_estimate=cost(9),
        name="near_product",
    )(virt, me, energy, inverse, kinetic, values, laplacians, *after)


def far_kernel(weights, count, tile, first, split, virt_ref, me_ref, energy_ref, far_ref, near_ref, values_ref, laps_ref, *rest):
    send_refs, (keep_ref, place_ref) = rest[-split - 2 : -2], rest[-2:]
    _, height, depth = far_ref.shape
    width = near_ref.shape[3]
    rows = height // count
    half = height // 2
    f32 = jnp.float32
    scale = 2.0 * (energy_ref[0] - OFFSET)

    @pl.loop(0, width // tile)
    def _(index):
        columns = pl.ds(pl.multiple_of(index * tile, tile), tile)
        near = near_ref[:, :, first : first + rows, columns].reshape(2, height, tile)
        both = jnp.dot(far_ref[...].reshape(2 * height, depth), values_ref[:, columns], preferred_element_type=f32)
        laps = jnp.dot(far_ref[0], laps_ref[:, columns], preferred_element_type=f32)
        log = both[:height] + near[1]
        weighted = scale * log + (0.5 * (both[height:] - laps) + near[0])
        for dest in range(count):
            difference = dest ^ me_ref[0]
            place = 0
            for bit, weight in enumerate(weights):
                place = place ^ (((difference >> bit) & 1) * weight)
            target = pl.ds(pl.multiple_of(place * rows, rows), rows)
            source = slice(dest * rows, (dest + 1) * rows)
            place_ref[0, target, columns] = weighted[source]
            place_ref[1, target, columns] = log[source]

    energy = jnp.full((8, EXTRA), energy_ref[0], f32)
    keep_ref[:, :, :width] = place_ref[:, :half]
    keep_ref[0, :8, width:] = energy
    blocks = [place_ref[array, row : row + 8, :] for array in range(2) for row in range(half, height, 8)]
    store_coded(send_refs, blocks, energy)


def far_product(virt, me, energy, theirs, near, first, values, laplacians, tile, stages, split, after, length):
    _, height, depth = theirs.shape
    width = values.shape[1]
    half = height // 2
    count = 1 << sum(len(stage) for stage in stages)
    *sends, keep = pl.pallas_call(
        functools.partial(far_kernel, place_weights(stages), count, tile, first, split),
        out_shape=(jax.ShapeDtypeStruct((2 * half // split, width + EXTRA), jnp.bfloat16),) * split
        + (jax.ShapeDtypeStruct((2, half, width + EXTRA), jnp.float32),),
        in_specs=[SCALAR, SCALAR, SCALAR, WHOLE, WHOLE, WHOLE, WHOLE] + [ANYWHERE] * len(after),
        out_specs=(WHOLE,) * (split + 1),
        scratch_shapes=[pltpu.VMEM((2, height, width), jnp.float32)],
        compiler_params=limit(24),
        cost_estimate=cost(length),
        name="far_product",
    )(virt, me, energy, theirs, near, values, laplacians, *after)
    return [sends], keep


def combine_kernel(layout, ordered, *refs):
    count = len(layout)
    keep_refs, refs = refs[:count], refs[count:]
    came = []
    for parts in layout:
        came.append([])
        for index, first, last in parts:
            came[-1].append([refs[position].at[first:last, :] for position in index])
    inputs = 1 + max(position for parts in layout for index, _, _ in parts for position in index)
    refs = refs[inputs + ordered :]
    kept_refs, send_refs = refs[:count], refs[count:]
    width = keep_refs[0].shape[2] - EXTRA
    for piece, (keep_ref, kept_ref) in enumerate(zip(keep_refs, kept_refs)):
        sums, energy = add_came(keep_ref, came[piece])
        kept = kept_ref.shape[1] // 8
        for array, blocks in enumerate(sums):
            for index, block in enumerate(blocks[:kept]):
                kept_ref[array, 8 * index : 8 * index + 8, :width] = block
        kept_ref[0, :8, width:] = energy
        rows = slice(16 * kept * piece, 16 * kept * (piece + 1))
        for index, send_ref in enumerate(send_refs):
            first = kept * (index + 1)
            store_coded([send_ref.at[rows, :]], [block for blocks in sums for block in blocks[first : first + kept]], energy)


def combine(keeps, came, layout, sent, after, length):
    _, height, width = keeps[0].shape
    kept = height // (sent + 1)
    count = len(keeps)
    outs = pl.pallas_call(
        functools.partial(combine_kernel, layout, len(after)),
        out_shape=(jax.ShapeDtypeStruct((2, kept, width), jnp.float32),) * count
        + (jax.ShapeDtypeStruct((2 * kept * count, width), jnp.bfloat16),) * sent,
        in_specs=[WHOLE] * (count + len(came)) + [ANYWHERE] * len(after),
        out_specs=(WHOLE,) * (count + sent),
        compiler_params=limit(10),
        cost_estimate=cost(length),
        name="combine",
    )(*keeps, *came, *after)
    return outs[count:], outs[:count]


def first_layout(count, split, rows):
    return tuple(((tuple(range(piece * split, piece * split + split)), 0, rows),) for piece in range(count))


def joint_layout(count, senders, rows):
    return tuple(
        tuple(((sender,), piece * rows, piece * rows + rows) for sender in range(senders)) for piece in range(count)
    )


def outputs_of(keep_ref, came, count):
    (gradient, log), energy = add_came(keep_ref, came)
    correction = 2.0 * (energy[:, :1] / count - OFFSET)
    log = [block / count for block in log]
    return [block / count - correction * mean for block, mean in zip(gradient, log)], log


def share_kernel(count, ordered, *refs):
    out_ref, row = refs[-1], 0
    for keep_ref in refs[: -1 - ordered]:
        for gradient, log in zip(*outputs_of(keep_ref, [], count)):
            out_ref[0, row : row + 8, :] = gradient
            out_ref[1, row : row + 8, :] = log
            row += 8


def share(keeps, after, count):
    _, rows, width = keeps[0].shape
    return pl.pallas_call(
        functools.partial(share_kernel, count, len(after)),
        out_shape=jax.ShapeDtypeStruct((2, rows * len(keeps), width - EXTRA), jnp.float32),
        in_specs=[WHOLE] * len(keeps) + [ANYWHERE] * len(after),
        out_specs=WHOLE,
        compiler_params=limit(8),
        cost_estimate=cost(BESIDE),
        name="share",
    )(*keeps, *after)


def finish_kernel(count, ready_ref, *refs):
    (gradient_ref, log_ref), refs = refs[-2:], refs[:-2]
    later = UNITS[1:]
    came = []
    for ref, group in zip(refs[-len(later) :], later):
        came += [ref.at[16 * place : 16 * place + 16, :] for place in range(len(group))]
    row = ready_ref.shape[1]
    gradient_ref[:row, :] = ready_ref[0]
    log_ref[:row, :] = ready_ref[1]
    for keep_ref, part in zip(refs[: -len(later)], came):
        for gradient, log in zip(*outputs_of(keep_ref, [[part]], count)):
            gradient_ref[row : row + 8, :] = gradient
            log_ref[row : row + 8, :] = log
            row += 8


def finish(ready, keeps, came, count):
    _, rows, width = keeps[0].shape
    out = jax.ShapeDtypeStruct((ready.shape[1] + rows * len(keeps), width - EXTRA), jnp.float32)
    return pl.pallas_call(
        functools.partial(finish_kernel, count),
        out_shape=(out, out),
        in_specs=[WHOLE] * (1 + len(keeps) + len(came)),
        out_specs=(WHOLE, WHOLE),
        compiler_params=limit(8),
        cost_estimate=cost(0.1),
        name="finish",
    )(ready, *keeps, *came)


def second_sums(group, keep, came, sent, stages, after):
    layout = joint_layout(len(group), len(sent), sent[0].shape[0] // len(group))
    sends, keeps = combine([keep[piece] for piece in group], sent, layout, 1, after, 0.1)
    keep = keep | dict(zip(group, keeps))
    return keep, came + [swap(sends[0], "walk", stages[2][0])], [keeps[0]]


def pieced_body(pieces, tile, inverse_rows, kinetic_rows, virt_values, virt_laplacians, local_energy):
    count = lax.axis_size("walk")
    stages = stage_masks(count)
    me = lax.axis_index("walk").astype(jnp.int32).reshape(1)
    virt = lax.axis_index("virt").astype(jnp.int32).reshape(1)
    occupied, depth = inverse_rows.shape[1:]
    by_dest = (count, occupied // count, depth)
    inverse, kinetic = inverse_rows.reshape(by_dest), kinetic_rows.reshape(by_dest)
    rows = occupied // (count * pieces)

    inverse, kinetic, values, laplacians = (
        pltpu.with_memory_space_constraint(array, pltpu.HBM)
        for array in (inverse, kinetic, virt_values[0], virt_laplacians[0])
    )
    mine = [part for group in range(pieces // 2) for part in cut(inverse, kinetic, group)]
    theirs = [swap(part, "virt", 1) for part in mine[:2]]
    near, values, laplacians = near_product(virt, me, local_energy, inverse, kinetic, values, laplacians, mine[2:])

    second = partners(stages[1])
    kept, first, keep, came = {}, {}, {}, []
    unit, sent, last = 0, (), []
    for turn in range(pieces):
        send, kept[turn] = far_product(
            virt, me, local_energy, theirs[turn], near, turn * rows, values, laplacians, tile, stages, SPLIT[turn], last, FAR[turn]
        )
        if turn + 2 < pieces:
            part, kept[turn] = lax.optimization_barrier((mine[turn + 2], kept[turn]))
            theirs.append(swap(part, "virt", 1))
        first[turn] = [swap(part, "walk", stages[0][0]) for part in send[0]]
        last = [kept[turn]]
        if sent and turn < pieces - 1:
            keep, came, last = second_sums(UNITS[unit - 1], keep, came, sent, stages, last)
            sent = ()
        group = UNITS[unit]
        if turn == pieces - 1:
            ready = share([keep[piece] for piece in UNITS[0]], last, count)
            last = [ready]
        if turn == pieces - 2:
            early = UNITS[0]
            layout = joint_layout(len(early), 1, came[0].shape[0] // len(early))
            _, keeps = combine([keep[piece] for piece in early], came[:1], layout, 0, last, BESIDE)
            keep, last = keep | dict(zip(early, keeps)), [keeps[0]]
        if turn == group[-1]:
            layout = first_layout(len(group), SPLIT[turn], first[turn][0].shape[0])
            arrays = [part for piece in group for part in first[piece]]
            sends, keeps = combine([kept[piece] for piece in group], arrays, layout, len(second), last, 0.1)
            last = [keeps[0]]
            if turn == pieces - 1 and sent:
                keep, came, last = second_sums(UNITS[unit - 1], keep, came, sent, stages, last)
            keep.update(zip(group, keeps))
            sent = [swap(part, "walk", mask) for part, mask in reversed(list(zip(sends, second)))]
            unit += 1
    keep, came, last = second_sums(UNITS[-1], keep, came, sent, stages, last)
    return finish(ready, [keep[piece] for unit in UNITS[1:] for piece in unit], came[1:], count)


def solution(mesh):
    placed = (
        P("walk", None, "virt"),
        P("walk", None, "virt"),
        P("walk", None, "virt"),
        P("walk", None, "virt"),
        P("walk"),
    )

    def body(inverse_rows, kinetic_rows, virt_values, virt_laplacians, local_energy):
        count = mesh.shape["walk"]
        walkers, occupied, depth = inverse_rows.shape
        width = virt_values.shape[2]
        tile = 512
        fits = (
            walkers == 1
            and mesh.shape["virt"] == 2
            and count == 16
            and count >= 4
            and occupied == count * PIECES * 8
            and depth % 256 == 0
            and width % tile == 0
        )
        form = functools.partial(pieced_body, PIECES, tile) if fits else general_body
        return form(inverse_rows, kinetic_rows, virt_values, virt_laplacians, local_energy)

    return jax.shard_map(
        body,
        mesh=mesh,
        in_specs=placed,
        out_specs=(P("walk", "virt"), P("walk", "virt")),
        check_vma=False,
    )
```

```python
import functools

import jax
import jax.numpy as jnp
from jax import lax
from jax.experimental import pallas as pl
from jax.experimental.pallas import tpu as pltpu
from jax.sharding import PartitionSpec as P

PIECES = 4
UNITS = ((0,), (1, 2), (3,))
SPLIT = (2, 1, 1, 1)
BESIDE = 6
FAR = (0.1, 0.1, 1.0, 0.1)


def product(left, right):
    return jnp.einsum("woe,wev->wov", left, right, preferred_element_type=jnp.float32)


def gradient_terms(log_grad, kin_part, weights):
    kin_grad = -0.5 * kin_part
    weighted = jnp.sum(weights[:, None, None] * log_grad + kin_grad, axis=0)
    return (weighted, jnp.sum(log_grad, axis=0))


def general_body(inverse_rows, kinetic_rows, virt_values, virt_laplacians, local_energy):
    walk_count = lax.axis_size("walk")
    walker_count = walk_count * local_energy.shape[0]
    energy_sum = lax.psum(jnp.sum(local_energy), "walk")
    average = energy_sum / walker_count
    weights = 2.0 * (local_energy - average)
    inverse_all, kinetic_all = (
        lax.all_gather(inverse_rows, "virt", axis=2, tiled=True),
        lax.all_gather(kinetic_rows, "virt", axis=2, tiled=True),
    )
    log_grad = product(inverse_all, virt_values)
    kin_part = product(inverse_all, virt_laplacians) - product(kinetic_all, virt_values)
    weighted, log_sum = gradient_terms(log_grad, kin_part, weights)
    summed = (
        lax.psum_scatter(weighted, "walk", scatter_dimension=0, tiled=True),
        lax.psum_scatter(log_sum, "walk", scatter_dimension=0, tiled=True),
    )
    gradient_part, log_part = (summed[0], summed[1])
    return (gradient_part / walker_count, log_part / walker_count)


SPAN = 248.0
EXTRA = 128
PART = EXTRA // 4
OFFSET = 3.1
TINY = 1e-30
MIB = 1024 * 1024


def stage_masks(count):
    bits = [1 << bit for bit in range(count.bit_length() - 1)]
    if len(bits) < 3:
        return [[bit] for bit in bits]
    return [bits[:1], bits[1:3]] + [[bit] for bit in bits[3:]]


def place_weights(stages):
    order = [mask for stage in stages for mask in stage]
    weights = [0] * len(order)
    for index, mask in enumerate(order):
        weights[mask.bit_length() - 1] = 1 << (len(order) - 1 - index)
    return weights


def partners(stage):
    if len(stage) == 1:
        return list(stage)
    first, second = stage
    return [second, first, first ^ second]


def swap(array, axis, mask):
    pairs = [(source, source ^ mask) for source in range(lax.axis_size(axis))]
    return lax.ppermute(array, axis, pairs)


def encode(rows):
    magnitude = jnp.abs(rows)
    largest = jnp.maximum(jnp.max(magnitude, axis=-1, keepdims=True), TINY)
    scale = (largest * (1.0 + 2.0**-7)).astype(jnp.bfloat16).astype(jnp.float32)
    code = jnp.exp2(magnitude * (SPAN / scale) - SPAN / 2)
    return jnp.where(rows < 0, -code, code).astype(jnp.bfloat16), scale


def decode(coded):
    width = coded.shape[1] - EXTRA
    code = coded[:, :width].astype(jnp.float32)
    scale = coded[:, width : width + 1].astype(jnp.float32)
    magnitude = (jnp.log2(jnp.abs(code)) + SPAN / 2) * (scale / SPAN)
    return jnp.where(code < 0, -magnitude, magnitude)


def store_coded(send_refs, blocks, energy):
    width = send_refs[0].shape[1] - EXTRA
    each = send_refs[0].shape[0]
    f32, bf16 = jnp.float32, jnp.bfloat16
    energy = jnp.concatenate([energy, energy], axis=0)
    high = energy.astype(bf16).astype(f32)
    middle = (energy - high).astype(bf16).astype(f32)
    low = energy - high - middle
    lane = lax.broadcasted_iota(jnp.int32, energy.shape, 1)
    terms = jnp.where(lane < 2 * PART, high, jnp.where(lane < 3 * PART, middle, low))
    for pair in range(len(blocks) // 2):
        code, scale = encode(jnp.concatenate(blocks[2 * pair : 2 * pair + 2], axis=0))
        send_ref = send_refs[16 * pair // each]
        target = slice(16 * pair % each, 16 * pair % each + 16)
        send_ref[target, :width] = code
        send_ref[target, width:] = jnp.where(lane < PART, scale, terms).astype(bf16)


def add_came(keep_ref, came_refs):
    arrays, height, width = keep_ref.shape
    width -= EXTRA
    per = height // 8
    sums = [keep_ref[index // per, 8 * (index % per) : 8 * (index % per) + 8, :width] for index in range(arrays * per)]
    energy = keep_ref[0, :8, width:]
    for parts in came_refs:
        index = 0
        for part in parts:
            for row in range(0, part.shape[0], 16):
                both = decode(part[row : row + 16, :])
                sums[index] += both[:8]
                sums[index + 1] += both[8:]
                index += 2
        terms = parts[0][:16, width:].astype(jnp.float32)[:8]
        for term in range(1, 4):
            energy += terms[:, term * PART : term * PART + 1]
    return [sums[array * per : (array + 1) * per] for array in range(arrays)], energy


def limit(mib):
    return pltpu.CompilerParams(vmem_limit_bytes=mib * MIB)


def cost(microseconds):
    return pl.CostEstimate(flops=int(microseconds * 1.1e9), bytes_accessed=0, transcendentals=0)


WHOLE = pl.BlockSpec(memory_space=pltpu.VMEM)
SCALAR = pl.BlockSpec(memory_space=pltpu.SMEM)
ANYWHERE = pl.BlockSpec(memory_space=pl.ANY)
HELD = pl.BlockSpec(memory_space=pltpu.HBM)
HELD = pl.BlockSpec(memory_space=pltpu.HBM)


def cut_kernel(inverse_ref, kinetic_ref, *out_refs):
    count = inverse_ref.shape[0]
    for array, ref in enumerate((inverse_ref, kinetic_ref)):
        for dest in range(0, count, 2):
            pair = [ref[dest + other].astype(jnp.float32) for other in range(2)]
            for index, out_ref in enumerate(out_refs):
                rows = jnp.concatenate([block[8 * index : 8 * index + 8] for block in pair], axis=0)
                out_ref[array, 8 * dest : 8 * dest + 16, :] = rows.astype(jnp.bfloat16)


def cut(inverse, kinetic, group):
    count, _, depth = inverse.shape
    block = pl.BlockSpec((count, 16, depth), lambda step: (0, group, 0))
    out = jax.ShapeDtypeStruct((2, 8 * count, depth), jnp.bfloat16)
    return pl.pallas_call(
        cut_kernel,
        out_shape=(out, out),
        grid=(1,),
        in_specs=[block, block],
        out_specs=(pl.BlockSpec(out.shape, lambda step: (0, 0, 0)),) * 2,
        compiler_params=limit(12),
        cost_estimate=cost(0.1),
        name="cut",
    )(inverse, kinetic)


def near_kernel(chunk, tile, virt_ref, me_ref, energy_ref, inverse_ref, kinetic_ref, values_ref, laps_ref, *rest):
    out_ref, far_values, far_laps, near_values, near_laps, own_inverse, own_kinetic, sems = rest[-8:]
    count, per, depth = inverse_ref.shape
    height = count * per
    width = out_ref.shape[3]
    f32 = jnp.float32
    own = pl.ds(pl.multiple_of(virt_ref[0] * depth, depth), depth)
    other = pl.ds(pl.multiple_of((1 - virt_ref[0]) * depth, depth), depth)
    chunks = width // chunk

    copies = []
    for index in range(chunks):
        columns = pl.ds(index * chunk, chunk)
        copies.append([
            pltpu.make_async_copy(table.at[own, columns], held.at[:, columns], sems.at[index, which])
            for which, (table, held) in enumerate(((values_ref, near_values), (laps_ref, near_laps)))
        ])
    last = [
        pltpu.make_async_copy(table.at[other, :], held, sems.at[chunks, which])
        for which, (table, held) in enumerate(((values_ref, far_values), (laps_ref, far_laps)))
    ]
    first = [
        pltpu.make_async_copy(rows, held, sems.at[chunks + 1, which])
        for which, (rows, held) in enumerate(((inverse_ref, own_inverse), (kinetic_ref, own_kinetic)))
    ]
    for copy in first + sum(copies, []) + last:
        copy.start()
    for copy in first:
        copy.wait()
    inverse = own_inverse[...].reshape(height, depth)
    kinetic = own_kinetic[...].reshape(height, depth)
    for index in range(chunks):
        for copy in copies[index]:
            copy.wait()

        @pl.loop(index * chunk // tile, (index + 1) * chunk // tile)
        def _(step):
            columns = pl.ds(pl.multiple_of(step * tile, tile), tile)
            values, laps = near_values[:, columns], near_laps[:, columns]
            out_ref[1, :, :, columns] = jnp.dot(inverse, values, preferred_element_type=f32).reshape(count, per, tile)
            rest = jnp.dot(kinetic, values, preferred_element_type=f32)
            rest -= jnp.dot(inverse, laps, preferred_element_type=f32)
            out_ref[0, :, :, columns] = (0.5 * rest).reshape(count, per, tile)

    for copy in last:
        copy.wait()


def near_product(virt, me, energy, inverse, kinetic, values, laplacians, after):
    count, per, depth = inverse.shape
    width = values.shape[1]
    chunk, tile = 512, 256
    table = pltpu.VMEM((depth, width), jnp.bfloat16)
    own = pltpu.VMEM((count, per, depth), jnp.bfloat16)
    return pl.pallas_call(
        functools.partial(near_kernel, chunk, tile),
        out_shape=(jax.ShapeDtypeStruct((2, count, per, width), jnp.float32), table, table),
        in_specs=[SCALAR, SCALAR, SCALAR, HELD, HELD, HELD, HELD] + [ANYWHERE] * len(after),
        out_specs=(WHOLE, WHOLE, WHOLE),
        scratch_shapes=[table, table, own, own, pltpu.SemaphoreType.DMA((width // chunk + 2, 2))],
        compiler_params=limit(24),
        cost_estimate=cost(9),
        name="near_product",
    )(virt, me, energy, inverse, kinetic, values, laplacians, *after)


def far_kernel(weights, count, tile, first, split, virt_ref, me_ref, energy_ref, far_ref, near_ref, values_ref, laps_ref, *rest):
    send_refs, (keep_ref, place_ref) = rest[-split - 2 : -2], rest[-2:]
    _, height, depth = far_ref.shape
    width = near_ref.shape[3]
    rows = height // count
    half = height // 2
    f32 = jnp.float32
    scale = 2.0 * (energy_ref[0] - OFFSET)

    @pl.loop(0, width // tile)
    def _(index):
        columns = pl.ds(pl.multiple_of(index * tile, tile), tile)
        near = near_ref[:, :, first : first + rows, columns].reshape(2, height, tile)
        both = jnp.dot(far_ref[...].reshape(2 * height, depth), values_ref[:, columns], preferred_element_type=f32)
        laps = jnp.dot(far_ref[0], laps_ref[:, columns], preferred_element_type=f32)
        log = both[:height] + near[1]
        weighted = scale * log + (0.5 * (both[height:] - laps) + near[0])
        for dest in range(count):
            difference = dest ^ me_ref[0]
            place = 0
            for bit, weight in enumerate(weights):
                place = place ^ (((difference >> bit) & 1) * weight)
            target = pl.ds(pl.multiple_of(place * rows, rows), rows)
            source = slice(dest * rows, (dest + 1) * rows)
            place_ref[0, target, columns] = weighted[source]
            place_ref[1, target, columns] = log[source]

    energy = jnp.full((8, EXTRA), energy_ref[0], f32)
    keep_ref[:, :, :width] = place_ref[:, :half]
    keep_ref[0, :8, width:] = energy
    blocks = [place_ref[array, row : row + 8, :] for array in range(2) for row in range(half, height, 8)]
    store_coded(send_refs, blocks, energy)


def far_product(virt, me, energy, theirs, near, first, values, laplacians, tile, stages, split, after, length):
    _, height, depth = theirs.shape
    width = values.shape[1]
    half = height // 2
    count = 1 << sum(len(stage) for stage in stages)
    *sends, keep = pl.pallas_call(
        functools.partial(far_kernel, place_weights(stages), count, tile, first, split),
        out_shape=(jax.ShapeDtypeStruct((2 * half // split, width + EXTRA), jnp.bfloat16),) * split
        + (jax.ShapeDtypeStruct((2, half, width + EXTRA), jnp.float32),),
        in_specs=[SCALAR, SCALAR, SCALAR, WHOLE, WHOLE, WHOLE, WHOLE] + [ANYWHERE] * len(after),
        out_specs=(WHOLE,) * (split + 1),
        scratch_shapes=[pltpu.VMEM((2, height, width), jnp.float32)],
        compiler_params=limit(24),
        cost_estimate=cost(length),
        name="far_product",
    )(virt, me, energy, theirs, near, values, laplacians, *after)
    return [sends], keep


def combine_kernel(layout, ordered, *refs):
    count = len(layout)
    keep_refs, refs = refs[:count], refs[count:]
    came = []
    for parts in layout:
        came.append([])
        for index, first, last in parts:
            came[-1].append([refs[position].at[first:last, :] for position in index])
    inputs = 1 + max(position for parts in layout for index, _, _ in parts for position in index)
    refs = refs[inputs + ordered :]
    kept_refs, send_refs = refs[:count], refs[count:]
    width = keep_refs[0].shape[2] - EXTRA
    for piece, (keep_ref, kept_ref) in enumerate(zip(keep_refs, kept_refs)):
        sums, energy = add_came(keep_ref, came[piece])
        kept = kept_ref.shape[1] // 8
        for array, blocks in enumerate(sums):
            for index, block in enumerate(blocks[:kept]):
                kept_ref[array, 8 * index : 8 * index + 8, :width] = block
        kept_ref[0, :8, width:] = energy
        rows = slice(16 * kept * piece, 16 * kept * (piece + 1))
        for index, send_ref in enumerate(send_refs):
            first = kept * (index + 1)
            store_coded([send_ref.at[rows, :]], [block for blocks in sums for block in blocks[first : first + kept]], energy)


def combine(keeps, came, layout, sent, after, length):
    _, height, width = keeps[0].shape
    kept = height // (sent + 1)
    count = len(keeps)
    outs = pl.pallas_call(
        functools.partial(combine_kernel, layout, len(after)),
        out_shape=(jax.ShapeDtypeStruct((2, kept, width), jnp.float32),) * count
        + (jax.ShapeDtypeStruct((2 * kept * count, width), jnp.bfloat16),) * sent,
        in_specs=[WHOLE] * (count + len(came)) + [ANYWHERE] * len(after),
        out_specs=(WHOLE,) * (count + sent),
        compiler_params=limit(10),
        cost_estimate=cost(length),
        name="combine",
    )(*keeps, *came, *after)
    return outs[count:], outs[:count]


def first_layout(count, split, rows):
    return tuple(((tuple(range(piece * split, piece * split + split)), 0, rows),) for piece in range(count))


def joint_layout(count, senders, rows):
    return tuple(
        tuple(((sender,), piece * rows, piece * rows + rows) for sender in range(senders)) for piece in range(count)
    )


def outputs_of(keep_ref, came, count):
    (gradient, log), energy = add_came(keep_ref, came)
    correction = 2.0 * (energy[:, :1] / count - OFFSET)
    log = [block / count for block in log]
    return [block / count - correction * mean for block, mean in zip(gradient, log)], log


def share_kernel(count, ordered, *refs):
    out_ref, row = refs[-1], 0
    for keep_ref in refs[: -1 - ordered]:
        for gradient, log in zip(*outputs_of(keep_ref, [], count)):
            out_ref[0, row : row + 8, :] = gradient
            out_ref[1, row : row + 8, :] = log
            row += 8


def share(keeps, after, count):
    _, rows, width = keeps[0].shape
    return pl.pallas_call(
        functools.partial(share_kernel, count, len(after)),
        out_shape=jax.ShapeDtypeStruct((2, rows * len(keeps), width - EXTRA), jnp.float32),
        in_specs=[WHOLE] * len(keeps) + [ANYWHERE] * len(after),
        out_specs=WHOLE,
        compiler_params=limit(8),
        cost_estimate=cost(BESIDE),
        name="share",
    )(*keeps, *after)


def finish_kernel(count, ready_ref, *refs):
    (gradient_ref, log_ref), refs = refs[-2:], refs[:-2]
    later = UNITS[1:]
    came = []
    for ref, group in zip(refs[-len(later) :], later):
        came += [ref.at[16 * place : 16 * place + 16, :] for place in range(len(group))]
    row = ready_ref.shape[1]
    gradient_ref[:row, :] = ready_ref[0]
    log_ref[:row, :] = ready_ref[1]
    for keep_ref, part in zip(refs[: -len(later)], came):
        for gradient, log in zip(*outputs_of(keep_ref, [[part]], count)):
            gradient_ref[row : row + 8, :] = gradient
            log_ref[row : row + 8, :] = log
            row += 8


def finish(ready, keeps, came, count):
    _, rows, width = keeps[0].shape
    out = jax.ShapeDtypeStruct((ready.shape[1] + rows * len(keeps), width - EXTRA), jnp.float32)
    return pl.pallas_call(
        functools.partial(finish_kernel, count),
        out_shape=(out, out),
        in_specs=[WHOLE] * (1 + len(keeps) + len(came)),
        out_specs=(WHOLE, WHOLE),
        compiler_params=limit(8),
        cost_estimate=cost(0.1),
        name="finish",
    )(ready, *keeps, *came)


def second_sums(group, keep, came, sent, stages, after):
    layout = joint_layout(len(group), len(sent), sent[0].shape[0] // len(group))
    sends, keeps = combine([keep[piece] for piece in group], sent, layout, 1, after, 0.1)
    keep = keep | dict(zip(group, keeps))
    return keep, came + [swap(sends[0], "walk", stages[2][0])], [keeps[0]]


def pieced_body(pieces, tile, inverse_rows, kinetic_rows, virt_values, virt_laplacians, local_energy):
    count = lax.axis_size("walk")
    stages = stage_masks(count)
    me = lax.axis_index("walk").astype(jnp.int32).reshape(1)
    virt = lax.axis_index("virt").astype(jnp.int32).reshape(1)
    occupied, depth = inverse_rows.shape[1:]
    by_dest = (count, occupied // count, depth)
    inverse, kinetic = inverse_rows.reshape(by_dest), kinetic_rows.reshape(by_dest)
    rows = occupied // (count * pieces)

    inverse, kinetic, values, laplacians = (
        pltpu.with_memory_space_constraint(array, pltpu.HBM)
        for array in (inverse, kinetic, virt_values[0], virt_laplacians[0])
    )
    mine = [part for group in range(pieces // 2) for part in cut(inverse, kinetic, group)]
    theirs = [swap(part, "virt", 1) for part in mine[:2]]
    near, values, laplacians = near_product(virt, me, local_energy, inverse, kinetic, values, laplacians, mine[2:])

    second = partners(stages[1])
    kept, first, keep, came = {}, {}, {}, []
    unit, sent, last = 0, (), []
    for turn in range(pieces):
        send, kept[turn] = far_product(
            virt, me, local_energy, theirs[turn], near, turn * rows, values, laplacians, tile, stages, SPLIT[turn], last, FAR[turn]
        )
        if turn + 2 < pieces:
            part, kept[turn] = lax.optimization_barrier((mine[turn + 2], kept[turn]))
            theirs.append(swap(part, "virt", 1))
        first[turn] = [swap(part, "walk", stages[0][0]) for part in send[0]]
        last = [kept[turn]]
        if sent and turn < pieces - 1:
            keep, came, last = second_sums(UNITS[unit - 1], keep, came, sent, stages, last)
            sent = ()
        group = UNITS[unit]
        if turn == pieces - 1:
            ready = share([keep[piece] for piece in UNITS[0]], last, count)
            last = [ready]
        if turn == pieces - 2:
            early = UNITS[0]
            layout = joint_layout(len(early), 1, came[0].shape[0] // len(early))
            _, keeps = combine([keep[piece] for piece in early], came[:1], layout, 0, last, BESIDE)
            keep, last = keep | dict(zip(early, keeps)), [keeps[0]]
        if turn == group[-1]:
            layout = first_layout(len(group), SPLIT[turn], first[turn][0].shape[0])
            arrays = [part for piece in group for part in first[piece]]
            sends, keeps = combine([kept[piece] for piece in group], arrays, layout, len(second), last, 0.1)
            last = [keeps[0]]
            if turn == pieces - 1 and sent:
                keep, came, last = second_sums(UNITS[unit - 1], keep, came, sent, stages, last)
            keep.update(zip(group, keeps))
            sent = [swap(part, "walk", mask) for part, mask in reversed(list(zip(sends, second)))]
            unit += 1
    keep, came, last = second_sums(UNITS[-1], keep, came, sent, stages, last)
    return finish(ready, [keep[piece] for unit in UNITS[1:] for piece in unit], came[1:], count)


def solution(mesh):
    placed = (
        P("walk", None, "virt"),
        P("walk", None, "virt"),
        P("walk", None, "virt"),
        P("walk", None, "virt"),
        P("walk"),
    )

    def body(inverse_rows, kinetic_rows, virt_values, virt_laplacians, local_energy):
        count = mesh.shape["walk"]
        walkers, occupied, depth = inverse_rows.shape
        width = virt_values.shape[2]
        tile = 512
        fits = (
            walkers == 1
            and mesh.shape["virt"] == 2
            and count == 16
            and count >= 4
            and occupied == count * PIECES * 8
            and depth % 256 == 0
            and width % tile == 0
        )
        form = functools.partial(pieced_body, PIECES, tile) if fits else general_body
        return form(inverse_rows, kinetic_rows, virt_values, virt_laplacians, local_energy)

    return jax.shard_map(
        body,
        mesh=mesh,
        in_specs=placed,
        out_specs=(P("walk", "virt"), P("walk", "virt")),
        check_vma=False,
    )
```

```python
import functools

import jax
import jax.numpy as jnp
from jax import lax
from jax.experimental import pallas as pl
from jax.experimental.pallas import tpu as pltpu
from jax.sharding import PartitionSpec as P

PIECES = 4
GROUPS = ((0,), (1, 2), (3,))
SPLIT = (2, 2, 2, 1)
BESIDE = (0, 2.3, 2.3, 6)
FAR = (0.1, 1.5, 0.1, 1.5)


def product(left, right):
    return jnp.einsum("woe,wev->wov", left, right, preferred_element_type=jnp.float32)


def gradient_terms(log_grad, kin_part, weights):
    kin_grad = -0.5 * kin_part
    weighted = jnp.sum(weights[:, None, None] * log_grad + kin_grad, axis=0)
    return (weighted, jnp.sum(log_grad, axis=0))


def general_body(inverse_rows, kinetic_rows, virt_values, virt_laplacians, local_energy):
    walk_count = lax.axis_size("walk")
    walker_count = walk_count * local_energy.shape[0]
    energy_sum = lax.psum(jnp.sum(local_energy), "walk")
    average = energy_sum / walker_count
    weights = 2.0 * (local_energy - average)
    inverse_all, kinetic_all = (
        lax.all_gather(inverse_rows, "virt", axis=2, tiled=True),
        lax.all_gather(kinetic_rows, "virt", axis=2, tiled=True),
    )
    log_grad = product(inverse_all, virt_values)
    kin_part = product(inverse_all, virt_laplacians) - product(kinetic_all, virt_values)
    weighted, log_sum = gradient_terms(log_grad, kin_part, weights)
    summed = (
        lax.psum_scatter(weighted, "walk", scatter_dimension=0, tiled=True),
        lax.psum_scatter(log_sum, "walk", scatter_dimension=0, tiled=True),
    )
    gradient_part, log_part = (summed[0], summed[1])
    return (gradient_part / walker_count, log_part / walker_count)


SPAN = 248.0
EXTRA = 128
PART = EXTRA // 4
OFFSET = 3.1
TINY = 1e-30
MIB = 1024 * 1024


def stage_masks(count):
    bits = [1 << bit for bit in range(count.bit_length() - 1)]
    if len(bits) < 3:
        return [[bit] for bit in bits]
    return [bits[:1], bits[1:3]] + [[bit] for bit in bits[3:]]


def place_weights(stages):
    order = [mask for stage in stages for mask in stage]
    weights = [0] * len(order)
    for index, mask in enumerate(order):
        weights[mask.bit_length() - 1] = 1 << (len(order) - 1 - index)
    return weights


def partners(stage):
    if len(stage) == 1:
        return list(stage)
    first, second = stage
    return [second, first, first ^ second]


def swap(array, axis, mask):
    pairs = [(source, source ^ mask) for source in range(lax.axis_size(axis))]
    return lax.ppermute(array, axis, pairs)


def encode(rows):
    magnitude = jnp.abs(rows)
    largest = jnp.maximum(jnp.max(magnitude, axis=-1, keepdims=True), TINY)
    scale = (largest * (1.0 + 2.0**-7)).astype(jnp.bfloat16).astype(jnp.float32)
    code = jnp.exp2(magnitude * (SPAN / scale) - SPAN / 2)
    return jnp.where(rows < 0, -code, code).astype(jnp.bfloat16), scale


def decode(coded):
    width = coded.shape[1] - EXTRA
    code = coded[:, :width].astype(jnp.float32)
    scale = coded[:, width : width + 1].astype(jnp.float32)
    magnitude = (jnp.log2(jnp.abs(code)) + SPAN / 2) * (scale / SPAN)
    return jnp.where(code < 0, -magnitude, magnitude)


def store_coded(send_refs, blocks, energy):
    width = send_refs[0].shape[1] - EXTRA
    each = send_refs[0].shape[0]
    f32, bf16 = jnp.float32, jnp.bfloat16
    energy = jnp.concatenate([energy, energy], axis=0)
    high = energy.astype(bf16).astype(f32)
    middle = (energy - high).astype(bf16).astype(f32)
    low = energy - high - middle
    lane = lax.broadcasted_iota(jnp.int32, energy.shape, 1)
    terms = jnp.where(lane < 2 * PART, high, jnp.where(lane < 3 * PART, middle, low))
    for pair in range(len(blocks) // 2):
        code, scale = encode(jnp.concatenate(blocks[2 * pair : 2 * pair + 2], axis=0))
        send_ref = send_refs[16 * pair // each]
        target = slice(16 * pair % each, 16 * pair % each + 16)
        send_ref[target, :width] = code
        send_ref[target, width:] = jnp.where(lane < PART, scale, terms).astype(bf16)


def add_came(keep_ref, came_refs):
    arrays, height, width = keep_ref.shape
    width -= EXTRA
    per = height // 8
    sums = [keep_ref[index // per, 8 * (index % per) : 8 * (index % per) + 8, :width] for index in range(arrays * per)]
    energy = keep_ref[0, :8, width:]
    for parts in came_refs:
        index = 0
        for part in parts:
            for row in range(0, part.shape[0], 16):
                both = decode(part[row : row + 16, :])
                sums[index] += both[:8]
                sums[index + 1] += both[8:]
                index += 2
        terms = parts[0][:16, width:].astype(jnp.float32)[:8]
        for term in range(1, 4):
            energy += terms[:, term * PART : term * PART + 1]
    return [sums[array * per : (array + 1) * per] for array in range(arrays)], energy


def limit(mib):
    return pltpu.CompilerParams(vmem_limit_bytes=mib * MIB)


def cost(microseconds):
    return pl.CostEstimate(flops=int(microseconds * 1.1e9), bytes_accessed=0, transcendentals=0)


WHOLE = pl.BlockSpec(memory_space=pltpu.VMEM)
SCALAR = pl.BlockSpec(memory_space=pltpu.SMEM)
ANYWHERE = pl.BlockSpec(memory_space=pl.ANY)
HELD = pl.BlockSpec(memory_space=pltpu.HBM)
HELD = pl.BlockSpec(memory_space=pltpu.HBM)


def cut_kernel(inverse_ref, kinetic_ref, *out_refs):
    count = inverse_ref.shape[0]
    for array, ref in enumerate((inverse_ref, kinetic_ref)):
        for dest in range(0, count, 2):
            pair = [ref[dest + other].astype(jnp.float32) for other in range(2)]
            for index, out_ref in enumerate(out_refs):
                rows = jnp.concatenate([block[8 * index : 8 * index + 8] for block in pair], axis=0)
                out_ref[array, 8 * dest : 8 * dest + 16, :] = rows.astype(jnp.bfloat16)


def cut(inverse, kinetic, group):
    count, _, depth = inverse.shape
    block = pl.BlockSpec((count, 16, depth), lambda step: (0, group, 0))
    out = jax.ShapeDtypeStruct((2, 8 * count, depth), jnp.bfloat16)
    return pl.pallas_call(
        cut_kernel,
        out_shape=(out, out),
        grid=(1,),
        in_specs=[block, block],
        out_specs=(pl.BlockSpec(out.shape, lambda step: (0, 0, 0)),) * 2,
        compiler_params=limit(12),
        cost_estimate=cost(0.1),
        name="cut",
    )(inverse, kinetic)


def near_kernel(chunk, tile, virt_ref, me_ref, energy_ref, inverse_ref, kinetic_ref, values_ref, laps_ref, *rest):
    out_ref, far_values, far_laps, near_values, near_laps, own_inverse, own_kinetic, sems = rest[-8:]
    count, per, depth = inverse_ref.shape
    height = count * per
    width = out_ref.shape[3]
    f32 = jnp.float32
    own = pl.ds(pl.multiple_of(virt_ref[0] * depth, depth), depth)
    other = pl.ds(pl.multiple_of((1 - virt_ref[0]) * depth, depth), depth)
    chunks = width // chunk

    copies = []
    for index in range(chunks):
        columns = pl.ds(index * chunk, chunk)
        copies.append([
            pltpu.make_async_copy(table.at[own, columns], held.at[:, columns], sems.at[index, which])
            for which, (table, held) in enumerate(((values_ref, near_values), (laps_ref, near_laps)))
        ])
    last = [
        pltpu.make_async_copy(table.at[other, :], held, sems.at[chunks, which])
        for which, (table, held) in enumerate(((values_ref, far_values), (laps_ref, far_laps)))
    ]
    first = [
        pltpu.make_async_copy(rows, held, sems.at[chunks + 1, which])
        for which, (rows, held) in enumerate(((inverse_ref, own_inverse), (kinetic_ref, own_kinetic)))
    ]
    for copy in first + sum(copies, []) + last:
        copy.start()
    for copy in first:
        copy.wait()
    inverse = own_inverse[...].reshape(height, depth)
    kinetic = own_kinetic[...].reshape(height, depth)
    for index in range(chunks):
        for copy in copies[index]:
            copy.wait()

        @pl.loop(index * chunk // tile, (index + 1) * chunk // tile)
        def _(step):
            columns = pl.ds(pl.multiple_of(step * tile, tile), tile)
            values, laps = near_values[:, columns], near_laps[:, columns]
            out_ref[1, :, :, columns] = jnp.dot(inverse, values, preferred_element_type=f32).reshape(count, per, tile)
            rest = jnp.dot(kinetic, values, preferred_element_type=f32)
            rest -= jnp.dot(inverse, laps, preferred_element_type=f32)
            out_ref[0, :, :, columns] = (0.5 * rest).reshape(count, per, tile)

    for copy in last:
        copy.wait()


def near_product(virt, me, energy, inverse, kinetic, values, laplacians, after):
    count, per, depth = inverse.shape
    width = values.shape[1]
    chunk, tile = 512, 256
    table = pltpu.VMEM((depth, width), jnp.bfloat16)
    own = pltpu.VMEM((count, per, depth), jnp.bfloat16)
    return pl.pallas_call(
        functools.partial(near_kernel, chunk, tile),
        out_shape=(jax.ShapeDtypeStruct((2, count, per, width), jnp.float32), table, table),
        in_specs=[SCALAR, SCALAR, SCALAR, HELD, HELD, HELD, HELD] + [ANYWHERE] * len(after),
        out_specs=(WHOLE, WHOLE, WHOLE),
        scratch_shapes=[table, table, own, own, pltpu.SemaphoreType.DMA((width // chunk + 2, 2))],
        compiler_params=limit(24),
        cost_estimate=cost(9),
        name="near_product",
    )(virt, me, energy, inverse, kinetic, values, laplacians, *after)


def far_kernel(weights, count, tile, first, split, virt_ref, me_ref, energy_ref, far_ref, near_ref, values_ref, laps_ref, *rest):
    send_refs, (keep_ref, place_ref) = rest[-split - 2 : -2], rest[-2:]
    _, height, depth = far_ref.shape
    width = near_ref.shape[3]
    rows = height // count
    half = height // 2
    f32 = jnp.float32
    scale = 2.0 * (energy_ref[0] - OFFSET)

    @pl.loop(0, width // tile)
    def _(index):
        columns = pl.ds(pl.multiple_of(index * tile, tile), tile)
        near = near_ref[:, :, first : first + rows, columns].reshape(2, height, tile)
        both = jnp.dot(far_ref[...].reshape(2 * height, depth), values_ref[:, columns], preferred_element_type=f32)
        laps = jnp.dot(far_ref[0], laps_ref[:, columns], preferred_element_type=f32)
        log = both[:height] + near[1]
        weighted = scale * log + (0.5 * (both[height:] - laps) + near[0])
        for dest in range(count):
            difference = dest ^ me_ref[0]
            place = 0
            for bit, weight in enumerate(weights):
                place = place ^ (((difference >> bit) & 1) * weight)
            target = pl.ds(pl.multiple_of(place * rows, rows), rows)
            source = slice(dest * rows, (dest + 1) * rows)
            place_ref[0, target, columns] = weighted[source]
            place_ref[1, target, columns] = log[source]

    energy = jnp.full((8, EXTRA), energy_ref[0], f32)
    keep_ref[:, :, :width] = place_ref[:, :half]
    keep_ref[0, :8, width:] = energy
    blocks = [place_ref[array, row : row + 8, :] for array in range(2) for row in range(half, height, 8)]
    store_coded(send_refs, blocks, energy)


def far_product(virt, me, energy, theirs, near, first, values, laplacians, tile, stages, split, after, length):
    _, height, depth = theirs.shape
    width = values.shape[1]
    half = height // 2
    count = 1 << sum(len(stage) for stage in stages)
    *sends, keep = pl.pallas_call(
        functools.partial(far_kernel, place_weights(stages), count, tile, first, split),
        out_shape=(jax.ShapeDtypeStruct((2 * half // split, width + EXTRA), jnp.bfloat16),) * split
        + (jax.ShapeDtypeStruct((2, half, width + EXTRA), jnp.float32),),
        in_specs=[SCALAR, SCALAR, SCALAR, WHOLE, WHOLE, WHOLE, WHOLE] + [ANYWHERE] * len(after),
        out_specs=(WHOLE,) * (split + 1),
        scratch_shapes=[pltpu.VMEM((2, height, width), jnp.float32)],
        compiler_params=limit(24),
        cost_estimate=cost(length),
        name="far_product",
    )(virt, me, energy, theirs, near, values, laplacians, *after)
    return [sends], keep


def combine_kernel(layout, ordered, carried, *refs):
    count = len(layout)
    keep_refs, refs = refs[:count], refs[count:]
    came = []
    for parts in layout:
        came.append([])
        for index, first, last in parts:
            came[-1].append([refs[position].at[first:last, :] for position in index])
    inputs = 1 + max(position for parts in layout for index, _, _ in parts for position in index)
    refs = refs[inputs + ordered :]
    kept_refs, send_refs = refs[carried : carried + count], refs[carried + count :]
    if carried:
        above = refs[0].shape[0]
        send_refs[0][:above, :] = refs[0][...]
        send_refs = [send_refs[0].at[above:, :]]
    width = keep_refs[0].shape[2] - EXTRA
    for piece, (keep_ref, kept_ref) in enumerate(zip(keep_refs, kept_refs)):
        sums, energy = add_came(keep_ref, came[piece])
        kept = kept_ref.shape[1] // 8
        for array, blocks in enumerate(sums):
            for index, block in enumerate(blocks[:kept]):
                kept_ref[array, 8 * index : 8 * index + 8, :width] = block
        kept_ref[0, :8, width:] = energy
        rows = slice(16 * kept * piece, 16 * kept * (piece + 1))
        for index, send_ref in enumerate(send_refs):
            first = kept * (index + 1)
            store_coded([send_ref.at[rows, :]], [block for blocks in sums for block in blocks[first : first + kept]], energy)


def combine(keeps, came, layout, sent, after, length, carry=()):
    _, height, width = keeps[0].shape
    kept = height // (sent + 1)
    count = len(keeps)
    above = sum(array.shape[0] for array in carry)
    outs = pl.pallas_call(
        functools.partial(combine_kernel, layout, len(after), len(carry)),
        out_shape=(jax.ShapeDtypeStruct((2, kept, width), jnp.float32),) * count
        + (jax.ShapeDtypeStruct((2 * kept * count + above, width), jnp.bfloat16),) * sent,
        in_specs=[WHOLE] * (count + len(came)) + [ANYWHERE] * len(after) + [WHOLE] * len(carry),
        out_specs=(WHOLE,) * (count + sent),
        compiler_params=limit(10),
        cost_estimate=cost(length),
        name="combine",
    )(*keeps, *came, *after, *carry)
    return outs[count:], outs[:count]


def first_layout(count, split, rows):
    return tuple(((tuple(range(piece * split, piece * split + split)), 0, rows),) for piece in range(count))


def joint_layout(count, senders, rows):
    return tuple(
        tuple(((sender,), piece * rows, piece * rows + rows) for sender in range(senders)) for piece in range(count)
    )


def outputs_of(keep_ref, came, count):
    (gradient, log), energy = add_came(keep_ref, came)
    correction = 2.0 * (energy[:, :1] / count - OFFSET)
    log = [block / count for block in log]
    return [block / count - correction * mean for block, mean in zip(gradient, log)], log


def share_kernel(count, ordered, *refs):
    out_ref, row = refs[-1], 0
    for keep_ref in refs[: -1 - ordered]:
        for gradient, log in zip(*outputs_of(keep_ref, [], count)):
            out_ref[0, row : row + 8, :] = gradient
            out_ref[1, row : row + 8, :] = log
            row += 8


def share(keeps, after, count):
    _, rows, width = keeps[0].shape
    return pl.pallas_call(
        functools.partial(share_kernel, count, len(after)),
        out_shape=jax.ShapeDtypeStruct((2, rows * len(keeps), width - EXTRA), jnp.float32),
        in_specs=[WHOLE] * len(keeps) + [ANYWHERE] * len(after),
        out_specs=WHOLE,
        compiler_params=limit(8),
        cost_estimate=cost(0.1),
        name="share",
    )(*keeps, *after)


def finish_kernel(count, ready_ref, *refs):
    (gradient_ref, log_ref), refs = refs[-2:], refs[:-2]
    later = GROUPS[1:]
    came = []
    for ref, group in zip(refs[-len(later) :], later):
        came += [ref.at[16 * place : 16 * place + 16, :] for place in range(len(group))]
    row = ready_ref.shape[1]
    gradient_ref[:row, :] = ready_ref[0]
    log_ref[:row, :] = ready_ref[1]
    for keep_ref, part in zip(refs[: -len(later)], came):
        for gradient, log in zip(*outputs_of(keep_ref, [[part]], count)):
            gradient_ref[row : row + 8, :] = gradient
            log_ref[row : row + 8, :] = log
            row += 8


def finish(ready, keeps, came, count):
    _, rows, width = keeps[0].shape
    out = jax.ShapeDtypeStruct((ready.shape[1] + rows * len(keeps), width - EXTRA), jnp.float32)
    return pl.pallas_call(
        functools.partial(finish_kernel, count),
        out_shape=(out, out),
        in_specs=[WHOLE] * (1 + len(keeps) + len(came)),
        out_specs=(WHOLE, WHOLE),
        compiler_params=limit(8),
        cost_estimate=cost(0.1),
        name="finish",
    )(ready, *keeps, *came)


def pieced_body(pieces, tile, inverse_rows, kinetic_rows, virt_values, virt_laplacians, local_energy):
    count = lax.axis_size("walk")
    stages = stage_masks(count)
    me = lax.axis_index("walk").astype(jnp.int32).reshape(1)
    virt = lax.axis_index("virt").astype(jnp.int32).reshape(1)
    occupied, depth = inverse_rows.shape[1:]
    by_dest = (count, occupied // count, depth)
    inverse, kinetic = inverse_rows.reshape(by_dest), kinetic_rows.reshape(by_dest)
    rows = occupied // (count * pieces)

    inverse, kinetic, values, laplacians = (
        pltpu.with_memory_space_constraint(array, pltpu.HBM)
        for array in (inverse, kinetic, virt_values[0], virt_laplacians[0])
    )
    mine = [part for group in range(pieces // 2) for part in cut(inverse, kinetic, group)]
    theirs = [swap(part, "virt", 1) for part in mine[:2]]
    near, values, laplacians = near_product(virt, me, local_energy, inverse, kinetic, values, laplacians, mine[2:])

    second = partners(stages[1])
    keep, came, carry, sent, last = {}, [], (), (), []

    def second_sums(piece, carry, after, length):
        layout = joint_layout(1, len(sent), sent[0].shape[0])
        (send,), (keep[piece],) = combine([keep[piece]], sent, layout, 1, after, length, carry)
        group = next(group for group in GROUPS if piece in group)
        if piece < group[-1]:
            return (send,), [keep[piece]]
        held.append(send)
        return (), [keep[piece]]

    held = []
    for turn in range(pieces):
        final = turn == pieces - 1
        send, kept = far_product(
            virt, me, local_energy, theirs[turn], near, turn * rows, values, laplacians, tile, stages, SPLIT[turn], last, FAR[turn]
        )
        if turn + 2 < pieces:
            part, kept = lax.optimization_barrier((mine[turn + 2], kept))
            theirs.append(swap(part, "virt", 1))
        if held and turn == pieces - 2:
            held[0], kept = lax.optimization_barrier((held[0], kept))
            came.append(swap(held.pop(), "walk", stages[2][0]))
        first = [swap(part, "walk", stages[0][0]) for part in send[0]]
        last = [kept]
        if final:
            layout = joint_layout(1, 1, came[0].shape[0])
            _, (keep[0],) = combine([keep[0]], came[:1], layout, 0, last, BESIDE[turn])
            last = [keep[0]]
        elif turn:
            carry, last = second_sums(turn - 1, carry, last, BESIDE[turn])
        layout = first_layout(1, SPLIT[turn], first[0].shape[0])
        sends, (keep[turn],) = combine([kept], first, layout, len(second), last, 0.1)
        last = [keep[turn]]
        if final:
            carry, last = second_sums(turn - 1, carry, last, 0.1)
            came.append(swap(held.pop(), "walk", stages[2][0]))
        sent = [swap(part, "walk", mask) for part, mask in reversed(list(zip(sends, second)))]
    second_sums(pieces - 1, (), last, 0.1)
    came.append(swap(held.pop(), "walk", stages[2][0]))
    ready = share([keep[piece] for piece in GROUPS[0]], last, count)
    return finish(ready, [keep[piece] for group in GROUPS[1:] for piece in group], came[1:], count)


def solution(mesh):
    placed = (
        P("walk", None, "virt"),
        P("walk", None, "virt"),
        P("walk", None, "virt"),
        P("walk", None, "virt"),
        P("walk"),
    )

    def body(inverse_rows, kinetic_rows, virt_values, virt_laplacians, local_energy):
        count = mesh.shape["walk"]
        walkers, occupied, depth = inverse_rows.shape
        width = virt_values.shape[2]
        tile = 512
        fits = (
            walkers == 1
            and mesh.shape["virt"] == 2
            and count == 16
            and count >= 4
            and occupied == count * PIECES * 8
            and depth % 256 == 0
            and width % tile == 0
        )
        form = functools.partial(pieced_body, PIECES, tile) if fits else general_body
        return form(inverse_rows, kinetic_rows, virt_values, virt_laplacians, local_energy)

    return jax.shard_map(
        body,
        mesh=mesh,
        in_specs=placed,
        out_specs=(P("walk", "virt"), P("walk", "virt")),
        check_vma=False,
    )
```

```python
import functools

import jax
import jax.numpy as jnp
from jax import lax
from jax.experimental import pallas as pl
from jax.experimental.pallas import tpu as pltpu
from jax.sharding import PartitionSpec as P

PIECES = 4
GROUPS = ((0,), (1, 2), (3,))
SPLIT = (2, 2, 1, 1)
BESIDE = (0, 2.3, 6, 6)
FAR = (0.1, 1.5, 1.5, 1.5)


def product(left, right):
    return jnp.einsum("woe,wev->wov", left, right, preferred_element_type=jnp.float32)


def gradient_terms(log_grad, kin_part, weights):
    kin_grad = -0.5 * kin_part
    weighted = jnp.sum(weights[:, None, None] * log_grad + kin_grad, axis=0)
    return (weighted, jnp.sum(log_grad, axis=0))


def general_body(inverse_rows, kinetic_rows, virt_values, virt_laplacians, local_energy):
    walk_count = lax.axis_size("walk")
    walker_count = walk_count * local_energy.shape[0]
    energy_sum = lax.psum(jnp.sum(local_energy), "walk")
    average = energy_sum / walker_count
    weights = 2.0 * (local_energy - average)
    inverse_all, kinetic_all = (
        lax.all_gather(inverse_rows, "virt", axis=2, tiled=True),
        lax.all_gather(kinetic_rows, "virt", axis=2, tiled=True),
    )
    log_grad = product(inverse_all, virt_values)
    kin_part = product(inverse_all, virt_laplacians) - product(kinetic_all, virt_values)
    weighted, log_sum = gradient_terms(log_grad, kin_part, weights)
    summed = (
        lax.psum_scatter(weighted, "walk", scatter_dimension=0, tiled=True),
        lax.psum_scatter(log_sum, "walk", scatter_dimension=0, tiled=True),
    )
    gradient_part, log_part = (summed[0], summed[1])
    return (gradient_part / walker_count, log_part / walker_count)


SPAN = 248.0
EXTRA = 128
PART = EXTRA // 4
OFFSET = 3.1
TINY = 1e-30
MIB = 1024 * 1024


def stage_masks(count):
    bits = [1 << bit for bit in range(count.bit_length() - 1)]
    if len(bits) < 3:
        return [[bit] for bit in bits]
    return [bits[:1], bits[1:3]] + [[bit] for bit in bits[3:]]


def place_weights(stages):
    order = [mask for stage in stages for mask in stage]
    weights = [0] * len(order)
    for index, mask in enumerate(order):
        weights[mask.bit_length() - 1] = 1 << (len(order) - 1 - index)
    return weights


def partners(stage):
    if len(stage) == 1:
        return list(stage)
    first, second = stage
    return [second, first, first ^ second]


def swap(array, axis, mask):
    pairs = [(source, source ^ mask) for source in range(lax.axis_size(axis))]
    return lax.ppermute(array, axis, pairs)


def encode(rows):
    magnitude = jnp.abs(rows)
    largest = jnp.maximum(jnp.max(magnitude, axis=-1, keepdims=True), TINY)
    scale = (largest * (1.0 + 2.0**-7)).astype(jnp.bfloat16).astype(jnp.float32)
    code = jnp.exp2(magnitude * (SPAN / scale) - SPAN / 2)
    return jnp.where(rows < 0, -code, code).astype(jnp.bfloat16), scale


def decode(coded):
    width = coded.shape[1] - EXTRA
    code = coded[:, :width].astype(jnp.float32)
    scale = coded[:, width : width + 1].astype(jnp.float32)
    magnitude = (jnp.log2(jnp.abs(code)) + SPAN / 2) * (scale / SPAN)
    return jnp.where(code < 0, -magnitude, magnitude)


def store_coded(send_refs, blocks, energy):
    width = send_refs[0].shape[1] - EXTRA
    each = send_refs[0].shape[0]
    f32, bf16 = jnp.float32, jnp.bfloat16
    energy = jnp.concatenate([energy, energy], axis=0)
    high = energy.astype(bf16).astype(f32)
    middle = (energy - high).astype(bf16).astype(f32)
    low = energy - high - middle
    lane = lax.broadcasted_iota(jnp.int32, energy.shape, 1)
    terms = jnp.where(lane < 2 * PART, high, jnp.where(lane < 3 * PART, middle, low))
    for pair in range(len(blocks) // 2):
        code, scale = encode(jnp.concatenate(blocks[2 * pair : 2 * pair + 2], axis=0))
        send_ref = send_refs[16 * pair // each]
        target = slice(16 * pair % each, 16 * pair % each + 16)
        send_ref[target, :width] = code
        send_ref[target, width:] = jnp.where(lane < PART, scale, terms).astype(bf16)


def add_came(keep_ref, came_refs):
    arrays, height, width = keep_ref.shape
    width -= EXTRA
    per = height // 8
    sums = [keep_ref[index // per, 8 * (index % per) : 8 * (index % per) + 8, :width] for index in range(arrays * per)]
    energy = keep_ref[0, :8, width:]
    for parts in came_refs:
        index = 0
        for part in parts:
            for row in range(0, part.shape[0], 16):
                both = decode(part[row : row + 16, :])
                sums[index] += both[:8]
                sums[index + 1] += both[8:]
                index += 2
        terms = parts[0][:16, width:].astype(jnp.float32)[:8]
        for term in range(1, 4):
            energy += terms[:, term * PART : term * PART + 1]
    return [sums[array * per : (array + 1) * per] for array in range(arrays)], energy


def limit(mib):
    return pltpu.CompilerParams(vmem_limit_bytes=mib * MIB)


def cost(microseconds):
    return pl.CostEstimate(flops=int(microseconds * 1.1e9), bytes_accessed=0, transcendentals=0)


WHOLE = pl.BlockSpec(memory_space=pltpu.VMEM)
SCALAR = pl.BlockSpec(memory_space=pltpu.SMEM)
ANYWHERE = pl.BlockSpec(memory_space=pl.ANY)
HELD = pl.BlockSpec(memory_space=pltpu.HBM)
HELD = pl.BlockSpec(memory_space=pltpu.HBM)


def cut_kernel(inverse_ref, kinetic_ref, *out_refs):
    count = inverse_ref.shape[0]
    for array, ref in enumerate((inverse_ref, kinetic_ref)):
        for dest in range(0, count, 2):
            pair = [ref[dest + other].astype(jnp.float32) for other in range(2)]
            for index, out_ref in enumerate(out_refs):
                rows = jnp.concatenate([block[8 * index : 8 * index + 8] for block in pair], axis=0)
                out_ref[array, 8 * dest : 8 * dest + 16, :] = rows.astype(jnp.bfloat16)


def cut(inverse, kinetic, group):
    count, _, depth = inverse.shape
    block = pl.BlockSpec((count, 16, depth), lambda step: (0, group, 0))
    out = jax.ShapeDtypeStruct((2, 8 * count, depth), jnp.bfloat16)
    return pl.pallas_call(
        cut_kernel,
        out_shape=(out, out),
        grid=(1,),
        in_specs=[block, block],
        out_specs=(pl.BlockSpec(out.shape, lambda step: (0, 0, 0)),) * 2,
        compiler_params=limit(12),
        cost_estimate=cost(0.1),
        name="cut",
    )(inverse, kinetic)


def near_kernel(chunk, tile, virt_ref, me_ref, energy_ref, inverse_ref, kinetic_ref, values_ref, laps_ref, *rest):
    out_ref, far_values, far_laps, near_values, near_laps, own_inverse, own_kinetic, sems = rest[-8:]
    count, per, depth = inverse_ref.shape
    height = count * per
    width = out_ref.shape[3]
    f32 = jnp.float32
    own = pl.ds(pl.multiple_of(virt_ref[0] * depth, depth), depth)
    other = pl.ds(pl.multiple_of((1 - virt_ref[0]) * depth, depth), depth)
    chunks = width // chunk

    copies = []
    for index in range(chunks):
        columns = pl.ds(index * chunk, chunk)
        copies.append([
            pltpu.make_async_copy(table.at[own, columns], held.at[:, columns], sems.at[index, which])
            for which, (table, held) in enumerate(((values_ref, near_values), (laps_ref, near_laps)))
        ])
    last = [
        pltpu.make_async_copy(table.at[other, :], held, sems.at[chunks, which])
        for which, (table, held) in enumerate(((values_ref, far_values), (laps_ref, far_laps)))
    ]
    first = [
        pltpu.make_async_copy(rows, held, sems.at[chunks + 1, which])
        for which, (rows, held) in enumerate(((inverse_ref, own_inverse), (kinetic_ref, own_kinetic)))
    ]
    for copy in first + sum(copies, []) + last:
        copy.start()
    for copy in first:
        copy.wait()
    inverse = own_inverse[...].reshape(height, depth)
    kinetic = own_kinetic[...].reshape(height, depth)
    for index in range(chunks):
        for copy in copies[index]:
            copy.wait()

        @pl.loop(index * chunk // tile, (index + 1) * chunk // tile)
        def _(step):
            columns = pl.ds(pl.multiple_of(step * tile, tile), tile)
            values, laps = near_values[:, columns], near_laps[:, columns]
            out_ref[1, :, :, columns] = jnp.dot(inverse, values, preferred_element_type=f32).reshape(count, per, tile)
            rest = jnp.dot(kinetic, values, preferred_element_type=f32)
            rest -= jnp.dot(inverse, laps, preferred_element_type=f32)
            out_ref[0, :, :, columns] = (0.5 * rest).reshape(count, per, tile)

    for copy in last:
        copy.wait()


def near_product(virt, me, energy, inverse, kinetic, values, laplacians, after):
    count, per, depth = inverse.shape
    width = values.shape[1]
    chunk, tile = 512, 256
    table = pltpu.VMEM((depth, width), jnp.bfloat16)
    own = pltpu.VMEM((count, per, depth), jnp.bfloat16)
    return pl.pallas_call(
        functools.partial(near_kernel, chunk, tile),
        out_shape=(jax.ShapeDtypeStruct((2, count, per, width), jnp.float32), table, table),
        in_specs=[SCALAR, SCALAR, SCALAR, HELD, HELD, HELD, HELD] + [ANYWHERE] * len(after),
        out_specs=(WHOLE, WHOLE, WHOLE),
        scratch_shapes=[table, table, own, own, pltpu.SemaphoreType.DMA((width // chunk + 2, 2))],
        compiler_params=limit(24),
        cost_estimate=cost(9),
        name="near_product",
    )(virt, me, energy, inverse, kinetic, values, laplacians, *after)


def far_kernel(weights, count, tile, first, split, virt_ref, me_ref, energy_ref, far_ref, near_ref, values_ref, laps_ref, *rest):
    send_refs, place_ref = rest[-split - 1 : -1], rest[-1]
    _, height, depth = far_ref.shape
    width = near_ref.shape[3]
    rows = height // count
    half = height // 2
    f32 = jnp.float32
    scale = 2.0 * (energy_ref[0] - OFFSET)

    @pl.loop(0, width // tile)
    def _(index):
        columns = pl.ds(pl.multiple_of(index * tile, tile), tile)
        near = near_ref[:, :, first : first + rows, columns].reshape(2, height, tile)
        both = jnp.dot(far_ref[...].reshape(2 * height, depth), values_ref[:, columns], preferred_element_type=f32)
        laps = jnp.dot(far_ref[0], laps_ref[:, columns], preferred_element_type=f32)
        log = both[:height] + near[1]
        weighted = scale * log + (0.5 * (both[height:] - laps) + near[0])
        for dest in range(count):
            difference = dest ^ me_ref[0]
            place = 0
            for bit, weight in enumerate(weights):
                place = place ^ (((difference >> bit) & 1) * weight)
            target = pl.ds(pl.multiple_of(place * rows, rows), rows)
            source = slice(dest * rows, (dest + 1) * rows)
            place_ref[0, target, columns] = weighted[source]
            place_ref[1, target, columns] = log[source]

    energy = jnp.full((8, EXTRA), energy_ref[0], f32)
    place_ref[0, :8, width:] = energy
    blocks = [place_ref[array, row : row + 8, :width] for array in range(2) for row in range(half, height, 8)]
    store_coded(send_refs, blocks, energy)


def far_product(virt, me, energy, theirs, near, first, values, laplacians, tile, stages, split, after, length):
    _, height, depth = theirs.shape
    width = values.shape[1]
    half = height // 2
    count = 1 << sum(len(stage) for stage in stages)
    *sends, keep = pl.pallas_call(
        functools.partial(far_kernel, place_weights(stages), count, tile, first, split),
        out_shape=(jax.ShapeDtypeStruct((2 * half // split, width + EXTRA), jnp.bfloat16),) * split
        + (jax.ShapeDtypeStruct((2, height, width + EXTRA), jnp.float32),),
        in_specs=[SCALAR, SCALAR, SCALAR, WHOLE, WHOLE, WHOLE, WHOLE] + [ANYWHERE] * len(after),
        out_specs=(WHOLE,) * (split + 1),
        compiler_params=limit(24),
        cost_estimate=cost(length),
        name="far_product",
    )(virt, me, energy, theirs, near, values, laplacians, *after)
    return [sends], keep


def combine_kernel(layout, ordered, carried, height, *refs):
    count = len(layout)
    keep_refs, refs = [ref.at[:, :height] for ref in refs[:count]], refs[count:]
    came = []
    for parts in layout:
        came.append([])
        for index, first, last in parts:
            came[-1].append([refs[position].at[first:last, :] for position in index])
    inputs = 1 + max(position for parts in layout for index, _, _ in parts for position in index)
    refs = refs[inputs + ordered :]
    kept_refs, send_refs = refs[carried : carried + count], refs[carried + count :]
    if carried:
        above = refs[0].shape[0]
        send_refs[0][:above, :] = refs[0][...]
        send_refs = [send_refs[0].at[above:, :]]
    width = keep_refs[0].shape[2] - EXTRA
    for piece, (keep_ref, kept_ref) in enumerate(zip(keep_refs, kept_refs)):
        sums, energy = add_came(keep_ref, came[piece])
        kept = kept_ref.shape[1] // 8
        for array, blocks in enumerate(sums):
            for index, block in enumerate(blocks[:kept]):
                kept_ref[array, 8 * index : 8 * index + 8, :width] = block
        kept_ref[0, :8, width:] = energy
        rows = slice(16 * kept * piece, 16 * kept * (piece + 1))
        for index, send_ref in enumerate(send_refs):
            first = kept * (index + 1)
            store_coded([send_ref.at[rows, :]], [block for blocks in sums for block in blocks[first : first + kept]], energy)


def combine(keeps, came, layout, sent, after, length, carry=(), part=1):
    _, height, width = keeps[0].shape
    height = height // part
    kept = height // (sent + 1)
    count = len(keeps)
    above = sum(array.shape[0] for array in carry)
    outs = pl.pallas_call(
        functools.partial(combine_kernel, layout, len(after), len(carry), height),
        out_shape=(jax.ShapeDtypeStruct((2, kept, width), jnp.float32),) * count
        + (jax.ShapeDtypeStruct((2 * kept * count + above, width), jnp.bfloat16),) * sent,
        in_specs=[WHOLE] * (count + len(came)) + [ANYWHERE] * len(after) + [WHOLE] * len(carry),
        out_specs=(WHOLE,) * (count + sent),
        compiler_params=limit(10),
        cost_estimate=cost(length),
        name="combine",
    )(*keeps, *came, *after, *carry)
    return outs[count:], outs[:count]


def first_layout(count, split, rows):
    return tuple(((tuple(range(piece * split, piece * split + split)), 0, rows),) for piece in range(count))


def joint_layout(count, senders, rows):
    return tuple(
        tuple(((sender,), piece * rows, piece * rows + rows) for sender in range(senders)) for piece in range(count)
    )


def outputs_of(keep_ref, came, count):
    (gradient, log), energy = add_came(keep_ref, came)
    correction = 2.0 * (energy[:, :1] / count - OFFSET)
    log = [block / count for block in log]
    return [block / count - correction * mean for block, mean in zip(gradient, log)], log


def share_kernel(count, *refs):
    (gradient_ref, log_ref), refs = refs[-2:], refs[:-2]
    early = GROUPS[1:-1]
    came = [[] for piece in GROUPS[0]]
    for ref, group in zip(refs[len(refs) - len(early) :], early):
        came += [[[ref.at[16 * place : 16 * place + 16, :]]] for place in range(len(group))]
    row = 0
    for keep_ref, parts in zip(refs, came):
        for gradient, log in zip(*outputs_of(keep_ref, parts, count)):
            gradient_ref[row : row + 8, :] = gradient
            log_ref[row : row + 8, :] = log
            row += 8


def share(keeps, came, rows, count):
    width = keeps[0].shape[2] - EXTRA
    out = pltpu.HBM((rows, width), jnp.float32)
    block = pl.BlockSpec((sum(keep.shape[1] for keep in keeps), width), lambda step: (0, 0))
    return pl.pallas_call(
        functools.partial(share_kernel, count),
        out_shape=(out, out),
        grid=(1,),
        in_specs=[WHOLE] * (len(keeps) + len(came)),
        out_specs=(block, block),
        compiler_params=limit(8),
        cost_estimate=cost(0.1),
        name="share",
    )(*keeps, *came)


def finish_kernel(count, keep_ref, came_ref, *refs):
    gradient, log = outputs_of(keep_ref, [[came_ref]], count)
    for ref, blocks in zip(refs[-2:], (gradient, log)):
        for index, block in enumerate(blocks):
            ref[8 * index : 8 * index + 8, :] = block


def finish(outputs, keep, came, count):
    _, rows, width = keep.shape
    out = pltpu.HBM(outputs[0].shape, jnp.float32)
    last = outputs[0].shape[0] // rows - 1
    block = pl.BlockSpec((rows, width - EXTRA), lambda step: (last, 0))
    return pl.pallas_call(
        functools.partial(finish_kernel, count),
        out_shape=(out, out),
        grid=(1,),
        in_specs=[WHOLE, WHOLE, HELD, HELD],
        out_specs=(block, block),
        input_output_aliases={2: 0, 3: 1},
        compiler_params=limit(8),
        cost_estimate=cost(0.1),
        name="finish",
    )(keep, came, *outputs)


def pieced_body(pieces, tile, inverse_rows, kinetic_rows, virt_values, virt_laplacians, local_energy):
    count = lax.axis_size("walk")
    stages = stage_masks(count)
    me = lax.axis_index("walk").astype(jnp.int32).reshape(1)
    virt = lax.axis_index("virt").astype(jnp.int32).reshape(1)
    occupied, depth = inverse_rows.shape[1:]
    by_dest = (count, occupied // count, depth)
    inverse, kinetic = inverse_rows.reshape(by_dest), kinetic_rows.reshape(by_dest)
    rows = occupied // (count * pieces)

    inverse, kinetic, values, laplacians = (
        pltpu.with_memory_space_constraint(array, pltpu.HBM)
        for array in (inverse, kinetic, virt_values[0], virt_laplacians[0])
    )
    mine = [part for group in range(pieces // 2) for part in cut(inverse, kinetic, group)]
    mine[1], mine[2] = lax.optimization_barrier((mine[1], mine[2]))
    theirs = [swap(part, "virt", 1) for part in mine[:2]]
    near, values, laplacians = near_product(virt, me, local_energy, inverse, kinetic, values, laplacians, mine[2:])

    second = partners(stages[1])
    keep, came, carry, sent, last = {}, [], (), (), []

    def second_sums(piece, carry, after, length):
        layout = joint_layout(1, len(sent), sent[0].shape[0])
        (send,), (keep[piece],) = combine([keep[piece]], sent, layout, 1, after, length, carry)
        group = next(group for group in GROUPS if piece in group)
        if piece < group[-1]:
            return (send,), [keep[piece]]
        held.append(send)
        return (), [keep[piece]]

    held = []
    for turn in range(pieces):
        final = turn == pieces - 1
        send, kept = far_product(
            virt, me, local_energy, theirs[turn], near, turn * rows, values, laplacians, tile, stages, SPLIT[turn], last, FAR[turn]
        )
        if turn + 2 < pieces:
            part, kept = lax.optimization_barrier((mine[turn + 2], kept))
            theirs.append(swap(part, "virt", 1))
        if held and turn == pieces - 2:
            held[0], kept = lax.optimization_barrier((held[0], kept))
            came.append(swap(held.pop(), "walk", stages[2][0]))
        first = [swap(part, "walk", stages[0][0]) for part in send[0]]
        last = [kept]
        if final:
            layout = joint_layout(1, 1, came[0].shape[0])
            _, (keep[0],) = combine([keep[0]], came[:1], layout, 0, last, BESIDE[turn])
            last = [keep[0]]
        elif turn:
            carry, last = second_sums(turn - 1, carry, last, BESIDE[turn])
        layout = first_layout(1, SPLIT[turn], first[0].shape[0])
        sends, (keep[turn],) = combine([kept], first, layout, len(second), last, 0.1, part=2)
        last = [keep[turn]]
        if final:
            carry, last = second_sums(turn - 1, carry, last, 0.1)
            came.append(swap(held.pop(), "walk", stages[2][0]))
        sent = [swap(part, "walk", mask) for part, mask in reversed(list(zip(sends, second)))]
    second_sums(pieces - 1, (), last, 0.1)
    came.append(swap(held.pop(), "walk", stages[2][0]))
    outputs = share([keep[piece] for piece in range(pieces - 1)], came[1:-1], occupied // count, count)
    return finish(outputs, keep[pieces - 1], came[-1], count)


def solution(mesh):
    placed = (
        P("walk", None, "virt"),
        P("walk", None, "virt"),
        P("walk", None, "virt"),
        P("walk", None, "virt"),
        P("walk"),
    )

    def body(inverse_rows, kinetic_rows, virt_values, virt_laplacians, local_energy):
        count = mesh.shape["walk"]
        walkers, occupied, depth = inverse_rows.shape
        width = virt_values.shape[2]
        tile = 512
        fits = (
            walkers == 1
            and mesh.shape["virt"] == 2
            and count == 16
            and count >= 4
            and occupied == count * PIECES * 8
            and depth % 256 == 0
            and width % tile == 0
        )
        form = functools.partial(pieced_body, PIECES, tile) if fits else general_body
        return form(inverse_rows, kinetic_rows, virt_values, virt_laplacians, local_energy)

    return jax.shard_map(
        body,
        mesh=mesh,
        in_specs=placed,
        out_specs=(P("walk", "virt"), P("walk", "virt")),
        check_vma=False,
    )
```

```python
import functools

import jax
import jax.numpy as jnp
from jax import lax
from jax.experimental import pallas as pl
from jax.experimental.pallas import tpu as pltpu
from jax.sharding import PartitionSpec as P

PIECES = 4
GROUPS = ((0,), (1, 2), (3,))
SPLIT = (2, 2, 1, 1)
BESIDE = (0, 2.3, 6, 6)
FAR = (0.1, 1.5, 1.5, 1.5)


def product(left, right):
    return jnp.einsum("woe,wev->wov", left, right, preferred_element_type=jnp.float32)


def gradient_terms(log_grad, kin_part, weights):
    kin_grad = -0.5 * kin_part
    weighted = jnp.sum(weights[:, None, None] * log_grad + kin_grad, axis=0)
    return (weighted, jnp.sum(log_grad, axis=0))


def general_body(inverse_rows, kinetic_rows, virt_values, virt_laplacians, local_energy):
    walk_count = lax.axis_size("walk")
    walker_count = walk_count * local_energy.shape[0]
    energy_sum = lax.psum(jnp.sum(local_energy), "walk")
    average = energy_sum / walker_count
    weights = 2.0 * (local_energy - average)
    inverse_all, kinetic_all = (
        lax.all_gather(inverse_rows, "virt", axis=2, tiled=True),
        lax.all_gather(kinetic_rows, "virt", axis=2, tiled=True),
    )
    log_grad = product(inverse_all, virt_values)
    kin_part = product(inverse_all, virt_laplacians) - product(kinetic_all, virt_values)
    weighted, log_sum = gradient_terms(log_grad, kin_part, weights)
    summed = (
        lax.psum_scatter(weighted, "walk", scatter_dimension=0, tiled=True),
        lax.psum_scatter(log_sum, "walk", scatter_dimension=0, tiled=True),
    )
    gradient_part, log_part = (summed[0], summed[1])
    return (gradient_part / walker_count, log_part / walker_count)


SPAN = 248.0
EXTRA = 128
PART = EXTRA // 4
OFFSET = 3.1
TINY = 1e-30
MIB = 1024 * 1024


def stage_masks(count):
    bits = [1 << bit for bit in range(count.bit_length() - 1)]
    if len(bits) < 3:
        return [[bit] for bit in bits]
    return [bits[:1], bits[1:3]] + [[bit] for bit in bits[3:]]


def place_weights(stages):
    order = [mask for stage in stages for mask in stage]
    weights = [0] * len(order)
    for index, mask in enumerate(order):
        weights[mask.bit_length() - 1] = 1 << (len(order) - 1 - index)
    return weights


def partners(stage):
    if len(stage) == 1:
        return list(stage)
    first, second = stage
    return [second, first, first ^ second]


def swap(array, axis, mask):
    pairs = [(source, source ^ mask) for source in range(lax.axis_size(axis))]
    return lax.ppermute(array, axis, pairs)


def encode(rows):
    magnitude = jnp.abs(rows)
    largest = jnp.maximum(jnp.max(magnitude, axis=-1, keepdims=True), TINY)
    scale = (largest * (1.0 + 2.0**-7)).astype(jnp.bfloat16).astype(jnp.float32)
    code = jnp.exp2(magnitude * (SPAN / scale) - SPAN / 2)
    return jnp.where(rows < 0, -code, code).astype(jnp.bfloat16), scale


def decode(coded):
    width = coded.shape[1] - EXTRA
    code = coded[:, :width].astype(jnp.float32)
    scale = coded[:, width : width + 1].astype(jnp.float32)
    magnitude = (jnp.log2(jnp.abs(code)) + SPAN / 2) * (scale / SPAN)
    return jnp.where(code < 0, -magnitude, magnitude)


def store_coded(send_refs, blocks, energy):
    width = send_refs[0].shape[1] - EXTRA
    each = send_refs[0].shape[0]
    f32, bf16 = jnp.float32, jnp.bfloat16
    energy = jnp.concatenate([energy, energy], axis=0)
    high = energy.astype(bf16).astype(f32)
    middle = (energy - high).astype(bf16).astype(f32)
    low = energy - high - middle
    lane = lax.broadcasted_iota(jnp.int32, energy.shape, 1)
    terms = jnp.where(lane < 2 * PART, high, jnp.where(lane < 3 * PART, middle, low))
    for pair in range(len(blocks) // 2):
        code, scale = encode(jnp.concatenate(blocks[2 * pair : 2 * pair + 2], axis=0))
        send_ref = send_refs[16 * pair // each]
        target = slice(16 * pair % each, 16 * pair % each + 16)
        send_ref[target, :width] = code
        send_ref[target, width:] = jnp.where(lane < PART, scale, terms).astype(bf16)


def add_came(keep_ref, came_refs):
    arrays, height, width = keep_ref.shape
    width -= EXTRA
    per = height // 8
    sums = [keep_ref[index // per, 8 * (index % per) : 8 * (index % per) + 8, :width] for index in range(arrays * per)]
    energy = keep_ref[0, :8, width:]
    for parts in came_refs:
        index = 0
        for part in parts:
            for row in range(0, part.shape[0], 16):
                both = decode(part[row : row + 16, :])
                sums[index] += both[:8]
                sums[index + 1] += both[8:]
                index += 2
        terms = parts[0][:16, width:].astype(jnp.float32)[:8]
        for term in range(1, 4):
            energy += terms[:, term * PART : term * PART + 1]
    return [sums[array * per : (array + 1) * per] for array in range(arrays)], energy


def limit(mib):
    return pltpu.CompilerParams(vmem_limit_bytes=mib * MIB)


def cost(microseconds):
    return pl.CostEstimate(flops=int(microseconds * 1.1e9), bytes_accessed=0, transcendentals=0)


WHOLE = pl.BlockSpec(memory_space=pltpu.VMEM)
SCALAR = pl.BlockSpec(memory_space=pltpu.SMEM)
ANYWHERE = pl.BlockSpec(memory_space=pl.ANY)
HELD = pl.BlockSpec(memory_space=pltpu.HBM)
HELD = pl.BlockSpec(memory_space=pltpu.HBM)


def cut_kernel(inverse_ref, kinetic_ref, *out_refs):
    count = inverse_ref.shape[0]
    for array, ref in enumerate((inverse_ref, kinetic_ref)):
        for dest in range(0, count, 2):
            pair = [ref[dest + other].astype(jnp.float32) for other in range(2)]
            for index, out_ref in enumerate(out_refs):
                rows = jnp.concatenate([block[8 * index : 8 * index + 8] for block in pair], axis=0)
                out_ref[array, 8 * dest : 8 * dest + 16, :] = rows.astype(jnp.bfloat16)


def cut(inverse, kinetic, group):
    count, _, depth = inverse.shape
    block = pl.BlockSpec((count, 16, depth), lambda step: (0, group, 0))
    out = jax.ShapeDtypeStruct((2, 8 * count, depth), jnp.bfloat16)
    return pl.pallas_call(
        cut_kernel,
        out_shape=(out, out),
        grid=(1,),
        in_specs=[block, block],
        out_specs=(pl.BlockSpec(out.shape, lambda step: (0, 0, 0)),) * 2,
        compiler_params=limit(12),
        cost_estimate=cost(0.1),
        name="cut",
    )(inverse, kinetic)


def near_kernel(chunk, tile, virt_ref, me_ref, energy_ref, inverse_ref, kinetic_ref, values_ref, laps_ref, *rest):
    out_ref, far_values, far_laps, near_values, near_laps, own_inverse, own_kinetic, sems = rest[-8:]
    count, per, depth = inverse_ref.shape
    height = count * per
    width = out_ref.shape[3]
    f32 = jnp.float32
    own = pl.ds(pl.multiple_of(virt_ref[0] * depth, depth), depth)
    other = pl.ds(pl.multiple_of((1 - virt_ref[0]) * depth, depth), depth)
    chunks = width // chunk

    copies = []
    for index in range(chunks):
        columns = pl.ds(index * chunk, chunk)
        copies.append([
            pltpu.make_async_copy(table.at[own, columns], held.at[:, columns], sems.at[index, which])
            for which, (table, held) in enumerate(((values_ref, near_values), (laps_ref, near_laps)))
        ])
    last = [
        pltpu.make_async_copy(table.at[other, :], held, sems.at[chunks, which])
        for which, (table, held) in enumerate(((values_ref, far_values), (laps_ref, far_laps)))
    ]
    first = [
        pltpu.make_async_copy(rows, held, sems.at[chunks + 1, which])
        for which, (rows, held) in enumerate(((inverse_ref, own_inverse), (kinetic_ref, own_kinetic)))
    ]
    for copy in first + sum(copies, []) + last:
        copy.start()
    for copy in first:
        copy.wait()
    inverse = own_inverse[...].reshape(height, depth)
    kinetic = own_kinetic[...].reshape(height, depth)
    for index in range(chunks):
        for copy in copies[index]:
            copy.wait()

        @pl.loop(index * chunk // tile, (index + 1) * chunk // tile)
        def _(step):
            columns = pl.ds(pl.multiple_of(step * tile, tile), tile)
            values, laps = near_values[:, columns], near_laps[:, columns]
            out_ref[1, :, :, columns] = jnp.dot(inverse, values, preferred_element_type=f32).reshape(count, per, tile)
            rest = jnp.dot(kinetic, values, preferred_element_type=f32)
            rest -= jnp.dot(inverse, laps, preferred_element_type=f32)
            out_ref[0, :, :, columns] = (0.5 * rest).reshape(count, per, tile)

    for copy in last:
        copy.wait()


def near_product(virt, me, energy, inverse, kinetic, values, laplacians, after):
    count, per, depth = inverse.shape
    width = values.shape[1]
    chunk, tile = 512, 256
    table = pltpu.VMEM((depth, width), jnp.bfloat16)
    own = pltpu.VMEM((count, per, depth), jnp.bfloat16)
    return pl.pallas_call(
        functools.partial(near_kernel, chunk, tile),
        out_shape=(jax.ShapeDtypeStruct((2, count, per, width), jnp.float32), table, table),
        in_specs=[SCALAR, SCALAR, SCALAR, HELD, HELD, HELD, HELD] + [ANYWHERE] * len(after),
        out_specs=(WHOLE, WHOLE, WHOLE),
        scratch_shapes=[table, table, own, own, pltpu.SemaphoreType.DMA((width // chunk + 2, 2))],
        compiler_params=limit(24),
        cost_estimate=cost(9),
        name="near_product",
    )(virt, me, energy, inverse, kinetic, values, laplacians, *after)


def far_kernel(weights, count, tile, first, split, virt_ref, me_ref, energy_ref, far_ref, near_ref, values_ref, laps_ref, *rest):
    send_refs, place_ref = rest[-split - 1 : -1], rest[-1]
    _, height, depth = far_ref.shape
    width = near_ref.shape[3]
    rows = height // count
    half = height // 2
    f32 = jnp.float32
    scale = 2.0 * (energy_ref[0] - OFFSET)

    @pl.loop(0, width // tile)
    def _(index):
        columns = pl.ds(pl.multiple_of(index * tile, tile), tile)
        near = near_ref[:, :, first : first + rows, columns].reshape(2, height, tile)
        both = jnp.dot(far_ref[...].reshape(2 * height, depth), values_ref[:, columns], preferred_element_type=f32)
        laps = jnp.dot(far_ref[0], laps_ref[:, columns], preferred_element_type=f32)
        log = both[:height] + near[1]
        weighted = scale * log + (0.5 * (both[height:] - laps) + near[0])
        for dest in range(count):
            difference = dest ^ me_ref[0]
            place = 0
            for bit, weight in enumerate(weights):
                place = place ^ (((difference >> bit) & 1) * weight)
            target = pl.ds(pl.multiple_of(place * rows, rows), rows)
            source = slice(dest * rows, (dest + 1) * rows)
            place_ref[0, target, columns] = weighted[source]
            place_ref[1, target, columns] = log[source]

    energy = jnp.full((8, EXTRA), energy_ref[0], f32)
    place_ref[0, :8, width:] = energy
    blocks = [place_ref[array, row : row + 8, :width] for array in range(2) for row in range(half, height, 8)]
    store_coded(send_refs, blocks, energy)


def far_product(virt, me, energy, theirs, near, first, values, laplacians, tile, stages, split, after, length):
    _, height, depth = theirs.shape
    width = values.shape[1]
    half = height // 2
    count = 1 << sum(len(stage) for stage in stages)
    *sends, keep = pl.pallas_call(
        functools.partial(far_kernel, place_weights(stages), count, tile, first, split),
        out_shape=(jax.ShapeDtypeStruct((2 * half // split, width + EXTRA), jnp.bfloat16),) * split
        + (jax.ShapeDtypeStruct((2, height, width + EXTRA), jnp.float32),),
        in_specs=[SCALAR, SCALAR, SCALAR, WHOLE, WHOLE, WHOLE, WHOLE] + [ANYWHERE] * len(after),
        out_specs=(WHOLE,) * (split + 1),
        compiler_params=limit(24),
        cost_estimate=cost(length),
        name="far_product",
    )(virt, me, energy, theirs, near, values, laplacians, *after)
    return [sends], keep


def combine_kernel(layout, ordered, carried, height, *refs):
    count = len(layout)
    keep_refs, refs = [ref.at[:, :height] for ref in refs[:count]], refs[count:]
    came = []
    for parts in layout:
        came.append([])
        for index, first, last in parts:
            came[-1].append([refs[position].at[first:last, :] for position in index])
    inputs = 1 + max(position for parts in layout for index, _, _ in parts for position in index)
    refs = refs[inputs + ordered :]
    kept_refs, send_refs = refs[carried : carried + count], refs[carried + count :]
    if carried:
        above = refs[0].shape[0]
        send_refs[0][:above, :] = refs[0][...]
        send_refs = [send_refs[0].at[above:, :]]
    width = keep_refs[0].shape[2] - EXTRA
    for piece, (keep_ref, kept_ref) in enumerate(zip(keep_refs, kept_refs)):
        sums, energy = add_came(keep_ref, came[piece])
        kept = kept_ref.shape[1] // 8
        for array, blocks in enumerate(sums):
            for index, block in enumerate(blocks[:kept]):
                kept_ref[array, 8 * index : 8 * index + 8, :width] = block
        kept_ref[0, :8, width:] = energy
        rows = slice(16 * kept * piece, 16 * kept * (piece + 1))
        for index, send_ref in enumerate(send_refs):
            first = kept * (index + 1)
            store_coded([send_ref.at[rows, :]], [block for blocks in sums for block in blocks[first : first + kept]], energy)


def combine(keeps, came, layout, sent, after, length, carry=(), part=1):
    _, height, width = keeps[0].shape
    height = height // part
    kept = height // (sent + 1)
    count = len(keeps)
    above = sum(array.shape[0] for array in carry)
    outs = pl.pallas_call(
        functools.partial(combine_kernel, layout, len(after), len(carry), height),
        out_shape=(jax.ShapeDtypeStruct((2, kept, width), jnp.float32),) * count
        + (jax.ShapeDtypeStruct((2 * kept * count + above, width), jnp.bfloat16),) * sent,
        in_specs=[WHOLE] * (count + len(came)) + [ANYWHERE] * len(after) + [WHOLE] * len(carry),
        out_specs=(WHOLE,) * (count + sent),
        compiler_params=limit(10),
        cost_estimate=cost(length),
        name="combine",
    )(*keeps, *came, *after, *carry)
    return outs[count:], outs[:count]


def first_layout(count, split, rows):
    return tuple(((tuple(range(piece * split, piece * split + split)), 0, rows),) for piece in range(count))


def joint_layout(count, senders, rows):
    return tuple(
        tuple(((sender,), piece * rows, piece * rows + rows) for sender in range(senders)) for piece in range(count)
    )


def outputs_of(keep_ref, came, count):
    (gradient, log), energy = add_came(keep_ref, came)
    correction = 2.0 * (energy[:, :1] / count - OFFSET)
    log = [block / count for block in log]
    return [block / count - correction * mean for block, mean in zip(gradient, log)], log


def share_kernel(count, *refs):
    (gradient_ref, log_ref), refs = refs[-2:], refs[:-2]
    early = GROUPS[1:-1]
    came = [[] for piece in GROUPS[0]]
    for ref, group in zip(refs[len(refs) - len(early) :], early):
        came += [[[ref.at[16 * place : 16 * place + 16, :]]] for place in range(len(group))]
    row = 0
    for keep_ref, parts in zip(refs, came):
        for gradient, log in zip(*outputs_of(keep_ref, parts, count)):
            gradient_ref[row : row + 8, :] = gradient
            log_ref[row : row + 8, :] = log
            row += 8


def share(keeps, came, rows, count):
    width = keeps[0].shape[2] - EXTRA
    out = pltpu.HBM((rows, width), jnp.float32)
    block = pl.BlockSpec((sum(keep.shape[1] for keep in keeps), width), lambda step: (0, 0))
    return pl.pallas_call(
        functools.partial(share_kernel, count),
        out_shape=(out, out),
        grid=(1,),
        in_specs=[WHOLE] * (len(keeps) + len(came)),
        out_specs=(block, block),
        compiler_params=limit(8),
        cost_estimate=cost(0.1),
        name="share",
    )(*keeps, *came)


def finish_kernel(count, keep_ref, came_ref, *refs):
    gradient, log = outputs_of(keep_ref, [[came_ref]], count)
    for ref, blocks in zip(refs[-2:], (gradient, log)):
        for index, block in enumerate(blocks):
            ref[8 * index : 8 * index + 8, :] = block


def finish(outputs, keep, came, count):
    _, rows, width = keep.shape
    out = pltpu.HBM(outputs[0].shape, jnp.float32)
    last = outputs[0].shape[0] // rows - 1
    block = pl.BlockSpec((rows, width - EXTRA), lambda step: (last, 0))
    return pl.pallas_call(
        functools.partial(finish_kernel, count),
        out_shape=(out, out),
        grid=(1,),
        in_specs=[WHOLE, WHOLE, HELD, HELD],
        out_specs=(block, block),
        input_output_aliases={2: 0, 3: 1},
        compiler_params=limit(8),
        cost_estimate=cost(0.1),
        name="finish",
    )(keep, came, *outputs)


def pieced_body(pieces, tile, inverse_rows, kinetic_rows, virt_values, virt_laplacians, local_energy):
    count = lax.axis_size("walk")
    stages = stage_masks(count)
    me = lax.axis_index("walk").astype(jnp.int32).reshape(1)
    virt = lax.axis_index("virt").astype(jnp.int32).reshape(1)
    occupied, depth = inverse_rows.shape[1:]
    by_dest = (count, occupied // count, depth)
    inverse, kinetic = inverse_rows.reshape(by_dest), kinetic_rows.reshape(by_dest)
    rows = occupied // (count * pieces)

    inverse, kinetic, values, laplacians = (
        pltpu.with_memory_space_constraint(array, pltpu.HBM)
        for array in (inverse, kinetic, virt_values[0], virt_laplacians[0])
    )
    mine = [part for group in range(pieces // 2) for part in cut(inverse, kinetic, group)]
    mine[1], mine[2] = lax.optimization_barrier((mine[1], mine[2]))
    theirs = [swap(part, "virt", 1) for part in mine[:2]]
    near, values, laplacians = near_product(virt, me, local_energy, inverse, kinetic, values, laplacians, mine[2:])

    second = partners(stages[1])
    keep, came, carry, sent, last = {}, [], (), (), []

    def second_sums(piece, carry, after, length):
        layout = joint_layout(1, len(sent), sent[0].shape[0])
        (send,), (keep[piece],) = combine([keep[piece]], sent, layout, 1, after, length, carry)
        group = next(group for group in GROUPS if piece in group)
        if piece < group[-1]:
            return (send,), [keep[piece]]
        held.append(send)
        return (), [keep[piece]]

    held = []
    for turn in range(pieces):
        final = turn == pieces - 1
        send, kept = far_product(
            virt, me, local_energy, theirs[turn], near, turn * rows, values, laplacians, tile, stages, SPLIT[turn], last, FAR[turn]
        )
        if turn + 2 < pieces:
            part, kept = lax.optimization_barrier((mine[turn + 2], kept))
            theirs.append(swap(part, "virt", 1))
        if held and turn == pieces - 2:
            held[0], kept = lax.optimization_barrier((held[0], kept))
            came.append(swap(held.pop(), "walk", stages[2][0]))
        first = [swap(part, "walk", stages[0][0]) for part in send[0]]
        last = [kept]
        if final:
            layout = joint_layout(1, 1, came[0].shape[0])
            _, (keep[0],) = combine([keep[0]], came[:1], layout, 0, last, BESIDE[turn])
            last = [keep[0]]
        elif turn:
            carry, last = second_sums(turn - 1, carry, last, BESIDE[turn])
        layout = first_layout(1, SPLIT[turn], first[0].shape[0])
        sends, (keep[turn],) = combine([kept], first, layout, len(second), last, 0.1, part=2)
        last = [keep[turn]]
        if final:
            carry, last = second_sums(turn - 1, carry, last, 0.1)
            came.append(swap(held.pop(), "walk", stages[2][0]))
        sent = [swap(part, "walk", mask) for part, mask in reversed(list(zip(sends, second)))]
    second_sums(pieces - 1, (), last, 0.1)
    came.append(swap(held.pop(), "walk", stages[2][0]))
    outputs = share([keep[piece] for piece in range(pieces - 1)], came[1:-1], occupied // count, count)
    return finish(outputs, keep[pieces - 1], came[-1], count)


def solution(mesh):
    placed = (
        P("walk", None, "virt"),
        P("walk", None, "virt"),
        P("walk", None, "virt"),
        P("walk", None, "virt"),
        P("walk"),
    )

    def body(inverse_rows, kinetic_rows, virt_values, virt_laplacians, local_energy):
        count = mesh.shape["walk"]
        walkers, occupied, depth = inverse_rows.shape
        width = virt_values.shape[2]
        tile = 1024
        fits = (
            walkers == 1
            and mesh.shape["virt"] == 2
            and count == 16
            and count >= 4
            and occupied == count * PIECES * 8
            and depth % 256 == 0
            and width % tile == 0
        )
        form = functools.partial(pieced_body, PIECES, tile) if fits else general_body
        return form(inverse_rows, kinetic_rows, virt_values, virt_laplacians, local_energy)

    return jax.shard_map(
        body,
        mesh=mesh,
        in_specs=placed,
        out_specs=(P("walk", "virt"), P("walk", "virt")),
        check_vma=False,
    )
```

```python
import functools

import jax
import jax.numpy as jnp
from jax import lax
from jax.experimental import pallas as pl
from jax.experimental.pallas import tpu as pltpu
from jax.sharding import PartitionSpec as P

PIECES = 4
GROUPS = ((0,), (1, 2), (3,))
SPLIT = (2, 2, 1, 1)
BESIDE = (0, 2.3, 6, 6)
FAR = (0.1, 1.5, 1.5, 1.5)


def product(left, right):
    return jnp.einsum("woe,wev->wov", left, right, preferred_element_type=jnp.float32)


def gradient_terms(log_grad, kin_part, weights):
    kin_grad = -0.5 * kin_part
    weighted = jnp.sum(weights[:, None, None] * log_grad + kin_grad, axis=0)
    return (weighted, jnp.sum(log_grad, axis=0))


def general_body(inverse_rows, kinetic_rows, virt_values, virt_laplacians, local_energy):
    walk_count = lax.axis_size("walk")
    walker_count = walk_count * local_energy.shape[0]
    energy_sum = lax.psum(jnp.sum(local_energy), "walk")
    average = energy_sum / walker_count
    weights = 2.0 * (local_energy - average)
    inverse_all, kinetic_all = (
        lax.all_gather(inverse_rows, "virt", axis=2, tiled=True),
        lax.all_gather(kinetic_rows, "virt", axis=2, tiled=True),
    )
    log_grad = product(inverse_all, virt_values)
    kin_part = product(inverse_all, virt_laplacians) - product(kinetic_all, virt_values)
    weighted, log_sum = gradient_terms(log_grad, kin_part, weights)
    summed = (
        lax.psum_scatter(weighted, "walk", scatter_dimension=0, tiled=True),
        lax.psum_scatter(log_sum, "walk", scatter_dimension=0, tiled=True),
    )
    gradient_part, log_part = (summed[0], summed[1])
    return (gradient_part / walker_count, log_part / walker_count)


SPAN = 248.0
EXTRA = 128
PART = EXTRA // 4
OFFSET = 3.1
TINY = 1e-30
MIB = 1024 * 1024


def stage_masks(count):
    bits = [1 << bit for bit in range(count.bit_length() - 1)]
    if len(bits) < 3:
        return [[bit] for bit in bits]
    return [bits[:1], bits[1:3]] + [[bit] for bit in bits[3:]]


def place_weights(stages):
    order = [mask for stage in stages for mask in stage]
    weights = [0] * len(order)
    for index, mask in enumerate(order):
        weights[mask.bit_length() - 1] = 1 << (len(order) - 1 - index)
    return weights


def partners(stage):
    if len(stage) == 1:
        return list(stage)
    first, second = stage
    return [second, first, first ^ second]


def swap(array, axis, mask):
    pairs = [(source, source ^ mask) for source in range(lax.axis_size(axis))]
    return lax.ppermute(array, axis, pairs)


def encode(rows):
    magnitude = jnp.abs(rows)
    largest = jnp.maximum(jnp.max(magnitude, axis=-1, keepdims=True), TINY)
    scale = (largest * (1.0 + 2.0**-7)).astype(jnp.bfloat16).astype(jnp.float32)
    code = jnp.exp2(magnitude * (SPAN / scale) - SPAN / 2)
    return jnp.where(rows < 0, -code, code).astype(jnp.bfloat16), scale


def decode(coded):
    width = coded.shape[1] - EXTRA
    code = coded[:, :width].astype(jnp.float32)
    scale = coded[:, width : width + 1].astype(jnp.float32)
    magnitude = (jnp.log2(jnp.abs(code)) + SPAN / 2) * (scale / SPAN)
    return jnp.where(code < 0, -magnitude, magnitude)


def store_coded(send_refs, blocks, energy):
    width = send_refs[0].shape[1] - EXTRA
    each = send_refs[0].shape[0]
    f32, bf16 = jnp.float32, jnp.bfloat16
    energy = jnp.concatenate([energy, energy], axis=0)
    high = energy.astype(bf16).astype(f32)
    middle = (energy - high).astype(bf16).astype(f32)
    low = energy - high - middle
    lane = lax.broadcasted_iota(jnp.int32, energy.shape, 1)
    terms = jnp.where(lane < 2 * PART, high, jnp.where(lane < 3 * PART, middle, low))
    for pair in range(len(blocks) // 2):
        code, scale = encode(jnp.concatenate(blocks[2 * pair : 2 * pair + 2], axis=0))
        send_ref = send_refs[16 * pair // each]
        target = slice(16 * pair % each, 16 * pair % each + 16)
        send_ref[target, :width] = code
        send_ref[target, width:] = jnp.where(lane < PART, scale, terms).astype(bf16)


def add_came(keep_ref, came_refs):
    arrays, height, width = keep_ref.shape
    width -= EXTRA
    per = height // 8
    sums = [keep_ref[index // per, 8 * (index % per) : 8 * (index % per) + 8, :width] for index in range(arrays * per)]
    energy = keep_ref[0, :8, width:]
    for parts in came_refs:
        index = 0
        for part in parts:
            for row in range(0, part.shape[0], 16):
                both = decode(part[row : row + 16, :])
                sums[index] += both[:8]
                sums[index + 1] += both[8:]
                index += 2
        terms = parts[0][:16, width:].astype(jnp.float32)[:8]
        for term in range(1, 4):
            energy += terms[:, term * PART : term * PART + 1]
    return [sums[array * per : (array + 1) * per] for array in range(arrays)], energy


def limit(mib):
    return pltpu.CompilerParams(vmem_limit_bytes=mib * MIB)


def cost(microseconds):
    return pl.CostEstimate(flops=int(microseconds * 1.1e9), bytes_accessed=0, transcendentals=0)


WHOLE = pl.BlockSpec(memory_space=pltpu.VMEM)
SCALAR = pl.BlockSpec(memory_space=pltpu.SMEM)
ANYWHERE = pl.BlockSpec(memory_space=pl.ANY)
HELD = pl.BlockSpec(memory_space=pltpu.HBM)
HELD = pl.BlockSpec(memory_space=pltpu.HBM)


def cut_kernel(inverse_ref, kinetic_ref, *out_refs):
    count = inverse_ref.shape[0]
    for array, ref in enumerate((inverse_ref, kinetic_ref)):
        for dest in range(0, count, 2):
            pair = [ref[dest + other].astype(jnp.float32) for other in range(2)]
            for index, out_ref in enumerate(out_refs):
                rows = jnp.concatenate([block[8 * index : 8 * index + 8] for block in pair], axis=0)
                out_ref[array, 8 * dest : 8 * dest + 16, :] = rows.astype(jnp.bfloat16)


def cut(inverse, kinetic, group):
    count, _, depth = inverse.shape
    block = pl.BlockSpec((count, 16, depth), lambda step: (0, group, 0))
    out = jax.ShapeDtypeStruct((2, 8 * count, depth), jnp.bfloat16)
    return pl.pallas_call(
        cut_kernel,
        out_shape=(out, out),
        grid=(1,),
        in_specs=[block, block],
        out_specs=(pl.BlockSpec(out.shape, lambda step: (0, 0, 0)),) * 2,
        compiler_params=limit(12),
        cost_estimate=cost(0.1),
        name="cut",
    )(inverse, kinetic)


def near_kernel(chunk, tile, virt_ref, me_ref, energy_ref, inverse_ref, kinetic_ref, values_ref, laps_ref, *rest):
    out_ref, far_values, far_laps, near_values, near_laps, own_inverse, own_kinetic, sems = rest[-8:]
    count, per, depth = inverse_ref.shape
    height = count * per
    width = out_ref.shape[3]
    f32 = jnp.float32
    own = pl.ds(pl.multiple_of(virt_ref[0] * depth, depth), depth)
    other = pl.ds(pl.multiple_of((1 - virt_ref[0]) * depth, depth), depth)
    chunks = width // chunk

    copies = []
    for index in range(chunks):
        columns = pl.ds(index * chunk, chunk)
        copies.append([
            pltpu.make_async_copy(table.at[own, columns], held.at[:, columns], sems.at[index, which])
            for which, (table, held) in enumerate(((values_ref, near_values), (laps_ref, near_laps)))
        ])
    last = [
        pltpu.make_async_copy(table.at[other, :], held, sems.at[chunks, which])
        for which, (table, held) in enumerate(((values_ref, far_values), (laps_ref, far_laps)))
    ]
    first = [
        pltpu.make_async_copy(rows, held, sems.at[chunks + 1, which])
        for which, (rows, held) in enumerate(((inverse_ref, own_inverse), (kinetic_ref, own_kinetic)))
    ]
    for copy in first + sum(copies, []) + last:
        copy.start()
    for copy in first:
        copy.wait()
    inverse = own_inverse[...].reshape(height, depth)
    kinetic = own_kinetic[...].reshape(height, depth)
    for index in range(chunks):
        for copy in copies[index]:
            copy.wait()

        @pl.loop(index * chunk // tile, (index + 1) * chunk // tile)
        def _(step):
            columns = pl.ds(pl.multiple_of(step * tile, tile), tile)
            values, laps = near_values[:, columns], near_laps[:, columns]
            out_ref[1, :, :, columns] = jnp.dot(inverse, values, preferred_element_type=f32).reshape(count, per, tile)
            rest = jnp.dot(kinetic, values, preferred_element_type=f32)
            rest -= jnp.dot(inverse, laps, preferred_element_type=f32)
            out_ref[0, :, :, columns] = (0.5 * rest).reshape(count, per, tile)

    for copy in last:
        copy.wait()


def near_product(virt, me, energy, inverse, kinetic, values, laplacians, after):
    count, per, depth = inverse.shape
    width = values.shape[1]
    chunk, tile = 512, 256
    table = pltpu.VMEM((depth, width), jnp.bfloat16)
    own = pltpu.VMEM((count, per, depth), jnp.bfloat16)
    return pl.pallas_call(
        functools.partial(near_kernel, chunk, tile),
        out_shape=(jax.ShapeDtypeStruct((2, count, per, width), jnp.float32), table, table),
        in_specs=[SCALAR, SCALAR, SCALAR, HELD, HELD, HELD, HELD] + [ANYWHERE] * len(after),
        out_specs=(WHOLE, WHOLE, WHOLE),
        scratch_shapes=[table, table, own, own, pltpu.SemaphoreType.DMA((width // chunk + 2, 2))],
        compiler_params=limit(24),
        cost_estimate=cost(9),
        name="near_product",
    )(virt, me, energy, inverse, kinetic, values, laplacians, *after)


def far_kernel(weights, count, tile, first, split, virt_ref, me_ref, energy_ref, far_ref, near_ref, values_ref, laps_ref, *rest):
    send_refs, place_ref = rest[-split - 1 : -1], rest[-1]
    _, height, depth = far_ref.shape
    width = near_ref.shape[3]
    rows = height // count
    half = height // 2
    f32 = jnp.float32
    scale = 2.0 * (energy_ref[0] - OFFSET)

    @pl.loop(0, width // tile)
    def _(index):
        columns = pl.ds(pl.multiple_of(index * tile, tile), tile)
        near = near_ref[:, :, first : first + rows, columns].reshape(2, height, tile)
        both = jnp.dot(far_ref[...].reshape(2 * height, depth), values_ref[:, columns], preferred_element_type=f32)
        laps = jnp.dot(far_ref[0], laps_ref[:, columns], preferred_element_type=f32)
        log = both[:height] + near[1]
        weighted = scale * log + (0.5 * (both[height:] - laps) + near[0])
        for dest in range(count):
            difference = dest ^ me_ref[0]
            place = 0
            for bit, weight in enumerate(weights):
                place = place ^ (((difference >> bit) & 1) * weight)
            target = pl.ds(pl.multiple_of(place * rows, rows), rows)
            source = slice(dest * rows, (dest + 1) * rows)
            place_ref[0, target, columns] = weighted[source]
            place_ref[1, target, columns] = log[source]

    energy = jnp.full((8, EXTRA), energy_ref[0], f32)
    place_ref[0, :8, width:] = energy
    blocks = [place_ref[array, row : row + 8, :width] for array in range(2) for row in range(half, height, 8)]
    store_coded(send_refs, blocks, energy)


def far_product(virt, me, energy, theirs, near, first, values, laplacians, tile, stages, split, after, length):
    _, height, depth = theirs.shape
    width = values.shape[1]
    half = height // 2
    count = 1 << sum(len(stage) for stage in stages)
    *sends, keep = pl.pallas_call(
        functools.partial(far_kernel, place_weights(stages), count, tile, first, split),
        out_shape=(jax.ShapeDtypeStruct((2 * half // split, width + EXTRA), jnp.bfloat16),) * split
        + (jax.ShapeDtypeStruct((2, height, width + EXTRA), jnp.float32),),
        in_specs=[SCALAR, SCALAR, SCALAR, WHOLE, WHOLE, WHOLE, WHOLE] + [ANYWHERE] * len(after),
        out_specs=(WHOLE,) * (split + 1),
        compiler_params=limit(24),
        cost_estimate=cost(length),
        name="far_product",
    )(virt, me, energy, theirs, near, values, laplacians, *after)
    return [sends], keep


def combine_kernel(layout, ordered, carried, height, *refs):
    count = len(layout)
    keep_refs, refs = [ref.at[:, :height] for ref in refs[:count]], refs[count:]
    came = []
    for parts in layout:
        came.append([])
        for index, first, last in parts:
            came[-1].append([refs[position].at[first:last, :] for position in index])
    inputs = 1 + max(position for parts in layout for index, _, _ in parts for position in index)
    refs = refs[inputs + ordered :]
    kept_refs, send_refs = refs[carried : carried + count], refs[carried + count :]
    if carried:
        above = refs[0].shape[0]
        send_refs[0][:above, :] = refs[0][...]
        send_refs = [send_refs[0].at[above:, :]]
    width = keep_refs[0].shape[2] - EXTRA
    for piece, (keep_ref, kept_ref) in enumerate(zip(keep_refs, kept_refs)):
        sums, energy = add_came(keep_ref, came[piece])
        kept = kept_ref.shape[1] // 8
        for array, blocks in enumerate(sums):
            for index, block in enumerate(blocks[:kept]):
                kept_ref[array, 8 * index : 8 * index + 8, :width] = block
        kept_ref[0, :8, width:] = energy
        rows = slice(16 * kept * piece, 16 * kept * (piece + 1))
        for index, send_ref in enumerate(send_refs):
            first = kept * (index + 1)
            store_coded([send_ref.at[rows, :]], [block for blocks in sums for block in blocks[first : first + kept]], energy)


def combine(keeps, came, layout, sent, after, length, carry=(), part=1):
    _, height, width = keeps[0].shape
    height = height // part
    kept = height // (sent + 1)
    count = len(keeps)
    above = sum(array.shape[0] for array in carry)
    outs = pl.pallas_call(
        functools.partial(combine_kernel, layout, len(after), len(carry), height),
        out_shape=(jax.ShapeDtypeStruct((2, kept, width), jnp.float32),) * count
        + (jax.ShapeDtypeStruct((2 * kept * count + above, width), jnp.bfloat16),) * sent,
        in_specs=[WHOLE] * (count + len(came)) + [ANYWHERE] * len(after) + [WHOLE] * len(carry),
        out_specs=(WHOLE,) * (count + sent),
        compiler_params=limit(10),
        cost_estimate=cost(length),
        name="combine",
    )(*keeps, *came, *after, *carry)
    return outs[count:], outs[:count]


def first_layout(count, split, rows):
    return tuple(((tuple(range(piece * split, piece * split + split)), 0, rows),) for piece in range(count))


def joint_layout(count, senders, rows):
    return tuple(
        tuple(((sender,), piece * rows, piece * rows + rows) for sender in range(senders)) for piece in range(count)
    )


def outputs_of(keep_ref, came, count):
    (gradient, log), energy = add_came(keep_ref, came)
    correction = 2.0 * (energy[:, :1] / count - OFFSET)
    log = [block / count for block in log]
    return [block / count - correction * mean for block, mean in zip(gradient, log)], log


def share_kernel(count, *refs):
    (gradient_ref, log_ref), refs = refs[-2:], refs[:-2]
    early = GROUPS[1:-1]
    came = [[] for piece in GROUPS[0]]
    for ref, group in zip(refs[len(refs) - len(early) :], early):
        came += [[[ref.at[16 * place : 16 * place + 16, :]]] for place in range(len(group))]
    row = 0
    for keep_ref, parts in zip(refs, came):
        for gradient, log in zip(*outputs_of(keep_ref, parts, count)):
            gradient_ref[row : row + 8, :] = gradient
            log_ref[row : row + 8, :] = log
            row += 8


def share(keeps, came, rows, count):
    width = keeps[0].shape[2] - EXTRA
    out = pltpu.HBM((rows, width), jnp.float32)
    block = pl.BlockSpec((sum(keep.shape[1] for keep in keeps), width), lambda step: (0, 0))
    return pl.pallas_call(
        functools.partial(share_kernel, count),
        out_shape=(out, out),
        grid=(1,),
        in_specs=[WHOLE] * (len(keeps) + len(came)),
        out_specs=(block, block),
        compiler_params=limit(8),
        cost_estimate=cost(0.1),
        name="share",
    )(*keeps, *came)


def finish_kernel(count, keep_ref, came_ref, *refs):
    gradient, log = outputs_of(keep_ref, [[came_ref]], count)
    for ref, blocks in zip(refs[-2:], (gradient, log)):
        for index, block in enumerate(blocks):
            ref[8 * index : 8 * index + 8, :] = block


def finish(outputs, keep, came, count):
    _, rows, width = keep.shape
    out = pltpu.HBM(outputs[0].shape, jnp.float32)
    last = outputs[0].shape[0] // rows - 1
    block = pl.BlockSpec((rows, width - EXTRA), lambda step: (last, 0))
    return pl.pallas_call(
        functools.partial(finish_kernel, count),
        out_shape=(out, out),
        grid=(1,),
        in_specs=[WHOLE, WHOLE, HELD, HELD],
        out_specs=(block, block),
        input_output_aliases={2: 0, 3: 1},
        compiler_params=limit(8),
        cost_estimate=cost(0.1),
        name="finish",
    )(keep, came, *outputs)


def pieced_body(pieces, tile, inverse_rows, kinetic_rows, virt_values, virt_laplacians, local_energy):
    count = lax.axis_size("walk")
    stages = stage_masks(count)
    me = lax.axis_index("walk").astype(jnp.int32).reshape(1)
    virt = lax.axis_index("virt").astype(jnp.int32).reshape(1)
    occupied, depth = inverse_rows.shape[1:]
    by_dest = (count, occupied // count, depth)
    inverse, kinetic = inverse_rows.reshape(by_dest), kinetic_rows.reshape(by_dest)
    rows = occupied // (count * pieces)

    inverse, kinetic, values, laplacians = (
        pltpu.with_memory_space_constraint(array, pltpu.HBM)
        for array in (inverse, kinetic, virt_values[0], virt_laplacians[0])
    )
    mine = [part for group in range(pieces // 2) for part in cut(inverse, kinetic, group)]
    mine[1], mine[2] = lax.optimization_barrier((mine[1], mine[2]))
    theirs = [swap(part, "virt", 1) for part in mine[:2]]
    near, values, laplacians = near_product(virt, me, local_energy, inverse, kinetic, values, laplacians, mine[2:])

    second = partners(stages[1])
    keep, came, carry, sent, last = {}, [], (), (), []

    def second_sums(piece, carry, after, length):
        layout = joint_layout(1, len(sent), sent[0].shape[0])
        (send,), (keep[piece],) = combine([keep[piece]], sent, layout, 1, after, length, carry)
        group = next(group for group in GROUPS if piece in group)
        if piece < group[-1]:
            return (send,), [keep[piece]]
        held.append(send)
        return (), [keep[piece]]

    held = []
    for turn in range(pieces):
        final = turn == pieces - 1
        send, kept = far_product(
            virt, me, local_energy, theirs[turn], near, turn * rows, values, laplacians, tile, stages, SPLIT[turn], last, FAR[turn]
        )
        if turn + 2 < pieces:
            part, kept = lax.optimization_barrier((mine[turn + 2], kept))
            theirs.append(swap(part, "virt", 1))
        if held and turn == pieces - 2:
            held[0], kept = lax.optimization_barrier((held[0], kept))
            came.append(swap(held.pop(), "walk", stages[2][0]))
        first = [swap(part, "walk", stages[0][0]) for part in send[0]]
        last = [kept]
        if final:
            layout = joint_layout(1, 1, came[0].shape[0])
            _, (keep[0],) = combine([keep[0]], came[:1], layout, 0, last, BESIDE[turn])
            last = [keep[0]]
        elif turn:
            carry, last = second_sums(turn - 1, carry, last, BESIDE[turn])
        layout = first_layout(1, SPLIT[turn], first[0].shape[0])
        sends, (keep[turn],) = combine([kept], first, layout, len(second), last, 0.1, part=2)
        last = [keep[turn]]
        if final:
            carry, last = second_sums(turn - 1, carry, last, 0.1)
            came.append(swap(held.pop(), "walk", stages[2][0]))
        sent = [swap(part, "walk", mask) for part, mask in reversed(list(zip(sends, second)))]
    second_sums(pieces - 1, (), last, 0.1)
    came.append(swap(held.pop(), "walk", stages[2][0]))
    outputs = share([keep[piece] for piece in range(pieces - 1)], came[1:-1], occupied // count, count)
    return finish(outputs, keep[pieces - 1], came[-1], count)


def solution(mesh):
    placed = (
        P("walk", None, "virt"),
        P("walk", None, "virt"),
        P("walk", None, "virt"),
        P("walk", None, "virt"),
        P("walk"),
    )

    def body(inverse_rows, kinetic_rows, virt_values, virt_laplacians, local_energy):
        count = mesh.shape["walk"]
        walkers, occupied, depth = inverse_rows.shape
        width = virt_values.shape[2]
        tile = 2048
        fits = (
            walkers == 1
            and mesh.shape["virt"] == 2
            and count == 16
            and count >= 4
            and occupied == count * PIECES * 8
            and depth % 256 == 0
            and width % tile == 0
        )
        form = functools.partial(pieced_body, PIECES, tile) if fits else general_body
        return form(inverse_rows, kinetic_rows, virt_values, virt_laplacians, local_energy)

    return jax.shard_map(
        body,
        mesh=mesh,
        in_specs=placed,
        out_specs=(P("walk", "virt"), P("walk", "virt")),
        check_vma=False,
    )
```

```python
import functools

import jax
import jax.numpy as jnp
from jax import lax
from jax.experimental import pallas as pl
from jax.experimental.pallas import tpu as pltpu
from jax.sharding import PartitionSpec as P

PIECES = 4
GROUPS = ((0, 1), (2,), (3,))
SPLIT = (2, 2, 1, 1)
BESIDE = (0, 2.3, 6, 6)
FAR = (0.1, 1.5, 1.5, 1.5)


def product(left, right):
    return jnp.einsum("woe,wev->wov", left, right, preferred_element_type=jnp.float32)


def gradient_terms(log_grad, kin_part, weights):
    kin_grad = -0.5 * kin_part
    weighted = jnp.sum(weights[:, None, None] * log_grad + kin_grad, axis=0)
    return (weighted, jnp.sum(log_grad, axis=0))


def general_body(inverse_rows, kinetic_rows, virt_values, virt_laplacians, local_energy):
    walk_count = lax.axis_size("walk")
    walker_count = walk_count * local_energy.shape[0]
    energy_sum = lax.psum(jnp.sum(local_energy), "walk")
    average = energy_sum / walker_count
    weights = 2.0 * (local_energy - average)
    inverse_all, kinetic_all = (
        lax.all_gather(inverse_rows, "virt", axis=2, tiled=True),
        lax.all_gather(kinetic_rows, "virt", axis=2, tiled=True),
    )
    log_grad = product(inverse_all, virt_values)
    kin_part = product(inverse_all, virt_laplacians) - product(kinetic_all, virt_values)
    weighted, log_sum = gradient_terms(log_grad, kin_part, weights)
    summed = (
        lax.psum_scatter(weighted, "walk", scatter_dimension=0, tiled=True),
        lax.psum_scatter(log_sum, "walk", scatter_dimension=0, tiled=True),
    )
    gradient_part, log_part = (summed[0], summed[1])
    return (gradient_part / walker_count, log_part / walker_count)


SPAN = 248.0
EXTRA = 128
PART = EXTRA // 4
OFFSET = 3.1
TINY = 1e-30
MIB = 1024 * 1024


def stage_masks(count):
    bits = [1 << bit for bit in range(count.bit_length() - 1)]
    if len(bits) < 3:
        return [[bit] for bit in bits]
    return [bits[:1], bits[1:3]] + [[bit] for bit in bits[3:]]


def place_weights(stages):
    order = [mask for stage in stages for mask in stage]
    weights = [0] * len(order)
    for index, mask in enumerate(order):
        weights[mask.bit_length() - 1] = 1 << (len(order) - 1 - index)
    return weights


def partners(stage):
    if len(stage) == 1:
        return list(stage)
    first, second = stage
    return [second, first, first ^ second]


def swap(array, axis, mask):
    pairs = [(source, source ^ mask) for source in range(lax.axis_size(axis))]
    return lax.ppermute(array, axis, pairs)


def encode(rows):
    magnitude = jnp.abs(rows)
    largest = jnp.maximum(jnp.max(magnitude, axis=-1, keepdims=True), TINY)
    scale = (largest * (1.0 + 2.0**-7)).astype(jnp.bfloat16).astype(jnp.float32)
    code = jnp.exp2(magnitude * (SPAN / scale) - SPAN / 2)
    return jnp.where(rows < 0, -code, code).astype(jnp.bfloat16), scale


def decode(coded):
    width = coded.shape[1] - EXTRA
    code = coded[:, :width].astype(jnp.float32)
    scale = coded[:, width : width + 1].astype(jnp.float32)
    magnitude = (jnp.log2(jnp.abs(code)) + SPAN / 2) * (scale / SPAN)
    return jnp.where(code < 0, -magnitude, magnitude)


def store_coded(send_refs, blocks, energy):
    width = send_refs[0].shape[1] - EXTRA
    each = send_refs[0].shape[0]
    f32, bf16 = jnp.float32, jnp.bfloat16
    energy = jnp.concatenate([energy, energy], axis=0)
    high = energy.astype(bf16).astype(f32)
    middle = (energy - high).astype(bf16).astype(f32)
    low = energy - high - middle
    lane = lax.broadcasted_iota(jnp.int32, energy.shape, 1)
    terms = jnp.where(lane < 2 * PART, high, jnp.where(lane < 3 * PART, middle, low))
    for pair in range(len(blocks) // 2):
        code, scale = encode(jnp.concatenate(blocks[2 * pair : 2 * pair + 2], axis=0))
        send_ref = send_refs[16 * pair // each]
        target = slice(16 * pair % each, 16 * pair % each + 16)
        send_ref[target, :width] = code
        send_ref[target, width:] = jnp.where(lane < PART, scale, terms).astype(bf16)


def add_came(keep_ref, came_refs):
    arrays, height, width = keep_ref.shape
    width -= EXTRA
    per = height // 8
    sums = [keep_ref[index // per, 8 * (index % per) : 8 * (index % per) + 8, :width] for index in range(arrays * per)]
    energy = keep_ref[0, :8, width:]
    for parts in came_refs:
        index = 0
        for part in parts:
            for row in range(0, part.shape[0], 16):
                both = decode(part[row : row + 16, :])
                sums[index] += both[:8]
                sums[index + 1] += both[8:]
                index += 2
        terms = parts[0][:16, width:].astype(jnp.float32)[:8]
        for term in range(1, 4):
            energy += terms[:, term * PART : term * PART + 1]
    return [sums[array * per : (array + 1) * per] for array in range(arrays)], energy


def limit(mib):
    return pltpu.CompilerParams(vmem_limit_bytes=mib * MIB)


def cost(microseconds):
    return pl.CostEstimate(flops=int(microseconds * 1.1e9), bytes_accessed=0, transcendentals=0)


WHOLE = pl.BlockSpec(memory_space=pltpu.VMEM)
SCALAR = pl.BlockSpec(memory_space=pltpu.SMEM)
ANYWHERE = pl.BlockSpec(memory_space=pl.ANY)
HELD = pl.BlockSpec(memory_space=pltpu.HBM)
HELD = pl.BlockSpec(memory_space=pltpu.HBM)


def cut_kernel(inverse_ref, kinetic_ref, *out_refs):
    count = inverse_ref.shape[0]
    for array, ref in enumerate((inverse_ref, kinetic_ref)):
        for dest in range(0, count, 2):
            pair = [ref[dest + other].astype(jnp.float32) for other in range(2)]
            for index, out_ref in enumerate(out_refs):
                rows = jnp.concatenate([block[8 * index : 8 * index + 8] for block in pair], axis=0)
                out_ref[array, 8 * dest : 8 * dest + 16, :] = rows.astype(jnp.bfloat16)


def cut(inverse, kinetic, group):
    count, _, depth = inverse.shape
    block = pl.BlockSpec((count, 16, depth), lambda step: (0, group, 0))
    out = jax.ShapeDtypeStruct((2, 8 * count, depth), jnp.bfloat16)
    return pl.pallas_call(
        cut_kernel,
        out_shape=(out, out),
        grid=(1,),
        in_specs=[block, block],
        out_specs=(pl.BlockSpec(out.shape, lambda step: (0, 0, 0)),) * 2,
        compiler_params=limit(12),
        cost_estimate=cost(0.1),
        name="cut",
    )(inverse, kinetic)


def near_kernel(chunk, tile, virt_ref, me_ref, energy_ref, inverse_ref, kinetic_ref, values_ref, laps_ref, *rest):
    out_ref, far_values, far_laps, near_values, near_laps, own_inverse, own_kinetic, sems = rest[-8:]
    count, per, depth = inverse_ref.shape
    height = count * per
    width = out_ref.shape[3]
    f32 = jnp.float32
    own = pl.ds(pl.multiple_of(virt_ref[0] * depth, depth), depth)
    other = pl.ds(pl.multiple_of((1 - virt_ref[0]) * depth, depth), depth)
    chunks = width // chunk

    copies = []
    for index in range(chunks):
        columns = pl.ds(index * chunk, chunk)
        copies.append([
            pltpu.make_async_copy(table.at[own, columns], held.at[:, columns], sems.at[index, which])
            for which, (table, held) in enumerate(((values_ref, near_values), (laps_ref, near_laps)))
        ])
    last = [
        pltpu.make_async_copy(table.at[other, :], held, sems.at[chunks, which])
        for which, (table, held) in enumerate(((values_ref, far_values), (laps_ref, far_laps)))
    ]
    first = [
        pltpu.make_async_copy(rows, held, sems.at[chunks + 1, which])
        for which, (rows, held) in enumerate(((inverse_ref, own_inverse), (kinetic_ref, own_kinetic)))
    ]
    for copy in first + sum(copies, []) + last:
        copy.start()
    for copy in first:
        copy.wait()
    inverse = own_inverse[...].reshape(height, depth)
    kinetic = own_kinetic[...].reshape(height, depth)
    for index in range(chunks):
        for copy in copies[index]:
            copy.wait()

        @pl.loop(index * chunk // tile, (index + 1) * chunk // tile)
        def _(step):
            columns = pl.ds(pl.multiple_of(step * tile, tile), tile)
            values, laps = near_values[:, columns], near_laps[:, columns]
            out_ref[1, :, :, columns] = jnp.dot(inverse, values, preferred_element_type=f32).reshape(count, per, tile)
            rest = jnp.dot(kinetic, values, preferred_element_type=f32)
            rest -= jnp.dot(inverse, laps, preferred_element_type=f32)
            out_ref[0, :, :, columns] = (0.5 * rest).reshape(count, per, tile)

    for copy in last:
        copy.wait()


def near_product(virt, me, energy, inverse, kinetic, values, laplacians, after):
    count, per, depth = inverse.shape
    width = values.shape[1]
    chunk, tile = 512, 256
    table = pltpu.VMEM((depth, width), jnp.bfloat16)
    own = pltpu.VMEM((count, per, depth), jnp.bfloat16)
    return pl.pallas_call(
        functools.partial(near_kernel, chunk, tile),
        out_shape=(jax.ShapeDtypeStruct((2, count, per, width), jnp.float32), table, table),
        in_specs=[SCALAR, SCALAR, SCALAR, HELD, HELD, HELD, HELD] + [ANYWHERE] * len(after),
        out_specs=(WHOLE, WHOLE, WHOLE),
        scratch_shapes=[table, table, own, own, pltpu.SemaphoreType.DMA((width // chunk + 2, 2))],
        compiler_params=limit(24),
        cost_estimate=cost(9),
        name="near_product",
    )(virt, me, energy, inverse, kinetic, values, laplacians, *after)


def far_kernel(weights, count, tile, first, split, virt_ref, me_ref, energy_ref, far_ref, near_ref, values_ref, laps_ref, *rest):
    send_refs, place_ref = rest[-split - 1 : -1], rest[-1]
    _, height, depth = far_ref.shape
    width = near_ref.shape[3]
    rows = height // count
    half = height // 2
    f32 = jnp.float32
    scale = 2.0 * (energy_ref[0] - OFFSET)

    @pl.loop(0, width // tile)
    def _(index):
        columns = pl.ds(pl.multiple_of(index * tile, tile), tile)
        near = near_ref[:, :, first : first + rows, columns].reshape(2, height, tile)
        both = jnp.dot(far_ref[...].reshape(2 * height, depth), values_ref[:, columns], preferred_element_type=f32)
        laps = jnp.dot(far_ref[0], laps_ref[:, columns], preferred_element_type=f32)
        log = both[:height] + near[1]
        weighted = scale * log + (0.5 * (both[height:] - laps) + near[0])
        for dest in range(count):
            difference = dest ^ me_ref[0]
            place = 0
            for bit, weight in enumerate(weights):
                place = place ^ (((difference >> bit) & 1) * weight)
            target = pl.ds(pl.multiple_of(place * rows, rows), rows)
            source = slice(dest * rows, (dest + 1) * rows)
            place_ref[0, target, columns] = weighted[source]
            place_ref[1, target, columns] = log[source]

    energy = jnp.full((8, EXTRA), energy_ref[0], f32)
    place_ref[0, :8, width:] = energy
    blocks = [place_ref[array, row : row + 8, :width] for array in range(2) for row in range(half, height, 8)]
    store_coded(send_refs, blocks, energy)


def far_product(virt, me, energy, theirs, near, first, values, laplacians, tile, stages, split, after, length):
    _, height, depth = theirs.shape
    width = values.shape[1]
    half = height // 2
    count = 1 << sum(len(stage) for stage in stages)
    *sends, keep = pl.pallas_call(
        functools.partial(far_kernel, place_weights(stages), count, tile, first, split),
        out_shape=(jax.ShapeDtypeStruct((2 * half // split, width + EXTRA), jnp.bfloat16),) * split
        + (jax.ShapeDtypeStruct((2, height, width + EXTRA), jnp.float32),),
        in_specs=[SCALAR, SCALAR, SCALAR, WHOLE, WHOLE, WHOLE, WHOLE] + [ANYWHERE] * len(after),
        out_specs=(WHOLE,) * (split + 1),
        compiler_params=limit(24),
        cost_estimate=cost(length),
        name="far_product",
    )(virt, me, energy, theirs, near, values, laplacians, *after)
    return [sends], keep


def combine_kernel(layout, ordered, carried, height, *refs):
    count = len(layout)
    keep_refs, refs = [ref.at[:, :height] for ref in refs[:count]], refs[count:]
    came = []
    for parts in layout:
        came.append([])
        for index, first, last in parts:
            came[-1].append([refs[position].at[first:last, :] for position in index])
    inputs = 1 + max(position for parts in layout for index, _, _ in parts for position in index)
    refs = refs[inputs + ordered :]
    kept_refs, send_refs = refs[carried : carried + count], refs[carried + count :]
    if carried:
        above = refs[0].shape[0]
        send_refs[0][:above, :] = refs[0][...]
        send_refs = [send_refs[0].at[above:, :]]
    width = keep_refs[0].shape[2] - EXTRA
    for piece, (keep_ref, kept_ref) in enumerate(zip(keep_refs, kept_refs)):
        sums, energy = add_came(keep_ref, came[piece])
        kept = kept_ref.shape[1] // 8
        for array, blocks in enumerate(sums):
            for index, block in enumerate(blocks[:kept]):
                kept_ref[array, 8 * index : 8 * index + 8, :width] = block
        kept_ref[0, :8, width:] = energy
        rows = slice(16 * kept * piece, 16 * kept * (piece + 1))
        for index, send_ref in enumerate(send_refs):
            first = kept * (index + 1)
            store_coded([send_ref.at[rows, :]], [block for blocks in sums for block in blocks[first : first + kept]], energy)


def combine(keeps, came, layout, sent, after, length, carry=(), part=1):
    _, height, width = keeps[0].shape
    height = height // part
    kept = height // (sent + 1)
    count = len(keeps)
    above = sum(array.shape[0] for array in carry)
    outs = pl.pallas_call(
        functools.partial(combine_kernel, layout, len(after), len(carry), height),
        out_shape=(jax.ShapeDtypeStruct((2, kept, width), jnp.float32),) * count
        + (jax.ShapeDtypeStruct((2 * kept * count + above, width), jnp.bfloat16),) * sent,
        in_specs=[WHOLE] * (count + len(came)) + [ANYWHERE] * len(after) + [WHOLE] * len(carry),
        out_specs=(WHOLE,) * (count + sent),
        compiler_params=limit(10),
        cost_estimate=cost(length),
        name="combine",
    )(*keeps, *came, *after, *carry)
    return outs[count:], outs[:count]


def first_layout(count, split, rows):
    return tuple(((tuple(range(piece * split, piece * split + split)), 0, rows),) for piece in range(count))


def joint_layout(count, senders, rows):
    return tuple(
        tuple(((sender,), piece * rows, piece * rows + rows) for sender in range(senders)) for piece in range(count)
    )


def outputs_of(keep_ref, came, count):
    (gradient, log), energy = add_came(keep_ref, came)
    correction = 2.0 * (energy[:, :1] / count - OFFSET)
    log = [block / count for block in log]
    return [block / count - correction * mean for block, mean in zip(gradient, log)], log


def share_kernel(count, *refs):
    (gradient_ref, log_ref), refs = refs[-2:], refs[:-2]
    early = GROUPS[1:-1]
    came = [[] for piece in GROUPS[0]]
    for ref, group in zip(refs[len(refs) - len(early) :], early):
        came += [[[ref.at[16 * place : 16 * place + 16, :]]] for place in range(len(group))]
    row = 0
    for keep_ref, parts in zip(refs, came):
        for gradient, log in zip(*outputs_of(keep_ref, parts, count)):
            gradient_ref[row : row + 8, :] = gradient
            log_ref[row : row + 8, :] = log
            row += 8


def share(keeps, came, rows, count):
    width = keeps[0].shape[2] - EXTRA
    out = pltpu.HBM((rows, width), jnp.float32)
    block = pl.BlockSpec((sum(keep.shape[1] for keep in keeps), width), lambda step: (0, 0))
    return pl.pallas_call(
        functools.partial(share_kernel, count),
        out_shape=(out, out),
        grid=(1,),
        in_specs=[WHOLE] * (len(keeps) + len(came)),
        out_specs=(block, block),
        compiler_params=limit(8),
        cost_estimate=cost(0.1),
        name="share",
    )(*keeps, *came)


def finish_kernel(count, keep_ref, came_ref, *refs):
    gradient, log = outputs_of(keep_ref, [[came_ref]], count)
    for ref, blocks in zip(refs[-2:], (gradient, log)):
        for index, block in enumerate(blocks):
            ref[8 * index : 8 * index + 8, :] = block


def finish(outputs, keep, came, count):
    _, rows, width = keep.shape
    out = pltpu.HBM(outputs[0].shape, jnp.float32)
    last = outputs[0].shape[0] // rows - 1
    block = pl.BlockSpec((rows, width - EXTRA), lambda step: (last, 0))
    return pl.pallas_call(
        functools.partial(finish_kernel, count),
        out_shape=(out, out),
        grid=(1,),
        in_specs=[WHOLE, WHOLE, HELD, HELD],
        out_specs=(block, block),
        input_output_aliases={2: 0, 3: 1},
        compiler_params=limit(8),
        cost_estimate=cost(0.1),
        name="finish",
    )(keep, came, *outputs)


def pieced_body(pieces, tile, inverse_rows, kinetic_rows, virt_values, virt_laplacians, local_energy):
    count = lax.axis_size("walk")
    stages = stage_masks(count)
    me = lax.axis_index("walk").astype(jnp.int32).reshape(1)
    virt = lax.axis_index("virt").astype(jnp.int32).reshape(1)
    occupied, depth = inverse_rows.shape[1:]
    by_dest = (count, occupied // count, depth)
    inverse, kinetic = inverse_rows.reshape(by_dest), kinetic_rows.reshape(by_dest)
    rows = occupied // (count * pieces)

    inverse, kinetic, values, laplacians = (
        pltpu.with_memory_space_constraint(array, pltpu.HBM)
        for array in (inverse, kinetic, virt_values[0], virt_laplacians[0])
    )
    mine = [part for group in range(pieces // 2) for part in cut(inverse, kinetic, group)]
    mine[1], mine[2] = lax.optimization_barrier((mine[1], mine[2]))
    theirs = [swap(part, "virt", 1) for part in mine[:2]]
    near, values, laplacians = near_product(virt, me, local_energy, inverse, kinetic, values, laplacians, mine[2:])

    second = partners(stages[1])
    keep, came, carry, sent, last = {}, [], (), (), []

    def second_sums(piece, carry, after, length):
        layout = joint_layout(1, len(sent), sent[0].shape[0])
        (send,), (keep[piece],) = combine([keep[piece]], sent, layout, 1, after, length, carry)
        group = next(group for group in GROUPS if piece in group)
        if piece < group[-1]:
            return (send,), [keep[piece]]
        held.append(send)
        return (), [keep[piece]]

    held = []
    for turn in range(pieces):
        final = turn == pieces - 1
        send, kept = far_product(
            virt, me, local_energy, theirs[turn], near, turn * rows, values, laplacians, tile, stages, SPLIT[turn], last, FAR[turn]
        )
        if turn + 2 < pieces:
            part, kept = lax.optimization_barrier((mine[turn + 2], kept))
            theirs.append(swap(part, "virt", 1))
        first = [swap(part, "walk", stages[0][0]) for part in send[0]]
        last = [kept]
        if final:
            group = GROUPS[0]
            layout = joint_layout(len(group), 1, came[0].shape[0] // len(group))
            _, keeps = combine([keep[piece] for piece in group], came[:1], layout, 0, last, BESIDE[turn])
            keep.update(zip(group, keeps))
            last = [keep[group[0]]]
        elif turn:
            carry, last = second_sums(turn - 1, carry, last, BESIDE[turn])
            if held:
                came.append(swap(held.pop(), "walk", stages[2][0]))
        layout = first_layout(1, SPLIT[turn], first[0].shape[0])
        sends, (keep[turn],) = combine([kept], first, layout, len(second), last, 0.1, part=2)
        last = [keep[turn]]
        if final:
            carry, last = second_sums(turn - 1, carry, last, 0.1)
            came.append(swap(held.pop(), "walk", stages[2][0]))
        sent = [swap(part, "walk", mask) for part, mask in reversed(list(zip(sends, second)))]
    second_sums(pieces - 1, (), last, 0.1)
    came.append(swap(held.pop(), "walk", stages[2][0]))
    outputs = share([keep[piece] for piece in range(pieces - 1)], came[1:-1], occupied // count, count)
    return finish(outputs, keep[pieces - 1], came[-1], count)


def solution(mesh):
    placed = (
        P("walk", None, "virt"),
        P("walk", None, "virt"),
        P("walk", None, "virt"),
        P("walk", None, "virt"),
        P("walk"),
    )

    def body(inverse_rows, kinetic_rows, virt_values, virt_laplacians, local_energy):
        count = mesh.shape["walk"]
        walkers, occupied, depth = inverse_rows.shape
        width = virt_values.shape[2]
        tile = 2048
        fits = (
            walkers == 1
            and mesh.shape["virt"] == 2
            and count == 16
            and count >= 4
            and occupied == count * PIECES * 8
            and depth % 256 == 0
            and width % tile == 0
        )
        form = functools.partial(pieced_body, PIECES, tile) if fits else general_body
        return form(inverse_rows, kinetic_rows, virt_values, virt_laplacians, local_energy)

    return jax.shard_map(
        body,
        mesh=mesh,
        in_specs=placed,
        out_specs=(P("walk", "virt"), P("walk", "virt")),
        check_vma=False,
    )
```

```python
import functools

import jax
import jax.numpy as jnp
from jax import lax
from jax.experimental import pallas as pl
from jax.experimental.pallas import tpu as pltpu
from jax.sharding import PartitionSpec as P

PIECES = 4
GROUPS = ((0, 1), (2,), (3,))
SPLIT = (2, 1, 1, 1)
BESIDE = (0, 6, 6, 6)
FAR = (0.1, 1.5, 1.5, 1.5)


def product(left, right):
    return jnp.einsum("woe,wev->wov", left, right, preferred_element_type=jnp.float32)


def gradient_terms(log_grad, kin_part, weights):
    kin_grad = -0.5 * kin_part
    weighted = jnp.sum(weights[:, None, None] * log_grad + kin_grad, axis=0)
    return (weighted, jnp.sum(log_grad, axis=0))


def general_body(inverse_rows, kinetic_rows, virt_values, virt_laplacians, local_energy):
    walk_count = lax.axis_size("walk")
    walker_count = walk_count * local_energy.shape[0]
    energy_sum = lax.psum(jnp.sum(local_energy), "walk")
    average = energy_sum / walker_count
    weights = 2.0 * (local_energy - average)
    inverse_all, kinetic_all = (
        lax.all_gather(inverse_rows, "virt", axis=2, tiled=True),
        lax.all_gather(kinetic_rows, "virt", axis=2, tiled=True),
    )
    log_grad = product(inverse_all, virt_values)
    kin_part = product(inverse_all, virt_laplacians) - product(kinetic_all, virt_values)
    weighted, log_sum = gradient_terms(log_grad, kin_part, weights)
    summed = (
        lax.psum_scatter(weighted, "walk", scatter_dimension=0, tiled=True),
        lax.psum_scatter(log_sum, "walk", scatter_dimension=0, tiled=True),
    )
    gradient_part, log_part = (summed[0], summed[1])
    return (gradient_part / walker_count, log_part / walker_count)


SPAN = 248.0
EXTRA = 128
PART = EXTRA // 4
OFFSET = 3.1
TINY = 1e-30
MIB = 1024 * 1024


def stage_masks(count):
    bits = [1 << bit for bit in range(count.bit_length() - 1)]
    if len(bits) < 3:
        return [[bit] for bit in bits]
    return [bits[:1], bits[1:3]] + [[bit] for bit in bits[3:]]


def place_weights(stages):
    order = [mask for stage in stages for mask in stage]
    weights = [0] * len(order)
    for index, mask in enumerate(order):
        weights[mask.bit_length() - 1] = 1 << (len(order) - 1 - index)
    return weights


def partners(stage):
    if len(stage) == 1:
        return list(stage)
    first, second = stage
    return [second, first, first ^ second]


def swap(array, axis, mask):
    pairs = [(source, source ^ mask) for source in range(lax.axis_size(axis))]
    return lax.ppermute(array, axis, pairs)


def encode(rows):
    magnitude = jnp.abs(rows)
    largest = jnp.maximum(jnp.max(magnitude, axis=-1, keepdims=True), TINY)
    scale = (largest * (1.0 + 2.0**-7)).astype(jnp.bfloat16).astype(jnp.float32)
    code = jnp.exp2(magnitude * (SPAN / scale) - SPAN / 2)
    return jnp.where(rows < 0, -code, code).astype(jnp.bfloat16), scale


def decode(coded):
    width = coded.shape[1] - EXTRA
    code = coded[:, :width].astype(jnp.float32)
    scale = coded[:, width : width + 1].astype(jnp.float32)
    magnitude = (jnp.log2(jnp.abs(code)) + SPAN / 2) * (scale / SPAN)
    return jnp.where(code < 0, -magnitude, magnitude)


def store_coded(send_refs, blocks, energy):
    width = send_refs[0].shape[1] - EXTRA
    each = send_refs[0].shape[0]
    f32, bf16 = jnp.float32, jnp.bfloat16
    energy = jnp.concatenate([energy, energy], axis=0)
    high = energy.astype(bf16).astype(f32)
    middle = (energy - high).astype(bf16).astype(f32)
    low = energy - high - middle
    lane = lax.broadcasted_iota(jnp.int32, energy.shape, 1)
    terms = jnp.where(lane < 2 * PART, high, jnp.where(lane < 3 * PART, middle, low))
    for pair in range(len(blocks) // 2):
        code, scale = encode(jnp.concatenate(blocks[2 * pair : 2 * pair + 2], axis=0))
        send_ref = send_refs[16 * pair // each]
        target = slice(16 * pair % each, 16 * pair % each + 16)
        send_ref[target, :width] = code
        send_ref[target, width:] = jnp.where(lane < PART, scale, terms).astype(bf16)


def add_came(keep_ref, came_refs):
    arrays, height, width = keep_ref.shape
    width -= EXTRA
    per = height // 8
    sums = [keep_ref[index // per, 8 * (index % per) : 8 * (index % per) + 8, :width] for index in range(arrays * per)]
    energy = keep_ref[0, :8, width:]
    for parts in came_refs:
        index = 0
        for part in parts:
            for row in range(0, part.shape[0], 16):
                both = decode(part[row : row + 16, :])
                sums[index] += both[:8]
                sums[index + 1] += both[8:]
                index += 2
        terms = parts[0][:16, width:].astype(jnp.float32)[:8]
        for term in range(1, 4):
            energy += terms[:, term * PART : term * PART + 1]
    return [sums[array * per : (array + 1) * per] for array in range(arrays)], energy


def limit(mib):
    return pltpu.CompilerParams(vmem_limit_bytes=mib * MIB)


def cost(microseconds):
    return pl.CostEstimate(flops=int(microseconds * 1.1e9), bytes_accessed=0, transcendentals=0)


WHOLE = pl.BlockSpec(memory_space=pltpu.VMEM)
SCALAR = pl.BlockSpec(memory_space=pltpu.SMEM)
ANYWHERE = pl.BlockSpec(memory_space=pl.ANY)
HELD = pl.BlockSpec(memory_space=pltpu.HBM)
HELD = pl.BlockSpec(memory_space=pltpu.HBM)


def cut_kernel(inverse_ref, kinetic_ref, *out_refs):
    count = inverse_ref.shape[0]
    for array, ref in enumerate((inverse_ref, kinetic_ref)):
        for dest in range(0, count, 2):
            pair = [ref[dest + other].astype(jnp.float32) for other in range(2)]
            for index, out_ref in enumerate(out_refs):
                rows = jnp.concatenate([block[8 * index : 8 * index + 8] for block in pair], axis=0)
                out_ref[array, 8 * dest : 8 * dest + 16, :] = rows.astype(jnp.bfloat16)


def cut(inverse, kinetic, group):
    count, _, depth = inverse.shape
    block = pl.BlockSpec((count, 16, depth), lambda step: (0, group, 0))
    out = jax.ShapeDtypeStruct((2, 8 * count, depth), jnp.bfloat16)
    return pl.pallas_call(
        cut_kernel,
        out_shape=(out, out),
        grid=(1,),
        in_specs=[block, block],
        out_specs=(pl.BlockSpec(out.shape, lambda step: (0, 0, 0)),) * 2,
        compiler_params=limit(12),
        cost_estimate=cost(0.1),
        name="cut",
    )(inverse, kinetic)


def near_kernel(chunk, tile, virt_ref, me_ref, energy_ref, inverse_ref, kinetic_ref, values_ref, laps_ref, *rest):
    out_ref, far_values, far_laps, near_values, near_laps, own_inverse, own_kinetic, sems = rest[-8:]
    count, per, depth = inverse_ref.shape
    height = count * per
    width = out_ref.shape[3]
    f32 = jnp.float32
    own = pl.ds(pl.multiple_of(virt_ref[0] * depth, depth), depth)
    other = pl.ds(pl.multiple_of((1 - virt_ref[0]) * depth, depth), depth)
    chunks = width // chunk

    copies = []
    for index in range(chunks):
        columns = pl.ds(index * chunk, chunk)
        copies.append([
            pltpu.make_async_copy(table.at[own, columns], held.at[:, columns], sems.at[index, which])
            for which, (table, held) in enumerate(((values_ref, near_values), (laps_ref, near_laps)))
        ])
    last = [
        pltpu.make_async_copy(table.at[other, :], held, sems.at[chunks, which])
        for which, (table, held) in enumerate(((values_ref, far_values), (laps_ref, far_laps)))
    ]
    first = [
        pltpu.make_async_copy(rows, held, sems.at[chunks + 1, which])
        for which, (rows, held) in enumerate(((inverse_ref, own_inverse), (kinetic_ref, own_kinetic)))
    ]
    for copy in first + sum(copies, []) + last:
        copy.start()
    for copy in first:
        copy.wait()
    inverse = own_inverse[...].reshape(height, depth)
    kinetic = own_kinetic[...].reshape(height, depth)
    for index in range(chunks):
        for copy in copies[index]:
            copy.wait()

        @pl.loop(index * chunk // tile, (index + 1) * chunk // tile)
        def _(step):
            columns = pl.ds(pl.multiple_of(step * tile, tile), tile)
            values, laps = near_values[:, columns], near_laps[:, columns]
            out_ref[1, :, :, columns] = jnp.dot(inverse, values, preferred_element_type=f32).reshape(count, per, tile)
            rest = jnp.dot(kinetic, values, preferred_element_type=f32)
            rest -= jnp.dot(inverse, laps, preferred_element_type=f32)
            out_ref[0, :, :, columns] = (0.5 * rest).reshape(count, per, tile)

    for copy in last:
        copy.wait()


def near_product(virt, me, energy, inverse, kinetic, values, laplacians, after):
    count, per, depth = inverse.shape
    width = values.shape[1]
    chunk, tile = 512, 256
    table = pltpu.VMEM((depth, width), jnp.bfloat16)
    own = pltpu.VMEM((count, per, depth), jnp.bfloat16)
    return pl.pallas_call(
        functools.partial(near_kernel, chunk, tile),
        out_shape=(jax.ShapeDtypeStruct((2, count, per, width), jnp.float32), table, table),
        in_specs=[SCALAR, SCALAR, SCALAR, HELD, HELD, HELD, HELD] + [ANYWHERE] * len(after),
        out_specs=(WHOLE, WHOLE, WHOLE),
        scratch_shapes=[table, table, own, own, pltpu.SemaphoreType.DMA((width // chunk + 2, 2))],
        compiler_params=limit(24),
        cost_estimate=cost(9),
        name="near_product",
    )(virt, me, energy, inverse, kinetic, values, laplacians, *after)


def far_kernel(weights, count, tile, first, split, virt_ref, me_ref, energy_ref, far_ref, near_ref, values_ref, laps_ref, *rest):
    send_refs, place_ref = rest[-split - 1 : -1], rest[-1]
    _, height, depth = far_ref.shape
    width = near_ref.shape[3]
    rows = height // count
    half = height // 2
    f32 = jnp.float32
    scale = 2.0 * (energy_ref[0] - OFFSET)

    @pl.loop(0, width // tile)
    def _(index):
        columns = pl.ds(pl.multiple_of(index * tile, tile), tile)
        near = near_ref[:, :, first : first + rows, columns].reshape(2, height, tile)
        both = jnp.dot(far_ref[...].reshape(2 * height, depth), values_ref[:, columns], preferred_element_type=f32)
        laps = jnp.dot(far_ref[0], laps_ref[:, columns], preferred_element_type=f32)
        log = both[:height] + near[1]
        weighted = scale * log + (0.5 * (both[height:] - laps) + near[0])
        for dest in range(count):
            difference = dest ^ me_ref[0]
            place = 0
            for bit, weight in enumerate(weights):
                place = place ^ (((difference >> bit) & 1) * weight)
            target = pl.ds(pl.multiple_of(place * rows, rows), rows)
            source = slice(dest * rows, (dest + 1) * rows)
            place_ref[0, target, columns] = weighted[source]
            place_ref[1, target, columns] = log[source]

    energy = jnp.full((8, EXTRA), energy_ref[0], f32)
    place_ref[0, :8, width:] = energy
    blocks = [place_ref[array, row : row + 8, :width] for array in range(2) for row in range(half, height, 8)]
    store_coded(send_refs, blocks, energy)


def far_product(virt, me, energy, theirs, near, first, values, laplacians, tile, stages, split, after, length):
    _, height, depth = theirs.shape
    width = values.shape[1]
    half = height // 2
    count = 1 << sum(len(stage) for stage in stages)
    *sends, keep = pl.pallas_call(
        functools.partial(far_kernel, place_weights(stages), count, tile, first, split),
        out_shape=(jax.ShapeDtypeStruct((2 * half // split, width + EXTRA), jnp.bfloat16),) * split
        + (jax.ShapeDtypeStruct((2, height, width + EXTRA), jnp.float32),),
        in_specs=[SCALAR, SCALAR, SCALAR, WHOLE, WHOLE, WHOLE, WHOLE] + [ANYWHERE] * len(after),
        out_specs=(WHOLE,) * (split + 1),
        compiler_params=limit(24),
        cost_estimate=cost(length),
        name="far_product",
    )(virt, me, energy, theirs, near, values, laplacians, *after)
    return [sends], keep


def combine_kernel(layout, ordered, carried, height, *refs):
    count = len(layout)
    keep_refs, refs = [ref.at[:, :height] for ref in refs[:count]], refs[count:]
    came = []
    for parts in layout:
        came.append([])
        for index, first, last in parts:
            came[-1].append([refs[position].at[first:last, :] for position in index])
    inputs = 1 + max(position for parts in layout for index, _, _ in parts for position in index)
    refs = refs[inputs + ordered :]
    kept_refs, send_refs = refs[carried : carried + count], refs[carried + count :]
    if carried:
        above = refs[0].shape[0]
        send_refs[0][:above, :] = refs[0][...]
        send_refs = [send_refs[0].at[above:, :]]
    width = keep_refs[0].shape[2] - EXTRA
    for piece, (keep_ref, kept_ref) in enumerate(zip(keep_refs, kept_refs)):
        sums, energy = add_came(keep_ref, came[piece])
        kept = kept_ref.shape[1] // 8
        for array, blocks in enumerate(sums):
            for index, block in enumerate(blocks[:kept]):
                kept_ref[array, 8 * index : 8 * index + 8, :width] = block
        kept_ref[0, :8, width:] = energy
        rows = slice(16 * kept * piece, 16 * kept * (piece + 1))
        for index, send_ref in enumerate(send_refs):
            first = kept * (index + 1)
            store_coded([send_ref.at[rows, :]], [block for blocks in sums for block in blocks[first : first + kept]], energy)


def combine(keeps, came, layout, sent, after, length, carry=(), part=1):
    _, height, width = keeps[0].shape
    height = height // part
    kept = height // (sent + 1)
    count = len(keeps)
    above = sum(array.shape[0] for array in carry)
    outs = pl.pallas_call(
        functools.partial(combine_kernel, layout, len(after), len(carry), height),
        out_shape=(jax.ShapeDtypeStruct((2, kept, width), jnp.float32),) * count
        + (jax.ShapeDtypeStruct((2 * kept * count + above, width), jnp.bfloat16),) * sent,
        in_specs=[WHOLE] * (count + len(came)) + [ANYWHERE] * len(after) + [WHOLE] * len(carry),
        out_specs=(WHOLE,) * (count + sent),
        compiler_params=limit(10),
        cost_estimate=cost(length),
        name="combine",
    )(*keeps, *came, *after, *carry)
    return outs[count:], outs[:count]


def first_layout(count, split, rows):
    return tuple(((tuple(range(piece * split, piece * split + split)), 0, rows),) for piece in range(count))


def joint_layout(count, senders, rows):
    return tuple(
        tuple(((sender,), piece * rows, piece * rows + rows) for sender in range(senders)) for piece in range(count)
    )


def outputs_of(keep_ref, came, count):
    (gradient, log), energy = add_came(keep_ref, came)
    correction = 2.0 * (energy[:, :1] / count - OFFSET)
    log = [block / count for block in log]
    return [block / count - correction * mean for block, mean in zip(gradient, log)], log


def share_kernel(count, *refs):
    (gradient_ref, log_ref), refs = refs[-2:], refs[:-2]
    early = GROUPS[1:-1]
    came = [[] for piece in GROUPS[0]]
    for ref, group in zip(refs[len(refs) - len(early) :], early):
        came += [[[ref.at[16 * place : 16 * place + 16, :]]] for place in range(len(group))]
    row = 0
    for keep_ref, parts in zip(refs, came):
        for gradient, log in zip(*outputs_of(keep_ref, parts, count)):
            gradient_ref[row : row + 8, :] = gradient
            log_ref[row : row + 8, :] = log
            row += 8


def share(keeps, came, rows, count):
    width = keeps[0].shape[2] - EXTRA
    out = pltpu.HBM((rows, width), jnp.float32)
    block = pl.BlockSpec((sum(keep.shape[1] for keep in keeps), width), lambda step: (0, 0))
    return pl.pallas_call(
        functools.partial(share_kernel, count),
        out_shape=(out, out),
        grid=(1,),
        in_specs=[WHOLE] * (len(keeps) + len(came)),
        out_specs=(block, block),
        compiler_params=limit(8),
        cost_estimate=cost(0.1),
        name="share",
    )(*keeps, *came)


def finish_kernel(count, keep_ref, came_ref, *refs):
    gradient, log = outputs_of(keep_ref, [[came_ref]], count)
    for ref, blocks in zip(refs[-2:], (gradient, log)):
        for index, block in enumerate(blocks):
            ref[8 * index : 8 * index + 8, :] = block


def finish(outputs, keep, came, count):
    _, rows, width = keep.shape
    out = pltpu.HBM(outputs[0].shape, jnp.float32)
    last = outputs[0].shape[0] // rows - 1
    block = pl.BlockSpec((rows, width - EXTRA), lambda step: (last, 0))
    return pl.pallas_call(
        functools.partial(finish_kernel, count),
        out_shape=(out, out),
        grid=(1,),
        in_specs=[WHOLE, WHOLE, HELD, HELD],
        out_specs=(block, block),
        input_output_aliases={2: 0, 3: 1},
        compiler_params=limit(8),
        cost_estimate=cost(0.1),
        name="finish",
    )(keep, came, *outputs)


def pieced_body(pieces, tile, inverse_rows, kinetic_rows, virt_values, virt_laplacians, local_energy):
    count = lax.axis_size("walk")
    stages = stage_masks(count)
    me = lax.axis_index("walk").astype(jnp.int32).reshape(1)
    virt = lax.axis_index("virt").astype(jnp.int32).reshape(1)
    occupied, depth = inverse_rows.shape[1:]
    by_dest = (count, occupied // count, depth)
    inverse, kinetic = inverse_rows.reshape(by_dest), kinetic_rows.reshape(by_dest)
    rows = occupied // (count * pieces)

    inverse, kinetic, values, laplacians = (
        pltpu.with_memory_space_constraint(array, pltpu.HBM)
        for array in (inverse, kinetic, virt_values[0], virt_laplacians[0])
    )
    mine = [part for group in range(pieces // 2) for part in cut(inverse, kinetic, group)]
    mine[1], mine[2] = lax.optimization_barrier((mine[1], mine[2]))
    theirs = [swap(part, "virt", 1) for part in mine[:2]]
    near, values, laplacians = near_product(virt, me, local_energy, inverse, kinetic, values, laplacians, mine[2:])

    second = partners(stages[1])
    keep, came, carry, sent, last = {}, [], (), (), []

    def second_sums(piece, carry, after, length):
        layout = joint_layout(1, len(sent), sent[0].shape[0])
        (send,), (keep[piece],) = combine([keep[piece]], sent, layout, 1, after, length, carry)
        group = next(group for group in GROUPS if piece in group)
        if piece < group[-1]:
            return (send,), [keep[piece]]
        held.append(send)
        return (), [keep[piece]]

    held = []
    for turn in range(pieces):
        final = turn == pieces - 1
        send, kept = far_product(
            virt, me, local_energy, theirs[turn], near, turn * rows, values, laplacians, tile, stages, SPLIT[turn], last, FAR[turn]
        )
        if turn + 2 < pieces:
            part, kept = lax.optimization_barrier((mine[turn + 2], kept))
            theirs.append(swap(part, "virt", 1))
        first = [swap(part, "walk", stages[0][0]) for part in send[0]]
        last = [kept]
        if final:
            group = GROUPS[0]
            layout = joint_layout(len(group), 1, came[0].shape[0] // len(group))
            _, keeps = combine([keep[piece] for piece in group], came[:1], layout, 0, last, BESIDE[turn])
            keep.update(zip(group, keeps))
            last = [keep[group[0]]]
        elif turn:
            carry, last = second_sums(turn - 1, carry, last, BESIDE[turn])
            if held:
                came.append(swap(held.pop(), "walk", stages[2][0]))
        layout = first_layout(1, SPLIT[turn], first[0].shape[0])
        sends, (keep[turn],) = combine([kept], first, layout, len(second), last, 0.1, part=2)
        last = [keep[turn]]
        if final:
            carry, last = second_sums(turn - 1, carry, last, 0.1)
            came.append(swap(held.pop(), "walk", stages[2][0]))
        sent = [swap(part, "walk", mask) for part, mask in reversed(list(zip(sends, second)))]
    second_sums(pieces - 1, (), last, 0.1)
    came.append(swap(held.pop(), "walk", stages[2][0]))
    outputs = share([keep[piece] for piece in range(pieces - 1)], came[1:-1], occupied // count, count)
    return finish(outputs, keep[pieces - 1], came[-1], count)


def solution(mesh):
    placed = (
        P("walk", None, "virt"),
        P("walk", None, "virt"),
        P("walk", None, "virt"),
        P("walk", None, "virt"),
        P("walk"),
    )

    def body(inverse_rows, kinetic_rows, virt_values, virt_laplacians, local_energy):
        count = mesh.shape["walk"]
        walkers, occupied, depth = inverse_rows.shape
        width = virt_values.shape[2]
        tile = 2048
        fits = (
            walkers == 1
            and mesh.shape["virt"] == 2
            and count == 16
            and count >= 4
            and occupied == count * PIECES * 8
            and depth % 256 == 0
            and width % tile == 0
        )
        form = functools.partial(pieced_body, PIECES, tile) if fits else general_body
        return form(inverse_rows, kinetic_rows, virt_values, virt_laplacians, local_energy)

    return jax.shard_map(
        body,
        mesh=mesh,
        in_specs=placed,
        out_specs=(P("walk", "virt"), P("walk", "virt")),
        check_vma=False,
    )
```

```python
import functools

import jax
import jax.numpy as jnp
from jax import lax
from jax.experimental import pallas as pl
from jax.experimental.pallas import tpu as pltpu
from jax.sharding import PartitionSpec as P

PIECES = 4
GROUPS = ((0, 1), (2,), (3,))
SPLIT = (2, 2, 1, 1)
BESIDE = (0, 2.3, 6, 6)
FAR = (0.1, 1.5, 1.5, 1.5)


def product(left, right):
    return jnp.einsum("woe,wev->wov", left, right, preferred_element_type=jnp.float32)


def gradient_terms(log_grad, kin_part, weights):
    kin_grad = -0.5 * kin_part
    weighted = jnp.sum(weights[:, None, None] * log_grad + kin_grad, axis=0)
    return (weighted, jnp.sum(log_grad, axis=0))


def general_body(inverse_rows, kinetic_rows, virt_values, virt_laplacians, local_energy):
    walk_count = lax.axis_size("walk")
    walker_count = walk_count * local_energy.shape[0]
    energy_sum = lax.psum(jnp.sum(local_energy), "walk")
    average = energy_sum / walker_count
    weights = 2.0 * (local_energy - average)
    inverse_all, kinetic_all = (
        lax.all_gather(inverse_rows, "virt", axis=2, tiled=True),
        lax.all_gather(kinetic_rows, "virt", axis=2, tiled=True),
    )
    log_grad = product(inverse_all, virt_values)
    kin_part = product(inverse_all, virt_laplacians) - product(kinetic_all, virt_values)
    weighted, log_sum = gradient_terms(log_grad, kin_part, weights)
    summed = (
        lax.psum_scatter(weighted, "walk", scatter_dimension=0, tiled=True),
        lax.psum_scatter(log_sum, "walk", scatter_dimension=0, tiled=True),
    )
    gradient_part, log_part = (summed[0], summed[1])
    return (gradient_part / walker_count, log_part / walker_count)


SPAN = 248.0
EXTRA = 128
PART = EXTRA // 4
OFFSET = 3.1
TINY = 1e-30
MIB = 1024 * 1024


def stage_masks(count):
    bits = [1 << bit for bit in range(count.bit_length() - 1)]
    if len(bits) < 3:
        return [[bit] for bit in bits]
    return [bits[:1], bits[1:3]] + [[bit] for bit in bits[3:]]


def place_weights(stages):
    order = [mask for stage in stages for mask in stage]
    weights = [0] * len(order)
    for index, mask in enumerate(order):
        weights[mask.bit_length() - 1] = 1 << (len(order) - 1 - index)
    return weights


def partners(stage):
    if len(stage) == 1:
        return list(stage)
    first, second = stage
    return [second, first, first ^ second]


def swap(array, axis, mask):
    pairs = [(source, source ^ mask) for source in range(lax.axis_size(axis))]
    return lax.ppermute(array, axis, pairs)


def encode(rows):
    magnitude = jnp.abs(rows)
    largest = jnp.maximum(jnp.max(magnitude, axis=-1, keepdims=True), TINY)
    scale = (largest * (1.0 + 2.0**-7)).astype(jnp.bfloat16).astype(jnp.float32)
    code = jnp.exp2(magnitude * (SPAN / scale) - SPAN / 2)
    return jnp.where(rows < 0, -code, code).astype(jnp.bfloat16), scale


def decode(coded):
    width = coded.shape[1] - EXTRA
    code = coded[:, :width].astype(jnp.float32)
    scale = coded[:, width : width + 1].astype(jnp.float32)
    magnitude = (jnp.log2(jnp.abs(code)) + SPAN / 2) * (scale / SPAN)
    return jnp.where(code < 0, -magnitude, magnitude)


def store_coded(send_refs, blocks, energy):
    width = send_refs[0].shape[1] - EXTRA
    each = send_refs[0].shape[0]
    f32, bf16 = jnp.float32, jnp.bfloat16
    energy = jnp.concatenate([energy, energy], axis=0)
    high = energy.astype(bf16).astype(f32)
    middle = (energy - high).astype(bf16).astype(f32)
    low = energy - high - middle
    lane = lax.broadcasted_iota(jnp.int32, energy.shape, 1)
    terms = jnp.where(lane < 2 * PART, high, jnp.where(lane < 3 * PART, middle, low))
    for pair in range(len(blocks) // 2):
        code, scale = encode(jnp.concatenate(blocks[2 * pair : 2 * pair + 2], axis=0))
        send_ref = send_refs[16 * pair // each]
        target = slice(16 * pair % each, 16 * pair % each + 16)
        send_ref[target, :width] = code
        send_ref[target, width:] = jnp.where(lane < PART, scale, terms).astype(bf16)


def add_came(keep_ref, came_refs):
    arrays, height, width = keep_ref.shape
    width -= EXTRA
    per = height // 8
    sums = [keep_ref[index // per, 8 * (index % per) : 8 * (index % per) + 8, :width] for index in range(arrays * per)]
    energy = keep_ref[0, :8, width:]
    for parts in came_refs:
        index = 0
        for part in parts:
            for row in range(0, part.shape[0], 16):
                both = decode(part[row : row + 16, :])
                sums[index] += both[:8]
                sums[index + 1] += both[8:]
                index += 2
        terms = parts[0][:16, width:].astype(jnp.float32)[:8]
        for term in range(1, 4):
            energy += terms[:, term * PART : term * PART + 1]
    return [sums[array * per : (array + 1) * per] for array in range(arrays)], energy


def limit(mib):
    return pltpu.CompilerParams(vmem_limit_bytes=mib * MIB)


def cost(microseconds):
    return pl.CostEstimate(flops=int(microseconds * 1.1e9), bytes_accessed=0, transcendentals=0)


WHOLE = pl.BlockSpec(memory_space=pltpu.VMEM)
SCALAR = pl.BlockSpec(memory_space=pltpu.SMEM)
ANYWHERE = pl.BlockSpec(memory_space=pl.ANY)
HELD = pl.BlockSpec(memory_space=pltpu.HBM)
HELD = pl.BlockSpec(memory_space=pltpu.HBM)


def cut_kernel(inverse_ref, kinetic_ref, *out_refs):
    count = inverse_ref.shape[0]
    for array, ref in enumerate((inverse_ref, kinetic_ref)):
        for dest in range(0, count, 2):
            pair = [ref[dest + other].astype(jnp.float32) for other in range(2)]
            for index, out_ref in enumerate(out_refs):
                rows = jnp.concatenate([block[8 * index : 8 * index + 8] for block in pair], axis=0)
                out_ref[array, 8 * dest : 8 * dest + 16, :] = rows.astype(jnp.bfloat16)


def cut(inverse, kinetic, group):
    count, _, depth = inverse.shape
    block = pl.BlockSpec((count, 16, depth), lambda step: (0, group, 0))
    out = jax.ShapeDtypeStruct((2, 8 * count, depth), jnp.bfloat16)
    return pl.pallas_call(
        cut_kernel,
        out_shape=(out, out),
        grid=(1,),
        in_specs=[block, block],
        out_specs=(pl.BlockSpec(out.shape, lambda step: (0, 0, 0)),) * 2,
        compiler_params=limit(12),
        cost_estimate=cost(0.1),
        name="cut",
    )(inverse, kinetic)


def near_kernel(chunk, tile, virt_ref, me_ref, energy_ref, inverse_ref, kinetic_ref, values_ref, laps_ref, *rest):
    out_ref, far_values, far_laps, near_values, near_laps, own_inverse, own_kinetic, sems = rest[-8:]
    count, per, depth = inverse_ref.shape
    height = count * per
    width = out_ref.shape[3]
    f32 = jnp.float32
    own = pl.ds(pl.multiple_of(virt_ref[0] * depth, depth), depth)
    other = pl.ds(pl.multiple_of((1 - virt_ref[0]) * depth, depth), depth)
    chunks = width // chunk

    copies = []
    for index in range(chunks):
        columns = pl.ds(index * chunk, chunk)
        copies.append([
            pltpu.make_async_copy(table.at[own, columns], held.at[:, columns], sems.at[index, which])
            for which, (table, held) in enumerate(((values_ref, near_values), (laps_ref, near_laps)))
        ])
    last = [
        pltpu.make_async_copy(table.at[other, :], held, sems.at[chunks, which])
        for which, (table, held) in enumerate(((values_ref, far_values), (laps_ref, far_laps)))
    ]
    first = [
        pltpu.make_async_copy(rows, held, sems.at[chunks + 1, which])
        for which, (rows, held) in enumerate(((inverse_ref, own_inverse), (kinetic_ref, own_kinetic)))
    ]
    for copy in first + sum(copies, []) + last:
        copy.start()
    for copy in first:
        copy.wait()
    inverse = own_inverse[...].reshape(height, depth)
    kinetic = own_kinetic[...].reshape(height, depth)
    for index in range(chunks):
        for copy in copies[index]:
            copy.wait()

        @pl.loop(index * chunk // tile, (index + 1) * chunk // tile)
        def _(step):
            columns = pl.ds(pl.multiple_of(step * tile, tile), tile)
            values, laps = near_values[:, columns], near_laps[:, columns]
            out_ref[1, :, :, columns] = jnp.dot(inverse, values, preferred_element_type=f32).reshape(count, per, tile)
            rest = jnp.dot(kinetic, values, preferred_element_type=f32)
            rest -= jnp.dot(inverse, laps, preferred_element_type=f32)
            out_ref[0, :, :, columns] = (0.5 * rest).reshape(count, per, tile)

    for copy in last:
        copy.wait()


def near_product(virt, me, energy, inverse, kinetic, values, laplacians, after):
    count, per, depth = inverse.shape
    width = values.shape[1]
    chunk, tile = 512, 256
    table = pltpu.VMEM((depth, width), jnp.bfloat16)
    own = pltpu.VMEM((count, per, depth), jnp.bfloat16)
    return pl.pallas_call(
        functools.partial(near_kernel, chunk, tile),
        out_shape=(jax.ShapeDtypeStruct((2, count, per, width), jnp.float32), table, table),
        in_specs=[SCALAR, SCALAR, SCALAR, HELD, HELD, HELD, HELD] + [ANYWHERE] * len(after),
        out_specs=(WHOLE, WHOLE, WHOLE),
        scratch_shapes=[table, table, own, own, pltpu.SemaphoreType.DMA((width // chunk + 2, 2))],
        compiler_params=limit(24),
        cost_estimate=cost(9),
        name="near_product",
    )(virt, me, energy, inverse, kinetic, values, laplacians, *after)


def far_kernel(weights, count, tile, first, split, virt_ref, me_ref, energy_ref, far_ref, near_ref, values_ref, laps_ref, *rest):
    send_refs, place_ref = rest[-split - 1 : -1], rest[-1]
    _, height, depth = far_ref.shape
    width = near_ref.shape[3]
    rows = height // count
    half = height // 2
    f32 = jnp.float32
    scale = 2.0 * (energy_ref[0] - OFFSET)

    @pl.loop(0, width // tile)
    def _(index):
        columns = pl.ds(pl.multiple_of(index * tile, tile), tile)
        near = near_ref[:, :, first : first + rows, columns].reshape(2, height, tile)
        both = jnp.dot(far_ref[...].reshape(2 * height, depth), values_ref[:, columns], preferred_element_type=f32)
        laps = jnp.dot(far_ref[0], laps_ref[:, columns], preferred_element_type=f32)
        log = both[:height] + near[1]
        weighted = scale * log + (0.5 * (both[height:] - laps) + near[0])
        for dest in range(count):
            difference = dest ^ me_ref[0]
            place = 0
            for bit, weight in enumerate(weights):
                place = place ^ (((difference >> bit) & 1) * weight)
            target = pl.ds(pl.multiple_of(place * rows, rows), rows)
            source = slice(dest * rows, (dest + 1) * rows)
            place_ref[0, target, columns] = weighted[source]
            place_ref[1, target, columns] = log[source]

    energy = jnp.full((8, EXTRA), energy_ref[0], f32)
    place_ref[0, :8, width:] = energy
    blocks = [place_ref[array, row : row + 8, :width] for array in range(2) for row in range(half, height, 8)]
    store_coded(send_refs, blocks, energy)


def far_product(virt, me, energy, theirs, near, first, values, laplacians, tile, stages, split, after, length):
    _, height, depth = theirs.shape
    width = values.shape[1]
    half = height // 2
    count = 1 << sum(len(stage) for stage in stages)
    *sends, keep = pl.pallas_call(
        functools.partial(far_kernel, place_weights(stages), count, tile, first, split),
        out_shape=(jax.ShapeDtypeStruct((2 * half // split, width + EXTRA), jnp.bfloat16),) * split
        + (jax.ShapeDtypeStruct((2, height, width + EXTRA), jnp.float32),),
        in_specs=[SCALAR, SCALAR, SCALAR, WHOLE, WHOLE, WHOLE, WHOLE] + [ANYWHERE] * len(after),
        out_specs=(WHOLE,) * (split + 1),
        compiler_params=limit(24),
        cost_estimate=cost(length),
        name="far_product",
    )(virt, me, energy, theirs, near, values, laplacians, *after)
    return [sends], keep


def combine_kernel(layout, ordered, carried, height, *refs):
    count = len(layout)
    keep_refs, refs = [ref.at[:, :height] for ref in refs[:count]], refs[count:]
    came = []
    for parts in layout:
        came.append([])
        for index, first, last in parts:
            came[-1].append([refs[position].at[first:last, :] for position in index])
    inputs = 1 + max(position for parts in layout for index, _, _ in parts for position in index)
    refs = refs[inputs + ordered :]
    kept_refs, send_refs = refs[carried : carried + count], refs[carried + count :]
    if carried:
        above = refs[0].shape[0]
        send_refs[0][:above, :] = refs[0][...]
        send_refs = [send_refs[0].at[above:, :]]
    width = keep_refs[0].shape[2] - EXTRA
    for piece, (keep_ref, kept_ref) in enumerate(zip(keep_refs, kept_refs)):
        sums, energy = add_came(keep_ref, came[piece])
        kept = kept_ref.shape[1] // 8
        for array, blocks in enumerate(sums):
            for index, block in enumerate(blocks[:kept]):
                kept_ref[array, 8 * index : 8 * index + 8, :width] = block
        kept_ref[0, :8, width:] = energy
        rows = slice(16 * kept * piece, 16 * kept * (piece + 1))
        for index, send_ref in enumerate(send_refs):
            first = kept * (index + 1)
            store_coded([send_ref.at[rows, :]], [block for blocks in sums for block in blocks[first : first + kept]], energy)


def combine(keeps, came, layout, sent, after, length, carry=(), part=1):
    _, height, width = keeps[0].shape
    height = height // part
    kept = height // (sent + 1)
    count = len(keeps)
    above = sum(array.shape[0] for array in carry)
    outs = pl.pallas_call(
        functools.partial(combine_kernel, layout, len(after), len(carry), height),
        out_shape=(jax.ShapeDtypeStruct((2, kept, width), jnp.float32),) * count
        + (jax.ShapeDtypeStruct((2 * kept * count + above, width), jnp.bfloat16),) * sent,
        in_specs=[WHOLE] * (count + len(came)) + [ANYWHERE] * len(after) + [WHOLE] * len(carry),
        out_specs=(WHOLE,) * (count + sent),
        compiler_params=limit(10),
        cost_estimate=cost(length),
        name="combine",
    )(*keeps, *came, *after, *carry)
    return outs[count:], outs[:count]


def first_layout(count, split, rows):
    return tuple(((tuple(range(piece * split, piece * split + split)), 0, rows),) for piece in range(count))


def joint_layout(count, senders, rows):
    return tuple(
        tuple(((sender,), piece * rows, piece * rows + rows) for sender in range(senders)) for piece in range(count)
    )


def outputs_of(keep_ref, came, count):
    (gradient, log), energy = add_came(keep_ref, came)
    correction = 2.0 * (energy[:, :1] / count - OFFSET)
    log = [block / count for block in log]
    return [block / count - correction * mean for block, mean in zip(gradient, log)], log


def share_kernel(count, *refs):
    (gradient_ref, log_ref), refs = refs[-2:], refs[:-2]
    early = GROUPS[1:-1]
    came = [[] for piece in GROUPS[0]]
    for ref, group in zip(refs[len(refs) - len(early) :], early):
        came += [[[ref.at[16 * place : 16 * place + 16, :]]] for place in range(len(group))]
    row = 0
    for keep_ref, parts in zip(refs, came):
        for gradient, log in zip(*outputs_of(keep_ref, parts, count)):
            gradient_ref[row : row + 8, :] = gradient
            log_ref[row : row + 8, :] = log
            row += 8


def share(keeps, came, rows, count):
    width = keeps[0].shape[2] - EXTRA
    out = pltpu.HBM((rows, width), jnp.float32)
    block = pl.BlockSpec((sum(keep.shape[1] for keep in keeps), width), lambda step: (0, 0))
    return pl.pallas_call(
        functools.partial(share_kernel, count),
        out_shape=(out, out),
        grid=(1,),
        in_specs=[WHOLE] * (len(keeps) + len(came)),
        out_specs=(block, block),
        compiler_params=limit(8),
        cost_estimate=cost(0.1),
        name="share",
    )(*keeps, *came)


def finish_kernel(count, keep_ref, came_ref, *refs):
    gradient, log = outputs_of(keep_ref, [[came_ref]], count)
    for ref, blocks in zip(refs[-2:], (gradient, log)):
        for index, block in enumerate(blocks):
            ref[8 * index : 8 * index + 8, :] = block


def finish(outputs, keep, came, count):
    _, rows, width = keep.shape
    out = pltpu.HBM(outputs[0].shape, jnp.float32)
    last = outputs[0].shape[0] // rows - 1
    block = pl.BlockSpec((rows, width - EXTRA), lambda step: (last, 0))
    return pl.pallas_call(
        functools.partial(finish_kernel, count),
        out_shape=(out, out),
        grid=(1,),
        in_specs=[WHOLE, WHOLE, HELD, HELD],
        out_specs=(block, block),
        input_output_aliases={2: 0, 3: 1},
        compiler_params=limit(8),
        cost_estimate=cost(0.1),
        name="finish",
    )(keep, came, *outputs)


def pieced_body(pieces, tile, inverse_rows, kinetic_rows, virt_values, virt_laplacians, local_energy):
    count = lax.axis_size("walk")
    stages = stage_masks(count)
    me = lax.axis_index("walk").astype(jnp.int32).reshape(1)
    virt = lax.axis_index("virt").astype(jnp.int32).reshape(1)
    occupied, depth = inverse_rows.shape[1:]
    by_dest = (count, occupied // count, depth)
    inverse, kinetic = inverse_rows.reshape(by_dest), kinetic_rows.reshape(by_dest)
    rows = occupied // (count * pieces)

    inverse, kinetic, values, laplacians = (
        pltpu.with_memory_space_constraint(array, pltpu.HBM)
        for array in (inverse, kinetic, virt_values[0], virt_laplacians[0])
    )
    mine = [part for group in range(pieces // 2) for part in cut(inverse, kinetic, group)]
    mine[1], mine[2] = lax.optimization_barrier((mine[1], mine[2]))
    theirs = [swap(part, "virt", 1) for part in mine[:2]]
    near, values, laplacians = near_product(virt, me, local_energy, inverse, kinetic, values, laplacians, mine[2:])

    second = partners(stages[1])
    keep, came, carry, sent, last = {}, [], (), (), []

    def second_sums(piece, carry, after, length):
        layout = joint_layout(1, len(sent), sent[0].shape[0])
        (send,), (keep[piece],) = combine([keep[piece]], sent, layout, 1, after, length, carry)
        group = next(group for group in GROUPS if piece in group)
        if piece < group[-1]:
            return (send,), [keep[piece]]
        held.append(send)
        return (), [keep[piece]]

    held = []
    for turn in range(pieces):
        final = turn == pieces - 1
        send, kept = far_product(
            virt, me, local_energy, theirs[turn], near, turn * rows, values, laplacians, tile, stages, SPLIT[turn], last, FAR[turn]
        )
        if turn + 2 < pieces:
            part, kept = lax.optimization_barrier((mine[turn + 2], kept))
            theirs.append(swap(part, "virt", 1))
        first = [swap(part, "walk", stages[0][0]) for part in send[0]]
        last = [kept]
        if final:
            group = GROUPS[0]
            layout = joint_layout(len(group), 1, came[0].shape[0] // len(group))
            _, keeps = combine([keep[piece] for piece in group], came[:1], layout, 0, last, BESIDE[turn])
            keep.update(zip(group, keeps))
            last = [keep[group[0]]]
        elif turn:
            carry, last = second_sums(turn - 1, carry, last, BESIDE[turn])
            if held:
                came.append(swap(held.pop(), "walk", stages[2][0]))
        layout = first_layout(1, SPLIT[turn], first[0].shape[0])
        sends, (keep[turn],) = combine([kept], first, layout, len(second), last, 0.1, part=2)
        last = [keep[turn]]
        if final:
            carry, last = second_sums(turn - 1, carry, last, 0.1)
            came.append(swap(held.pop(), "walk", stages[2][0]))
        pairs = list(zip(sends, second))
        sent = [swap(part, "walk", mask) for part, mask in (pairs if final else reversed(pairs))]
    second_sums(pieces - 1, (), last, 0.1)
    came.append(swap(held.pop(), "walk", stages[2][0]))
    outputs = share([keep[piece] for piece in range(pieces - 1)], came[1:-1], occupied // count, count)
    return finish(outputs, keep[pieces - 1], came[-1], count)


def solution(mesh):
    placed = (
        P("walk", None, "virt"),
        P("walk", None, "virt"),
        P("walk", None, "virt"),
        P("walk", None, "virt"),
        P("walk"),
    )

    def body(inverse_rows, kinetic_rows, virt_values, virt_laplacians, local_energy):
        count = mesh.shape["walk"]
        walkers, occupied, depth = inverse_rows.shape
        width = virt_values.shape[2]
        tile = 2048
        fits = (
            walkers == 1
            and mesh.shape["virt"] == 2
            and count == 16
            and count >= 4
            and occupied == count * PIECES * 8
            and depth % 256 == 0
            and width % tile == 0
        )
        form = functools.partial(pieced_body, PIECES, tile) if fits else general_body
        return form(inverse_rows, kinetic_rows, virt_values, virt_laplacians, local_energy)

    return jax.shard_map(
        body,
        mesh=mesh,
        in_specs=placed,
        out_specs=(P("walk", "virt"), P("walk", "virt")),
        check_vma=False,
    )
```
